256 devices in a mesh: dp: 4 (over y), tm: 64 (over z, x, core).
Axes of the slice: x: 4, y: 4, z: 8, core: 2. Of those that a mesh axis runs over, the one named last changes fastest.
Arguments:
- video_tile: bfloat16 [4, 128, 16, 16, 256], P('dp', 'tm'), may hold values from -30 to 30
- clip_lengths: int32 [4, 6], P('dp'), may hold values from 1 to 48, 128 in all within a row
- kernels: bfloat16 [1, 3, 3, 3, 256, 256], replicated, may hold values from -0.078125 to 0.078125
- norm_gains: float32 [1, 256], replicated, may hold values from 0.5 to 2
- norm_shifts: float32 [1, 256], replicated, may hold values from -1 to 1
- cotangent: bfloat16 [4, 128, 16, 16, 256], P('dp', 'tm'), may hold values from -6 to 6
Outputs:
- outputs: bfloat16 [4, 128, 16, 16, 256], P('dp', 'tm')
- input_grads: bfloat16 [4, 128, 16, 16, 256], P('dp', 'tm')
- weight_grads: float32 [1, 27, 65536], P(None, None, ('dp', 'tm'))
The draws below stay inside these ranges and needn't reach their ends.
Inputs may be any that keep to these rules, and one draw needn't show every extreme that they name: `clip_lengths`: each row lists 6 clip lengths in frames, in order, summing to 128; the longest is exactly 48.
All inputs are finite; a program needn't handle non-finite values.
Results may differ from the reference program's by a relative error of at most 0.0034.
Values may be sent and summed in bfloat16 or wider, within the bound.
A program may use at most 128 MiB of HBM per device.

```python
import math
import jax
import jax.numpy as jnp
import numpy as np
from jax import lax

CHANNELS = 256
GROUPS = 32
BLOCKS = 1
TILE_H = 16
TILE_W = 16
CLIPS = 6
SEQS = 4
FRAMES = 128
MOST_CLIP = 48


def draw_video_tile(key, part):
    key = jax.random.fold_in(key, 17)
    base_key, frame_key, chan_key = jax.random.split(key, 3)
    full_shape = (SEQS, FRAMES, TILE_H, TILE_W, CHANNELS)
    frame_pos = jnp.arange(FRAMES, dtype=jnp.float32) / FRAMES
    frame_scale = jnp.exp(jax.random.uniform(frame_key, (SEQS, FRAMES), jnp.float32, math.log(0.25), math.log(2.5))) * (0.5 + frame_pos)[None, :]
    chan_scale = jnp.exp(jax.random.uniform(chan_key, (CHANNELS,), jnp.float32, math.log(0.5), math.log(2.0)))
    values = jax.random.truncated_normal(base_key, -4.0, 4.0, full_shape, jnp.float32)
    return (values * frame_scale[:, :, None, None, None] * chan_scale).astype(jnp.bfloat16)


def levels(key, dims, shards, least, largest):
    factor_of, own = 1.0, jax.random.fold_in(key, 6)
    for axis_at, blocks in shards:
        heights = jnp.exp(jax.random.uniform(jax.random.fold_in(own, axis_at), (blocks,), jnp.float32, least / len(shards), largest / len(shards)))
        factor_of = factor_of * jnp.repeat(heights, dims[axis_at] // blocks).reshape([-1 if axis == axis_at else 1 for axis in range(len(dims))])
    return factor_of


def split_up(count, total, bound, skew):
    weights = [(1 << 20) // math.isqrt(standing ** skew) + 1 for standing in range(2, count + 1)]
    spare, holding = total - bound - (count - 1), [1] * (count - 1)
    while spare > 0:
        candidates = [i for i in range(count - 1) if holding[i] < bound]
        whole, left = sum([weights[i] for i in candidates]), spare
        for i in candidates:
            more = min(bound - holding[i], max(1, left * weights[i] // whole), spare)
            holding[i] = holding[i] + more
            spare = spare - more
    return np.array([bound] + holding)


def uneven_parts(own_key, amount, total, limit, skew):
    if amount == 2:
        one = jax.random.randint(own_key, (), max(1, total - limit), min(limit, total - 1) + 1)
        return jnp.stack([one, total - one])
    sizes = jnp.asarray(split_up(amount, total, limit, skew), jnp.int32)
    twos = (amount - 1) // 2
    giver, receiver = sizes[1:1 + 2 * twos:2], sizes[2:2 + 2 * twos:2]
    slack = jnp.minimum(giver - 1, limit - receiver)
    shifted = jax.random.randint(jax.random.fold_in(own_key, 1), (twos,), 0, 1 << 20) % (slack + 1)
    sizes = sizes.at[1:1 + 2 * twos:2].set(giver - shifted).at[2:2 + 2 * twos:2].set(receiver + shifted)
    return sizes[jax.random.permutation(jax.random.fold_in(own_key, 2), amount)]


def scatter_about(stream_key, dims, deviation, reach, shards=(), kind=jnp.bfloat16):
    drawn = deviation * jax.random.normal(stream_key, dims, jnp.float32)
    if shards:
        drawn = drawn * levels(stream_key, dims, shards, -0.22, 0.18)
    return jnp.clip(drawn, -reach, reach).astype(kind)


def setup_inputs(seed: int = 0) -> dict:
    seeds = jax.random.split(jax.random.key(seed), 7)
    return {
        "video_tile": draw_video_tile(jax.random.fold_in(seeds[6], 71), 0),
        "clip_lengths": jax.vmap(lambda own: uneven_parts(own, CLIPS, FRAMES, MOST_CLIP, 2))(jax.random.split(seeds[1], SEQS)).reshape((SEQS, CLIPS)).astype(jnp.int32),
        "kernels": scatter_about(seeds[2], (BLOCKS, 3, 3, 3, CHANNELS, CHANNELS), (27 * CHANNELS) ** -0.5, 0.078125),
        "norm_gains": jnp.clip(jnp.exp(jax.random.uniform(seeds[3], (BLOCKS, CHANNELS), jnp.float32, math.log(0.5), math.log(2.0))), 0.5, 2.0),
        "norm_shifts": jnp.clip(jax.random.uniform(seeds[4], (BLOCKS, CHANNELS), jnp.float32, -1.0, 1.0), -1.0, 1.0),
        "cotangent": scatter_about(seeds[5], (SEQS, FRAMES, TILE_H, TILE_W, CHANNELS), 1.0, 6.0, ((0, 4), (1, 64))),
    }


EPS = 1e-05

def clip_of(moments, starts):
    return lax.optimization_barrier(jnp.sum((starts[None, :] <= moments[:, None]).astype(jnp.int32), axis=1)) - 1

def taps_forward(act_ext, kernel, keep_mask):
    frames = act_ext.shape[0] - 2
    height = act_ext.shape[1]
    tile_width = act_ext.shape[2]
    channels = act_ext.shape[3]
    padded = jnp.pad(act_ext, ((0, 0), (1, 1), (1, 1), (0, 0)))
    summed = jnp.zeros((frames * height * tile_width, channels), jnp.float32)
    for delay_step in range(3):
        factor = keep_mask[:, delay_step][:, None, None, None]
        for row_off in range(3):
            for col_off in range(3):
                sliced = padded[2 - delay_step:2 - delay_step + frames, row_off:row_off + height, col_off:col_off + tile_width] * factor
                summed = summed + jnp.dot(sliced.reshape(-1, channels), kernel[delay_step, row_off, col_off], preferred_element_type=jnp.float32)
    return summed.reshape(frames, height, tile_width, channels)

def taps_backward(cot_ext, kernel, back_mask):
    frames = cot_ext.shape[0] - 2
    height = cot_ext.shape[1]
    tile_width = cot_ext.shape[2]
    channels = cot_ext.shape[3]
    padded = jnp.pad(cot_ext, ((0, 0), (1, 1), (1, 1), (0, 0)))
    summed = jnp.zeros((frames * height * tile_width, channels), jnp.float32)
    for delay_step in range(3):
        factor = back_mask[delay_step:delay_step + frames, delay_step][:, None, None, None]
        for row_off in range(3):
            for col_off in range(3):
                sliced = padded[delay_step:delay_step + frames, 2 - row_off:2 - row_off + height, 2 - col_off:2 - col_off + tile_width] * factor
                summed = summed + jnp.dot(sliced.reshape(-1, channels), kernel[delay_step, row_off, col_off].T, preferred_element_type=jnp.float32)
    return summed.reshape(frames, height, tile_width, channels)

def taps_weights(act_ext, upstream, keep_mask):
    frames = act_ext.shape[0] - 2
    height = act_ext.shape[1]
    tile_width = act_ext.shape[2]
    channels = act_ext.shape[3]
    padded = jnp.pad(act_ext, ((0, 0), (1, 1), (1, 1), (0, 0)))
    flat_up = upstream.reshape(-1, channels)
    pieces = []
    for delay_step in range(3):
        factor = keep_mask[:, delay_step][:, None, None, None]
        for row_off in range(3):
            for col_off in range(3):
                sliced = padded[2 - delay_step:2 - delay_step + frames, row_off:row_off + height, col_off:col_off + tile_width] * factor
                pieces.append(lax.dot_general(sliced.reshape(-1, channels), flat_up, (((0,), (0,)), ((), ())), preferred_element_type=jnp.float32))
    return jnp.stack(pieces)

def grouped_view(values, groups):
    return values.astype(jnp.float32).reshape(values.shape[0], values.shape[1], values.shape[2], groups, -1)

def frame_sums(inputs, groups):
    grouped = grouped_view(inputs, groups)
    return (lax.optimization_barrier(jnp.sum(grouped, axis=(1, 2, 4))), lax.optimization_barrier(jnp.sum(grouped * grouped, axis=(1, 2, 4))))

def spread_groups(stat):
    return stat[:, None, None, :, None]

def normalize(inputs, first_cum, second_cum, counted, gain, offset, groups):
    per_frame = inputs.shape[1] * inputs.shape[2] * (inputs.shape[3] // groups)
    entries = counted[:, None] * per_frame
    group_mean = first_cum / entries
    variance = second_cum / entries - group_mean * group_mean
    inv_std = lax.rsqrt(variance + EPS)
    grouped = grouped_view(inputs, groups)
    unit = (grouped - spread_groups(group_mean)) * spread_groups(inv_std)
    normed = unit.reshape(inputs.shape) * gain + offset
    return (normed, jax.nn.silu(normed).astype(jnp.bfloat16), group_mean, inv_std, entries)

def norm_backward(inputs, normed, act_grad, group_mean, inv_std, entries, gain, groups):
    sigmoid = jax.nn.sigmoid(normed)
    slope = act_grad * sigmoid * (1.0 + normed * (1.0 - sigmoid))
    grouped_grad = (slope * gain).reshape(inputs.shape[0], inputs.shape[1], inputs.shape[2], groups, -1)
    centred = grouped_view(inputs, groups) - spread_groups(group_mean)
    radius_grad = lax.optimization_barrier(jnp.sum(grouped_grad * centred, axis=(1, 2, 4)))
    mean_grad = -lax.optimization_barrier(jnp.sum(grouped_grad, axis=(1, 2, 4))) * inv_std
    cubed = inv_std * inv_std * inv_std
    first_grad = (mean_grad + radius_grad * cubed * group_mean) / entries
    second_grad = -0.5 * radius_grad * cubed / entries
    direct = grouped_grad * spread_groups(inv_std)
    return (direct, first_grad, second_grad)

def finish(upstream, inputs, direct, first_back, second_back, groups):
    grouped = grouped_view(inputs, groups)
    summed = grouped_view(upstream, groups) + direct + spread_groups(first_back) + 2.0 * grouped * spread_groups(second_back)
    return summed.reshape(inputs.shape).astype(jnp.bfloat16)

def one_sequence(inputs, lengths, kernels, norm_gains, norm_shifts, cotangent):
    frames = inputs.shape[0]
    starts = jnp.cumsum(lengths) - lengths
    moments = jnp.arange(frames, dtype=jnp.int32)
    clips = clip_of(moments, starts)
    within = ((clips[:, None] == clips[None, :]) & (moments[None, :] <= moments[:, None])).astype(jnp.float32)
    counted = lax.optimization_barrier(jnp.sum(within, axis=1))
    keep_mask = jnp.stack([clip_of(moments - delay_step, starts) == clips for delay_step in range(3)], axis=1).astype(jnp.bfloat16)
    longer = jnp.arange(frames + 2, dtype=jnp.int32)
    longer_clips = clip_of(longer, starts)
    back_mask = jnp.stack([clip_of(longer - delay_step, starts) == longer_clips for delay_step in range(3)], axis=1).astype(jnp.bfloat16)
    carry_zero = jnp.zeros((2,) + inputs.shape[1:], jnp.bfloat16)
    stored = []
    current = inputs
    for layer_index in range(BLOCKS):
        first_sums, second_sums = frame_sums(current, GROUPS)
        first_cum = jnp.dot(within, first_sums, precision=lax.Precision.HIGHEST)
        second_cum = jnp.dot(within, second_sums, precision=lax.Precision.HIGHEST)
        normed, activation, group_mean, inv_std, entries = normalize(current, first_cum, second_cum, counted, norm_gains[layer_index], norm_shifts[layer_index], GROUPS)
        act_ext = jnp.concatenate([carry_zero, activation], axis=0)
        conv_out = taps_forward(act_ext, kernels[layer_index], keep_mask)
        stored.append((current, normed, group_mean, inv_std, entries, act_ext))
        current = (current.astype(jnp.float32) + conv_out).astype(jnp.bfloat16)
    upstream = cotangent
    weight_terms = [None] * BLOCKS
    for layer_index in reversed(range(BLOCKS)):
        held, normed, group_mean, inv_std, entries, act_ext = stored[layer_index]
        cot_ext = jnp.concatenate([upstream, carry_zero], axis=0)
        act_grad = taps_backward(cot_ext, kernels[layer_index], back_mask)
        weight_terms[layer_index] = taps_weights(act_ext, upstream, keep_mask)
        direct, first_grad, second_grad = norm_backward(held, normed, act_grad, group_mean, inv_std, entries, norm_gains[layer_index], GROUPS)
        first_back = jnp.dot(within.T, first_grad, precision=lax.Precision.HIGHEST)
        second_back = jnp.dot(within.T, second_grad, precision=lax.Precision.HIGHEST)
        upstream = finish(upstream, held, direct, first_back, second_back, GROUPS)
    return (current, upstream, jnp.stack(weight_terms))

def reference(video_tile, clip_lengths, kernels, norm_gains, norm_shifts, cotangent):
    results = [one_sequence(video_tile[sequence], clip_lengths[sequence], kernels, norm_gains, norm_shifts, cotangent[sequence]) for sequence in range(SEQS)]
    outputs = jnp.stack([entry[0] for entry in results])
    input_grads = jnp.stack([entry[1] for entry in results])
    scale_factor = 1.0 / math.sqrt(SEQS * FRAMES * TILE_H * TILE_W)
    weight_sum = lax.optimization_barrier(jnp.sum(jnp.stack([entry[2] for entry in results]), axis=0)) * scale_factor
    weight_grads = weight_sum.reshape(BLOCKS, 27, CHANNELS * CHANNELS)
    return (outputs, input_grads, weight_grads)
```

```python
import functools
import math

import jax
import jax.numpy as jnp
from jax import lax
from jax.experimental import pallas as pl
from jax.experimental.pallas import tpu as pltpu
from jax.sharding import PartitionSpec as P

EPS = 1e-05
NX = 4
NC = 2
GROUP = NX * NC
TAPS = 27
X_SLOTS = ((0, 5), (5, 4), (9, 5))
Y_SLOTS = ((0, 4), (4, 5), (9, 4))
MESH = pl.DeviceIdType.MESH
F32 = jnp.float32
BF16 = jnp.bfloat16


def iota(shape, dim):
    return lax.broadcasted_iota(jnp.int32, shape, dim)


def clip_begin(starts, t):
    begin = jnp.int32(0)
    for start in starts:
        begin = jnp.where(start <= t, start, begin)
    return begin


def clip_end(starts, t, frames):
    end = jnp.int32(frames)
    for start in reversed(starts):
        end = jnp.where(start > t, start, end)
    return end


def flag(condition):
    return jnp.where(condition, jnp.float32(1.0), jnp.float32(0.0))


def dot(a, b, contract=(1, 0), precision=None):
    return lax.dot_general(
        a,
        b,
        (((contract[0],), (contract[1],)), ((), ())),
        preferred_element_type=F32,
        precision=precision,
    )


def sigmoid(z):
    return 0.5 * jnp.tanh(0.5 * z) + 0.5


def pack_rows(rows):
    place = iota((8, 256), 0)
    stacked = jnp.zeros((8, 256), F32)
    for k, row in enumerate(rows):
        stacked = jnp.where(place == k, row, stacked)
    gather = ((iota((256, 128), 0) >> 3) == (iota((256, 128), 1) & 31)).astype(F32)
    grouped = dot(stacked, gather, precision=lax.Precision.HIGHEST)
    mine = (iota((8, 128), 1) >> 5) == iota((8, 128), 0)
    return jnp.sum(jnp.where(mine, grouped, 0.0), axis=0, keepdims=True)


def spread(rows):
    lanes = iota((8, 128), 1)
    clean = jnp.where(lanes < 32, rows, 0.0)
    matrix = (iota((128, 256), 0) == (iota((128, 256), 1) >> 3)).astype(F32)
    return dot(clean, matrix, precision=lax.Precision.HIGHEST)


def masked_rows(buffer, bounds):
    values = buffer[...]
    frame = 2 * iota(values.shape, 0) + (iota(values.shape, 2) >> 6)
    place = iota((8, 128), 0)
    rows = jnp.zeros((8, 128), F32)
    for k, (low, high) in enumerate(bounds):
        inside = (frame >= low) & (frame < high)
        total = jnp.sum(jnp.where(inside, values, 0.0), axis=0)
        rows = jnp.where(place == k, total, rows)
    return rows + pltpu.roll(rows, 64, 1)


def kernel(
    nz,
    ny,
    scale,
    lens,
    gain,
    shift,
    video,
    cot,
    kern,
    out,
    grads,
    wgrads,
    xw,
    gwin,
    kv,
    gim,
    aim,
    act,
    lhs,
    stat,
    dstat,
    mean_rows,
    scale_rows,
    inv_rows,
    da,
    sx1,
    rx1,
    sy1,
    ry1,
    sx2,
    rx2,
    sy2,
    ry2,
    total3,
    s3,
    r3,
    out_v,
    grads_v,
    load_sem,
    halo_send,
    halo_recv,
    chain_send,
    chain_recv,
    one_send,
    one_recv,
    two_send,
    two_recv,
    three_send,
    three_recv,
    store_sem,
):
    y = lax.axis_index("dp")
    tm = lax.axis_index("tm")
    core = lax.rem(tm, NC)
    x = lax.rem(tm // NC, NX)
    z = tm // GROUP
    within = lax.rem(tm, GROUP)
    chip = tm // NC
    chips = nz * NX
    frames = 2 * nz * GROUP
    base = 4 * chip
    own = 2 * tm

    def at(tm_index, dp_index=None):
        return {"dp": y if dp_index is None else dp_index, "tm": tm_index}

    def x_peer(d):
        return z * GROUP + lax.rem(x + d, NX) * NC + core

    def z_peer(d):
        return lax.rem(z + d, nz) * GROUP + within

    def y_peer(d):
        return lax.rem(y + d, ny)

    def group_peer(d):
        return z * GROUP + lax.rem(within + d, GROUP)

    next_chip = lax.rem(chip + 1, chips)
    prev_chip = lax.rem(chip + chips - 1, chips)

    load_x = pltpu.make_async_copy(video.at[0], xw.at[pl.ds(2 + 2 * core, 2)], load_sem.at[0])
    load_g = pltpu.make_async_copy(cot.at[0], gwin.at[pl.ds(2 * core, 2)], load_sem.at[1])
    load_k = [
        pltpu.make_async_copy(kern.at[0, lag], kv.at[lag], load_sem.at[2 + lag]) for lag in range(3)
    ]
    load_x.start()
    load_g.start()

    barrier = pltpu.get_barrier_semaphore()

    def greet(device):
        pl.semaphore_signal(barrier, inc=1, device_id=device, device_id_type=MESH)

    def greet_group(d, carry):
        greet(at(group_peer(d)))
        return carry

    def greet_z(d, carry):
        greet(at(z_peer(d)))
        return carry

    def greet_y(d, carry):
        greet(at(tm, y_peer(d)))
        return carry

    lax.fori_loop(1, GROUP, greet_group, 0)
    lax.fori_loop(1, nz, greet_z, 0)
    lax.fori_loop(1, ny, greet_y, 0)
    for c in range(NC):
        greet(at(next_chip * NC + c))
        greet(at(prev_chip * NC + c))
    for copy in load_k:
        copy.start()

    starts = []
    begin = jnp.int32(0)
    for k in range(6):
        starts.append(begin)
        begin = begin + lens[0, k]

    load_x.wait()
    sums = []
    for f in range(2):
        values = xw[2 + 2 * core + f].reshape(256, 256).astype(F32)
        sums.append(jnp.sum(values, axis=0, keepdims=True))
        sums.append(jnp.sum(values * values, axis=0, keepdims=True))
    stat[pl.ds(tm, 1)] = pack_rows(sums).reshape(1, 1, 128)

    pl.semaphore_wait(barrier, (GROUP - 1) + (nz - 1) + (ny - 1) + 2 * NC)

    def first_copy(buffer, kind, d):
        mine = buffer.at[pl.ds(tm, 1)]
        return pltpu.make_async_remote_copy(
            src_ref=mine,
            dst_ref=mine,
            send_sem=chain_send.at[kind, d],
            recv_sem=chain_recv.at[kind, d],
            device_id=at(group_peer(d)),
            device_id_type=MESH,
        )

    def second_copy(buffer, kind, d):
        mine = buffer.at[pl.ds(z * GROUP, GROUP)]
        return pltpu.make_async_remote_copy(
            src_ref=mine,
            dst_ref=mine,
            send_sem=chain_send.at[kind, d],
            recv_sem=chain_recv.at[kind, d],
            device_id=at(z_peer(d)),
            device_id_type=MESH,
        )

    def loop(count, act_on):
        def body(d, carry):
            act_on(d)
            return carry

        lax.fori_loop(1, count, body, 0)

    loop(GROUP, lambda d: first_copy(stat, 0, d).start())

    def halo(src, dst, sent, received, device):
        return pltpu.make_async_remote_copy(
            src_ref=src,
            dst_ref=dst,
            send_sem=halo_send.at[sent],
            recv_sem=halo_recv.at[received],
            device_id=at(device),
            device_id_type=MESH,
        )

    partner = chip * NC + 1 - core
    own_g = gwin.at[pl.ds(2 * core, 2)]
    own_x = xw.at[pl.ds(2 + 2 * core, 2)]
    after_g = gwin.at[pl.ds(4, 2)]
    g_partner = halo(cot.at[0], own_g, 0, 0, partner)
    x_partner = halo(video.at[0], own_x, 1, 1, partner)
    g_back = [halo(cot.at[0], after_g, 2 + c, 2, prev_chip * NC + c) for c in range(NC)]
    x_ahead = halo(video.at[0], xw.at[pl.ds(0, 2)], 4, 3, next_chip * NC)
    g_partner.start()

    @pl.when(core == 0)
    def _():
        g_back[1].start()
        g_back[0].start()

    x_partner.start()

    @pl.when(core == 1)
    def _():
        x_ahead.start()

    pixel, source = iota((256, 256), 0), iota((256, 256), 1)
    right = ((source == pixel + 1) & ((pixel & 15) != 15)).astype(BF16)
    left = ((source == pixel - 1) & ((pixel & 15) != 0)).astype(BF16)
    both = jnp.concatenate([right, left], axis=0)

    def widen(target, k, values, first, last):
        shifted = dot(both, values).astype(BF16)
        target[k, 1:17, :, 256 * first : 256 * first + 256] = shifted[:256].reshape(16, 16, 256)
        target[k, 1:17, :, 256:512] = values.reshape(16, 16, 256)
        target[k, 1:17, :, 256 * last : 256 * last + 256] = shifted[256:].reshape(16, 16, 256)
        target[k, 0:1] = jnp.zeros((1, 16, 768), BF16)
        target[k, 17:18] = jnp.zeros((1, 16, 768), BF16)

    def widen_g(v, carry):
        widen(gim, v, gwin[v].reshape(256, 256), 0, 2)
        return carry

    load_g.wait()
    g_partner.wait_recv()
    lax.fori_loop(0, 4, widen_g, 0)

    loop(GROUP, lambda d: first_copy(stat, 0, d).wait_recv())
    loop(nz, lambda d: second_copy(stat, 1, d).start())

    g_back[1].wait_recv()
    lax.fori_loop(4, 6, widen_g, 0)
    for copy in load_k:
        copy.wait()

    for lag in range(3):
        taken = jnp.concatenate(
            [
                gim[pl.ds(2 * core + lag, 2), 2 - i : 18 - i].reshape(512, 768)
                for i in range(3)
            ],
            axis=1,
        )
        weights = jnp.concatenate(
            [kv[lag, i, j] for i in range(3) for j in range(3)], axis=1
        )
        part = dot(taken, weights, (1, 1))
        for f in range(2):
            piece = part[256 * f : 256 * f + 256]
            if lag == 0:
                da[f] = piece
            else:
                keep = flag(own + f + lag < clip_end(starts, own + f, frames))
                da[f] = da[f] + keep * piece

    loop(nz, lambda d: second_copy(stat, 1, d).wait_recv())
    bounds, counted = [], jnp.zeros((8, 128), F32)
    for k in range(6):
        t = base - 2 + k
        b = clip_begin(starts, t)
        bounds.append((b, t + 1))
        count = jnp.maximum(t + 1 - b, 1).astype(F32)
        counted = jnp.where(iota((8, 128), 0) == k, count, counted)
    counted = jnp.maximum(counted, 1.0) * 2048.0
    averaged = masked_rows(stat, bounds) / counted
    squares = pltpu.roll(averaged, 96, 1)
    inv_std = lax.rsqrt(squares - averaged * averaged + EPS)
    mean_rows[...] = spread(averaged)
    wide_inv = spread(inv_std)
    inv_rows[...] = wide_inv
    scale_rows[...] = wide_inv * gain[...]

    def activate(k, carry):
        values = xw[k].reshape(256, 256).astype(F32)
        normed = (values - mean_rows[pl.ds(k, 1)]) * scale_rows[pl.ds(k, 1)] + shift[...]
        act[k] = (normed * sigmoid(normed)).astype(BF16)
        return carry

    x_partner.wait_recv()
    lax.fori_loop(2, 6, activate, 0)

    row, channel = iota((128, 256), 0), iota((128, 256), 1)
    wanted = 64 * ((row >> 3) & 3) + 8 * (row & 7) + 2 * (row >> 5) + core
    select = (channel == wanted).astype(BF16)
    blank = jnp.zeros((128, 256), BF16)
    for lag, v in ((0, 4), (0, 5), (1, 0), (1, 5), (2, 0), (2, 1)):
        lhs[128 * lag : 128 * lag + 128, 256 * v : 256 * v + 256] = blank
    for u in range(4):
        turned = dot(select, act[2 + u], (1, 1))
        end = clip_end(starts, base + u, frames)
        for lag in range(3):
            masked = turned if lag == 0 else turned * flag(base + u + lag < end)
            v = u + lag
            lhs[128 * lag : 128 * lag + 128, 256 * v : 256 * v + 256] = masked.astype(BF16)

    def one_x(i, d):
        low, count = X_SLOTS[i]
        target = lax.rem(x + d, NX)
        return pltpu.make_async_remote_copy(
            src_ref=sx1.at[target, pl.ds(low, count)],
            dst_ref=rx1.at[d, pl.ds(low, count)],
            send_sem=one_send.at[0, i, d],
            recv_sem=one_recv.at[0, i, d],
            device_id=at(x_peer(d)),
            device_id_type=MESH,
        )

    def one_y(i, d):
        low, count = Y_SLOTS[i]
        target = lax.rem(y + d, ny)
        return pltpu.make_async_remote_copy(
            src_ref=sy1.at[target, pl.ds(low, count)],
            dst_ref=ry1.at[d, pl.ds(low, count)],
            send_sem=one_send.at[1, i, d],
            recv_sem=one_recv.at[1, i, d],
            device_id=at(tm, y_peer(d)),
            device_id_type=MESH,
        )

    for i in range(3):
        terms = dot(lhs[...], gim[:, 2 - i : 18 - i].reshape(1536, 768))
        for lag in range(3):
            for j in range(3):
                n = 9 * i + 3 * lag + j
                block = terms[128 * lag : 128 * lag + 128, 256 * j : 256 * j + 256]
                for p in range(4):
                    if n % 2 == 0:
                        sx1[p, n // 2] = block[32 * p : 32 * p + 32].astype(BF16)
                    else:
                        rows = [block[32 * q + 8 * p : 32 * q + 8 * p + 8] for q in range(4)]
                        sy1[p, n // 2] = jnp.concatenate(rows, axis=0).astype(BF16)
        for d in (2, 1, 3):
            one_x(i, d).start()
            one_y(i, d).start()

    @pl.when(core == 0)
    def _():
        x_ahead.wait_recv()
        lax.fori_loop(0, 2, activate, 0)

    def widen_a(k, carry):
        widen(aim, k, act[2 * core + k], 2, 0)
        return carry

    lax.fori_loop(0, 4, widen_a, 0)
    for lag in range(3):
        taken = jnp.concatenate(
            [aim[2 - lag : 4 - lag, i : i + 16].reshape(512, 768) for i in range(3)], axis=1
        )
        part = dot(taken, kv[lag].reshape(2304, 256))
        for f in range(2):
            piece = part[256 * f : 256 * f + 256]
            if lag == 0:
                total = xw[2 + 2 * core + f].reshape(256, 256).astype(F32) + piece
            else:
                keep = flag(own + f - lag >= clip_begin(starts, own + f))
                total = total_f[f] + keep * piece
            if f == 0:
                first = total
            else:
                total_f = [first, total]
    for f in range(2):
        out_v[f] = total_f[f].reshape(16, 16, 256).astype(BF16)
    store_out = pltpu.make_async_copy(out_v, out.at[0], store_sem.at[0])
    store_out.start()

    lanes = iota((1, 128), 1)
    sums = []
    for f in range(2):
        k = 2 + 2 * core + f
        centred = xw[k].reshape(256, 256).astype(F32) - mean_rows[pl.ds(k, 1)]
        normed = centred * scale_rows[pl.ds(k, 1)] + shift[...]
        sig = sigmoid(normed)
        du = da[f] * (sig * (1.0 + normed * (1.0 - sig))) * gain[...]
        da[f] = du
        sums.append(jnp.sum(du, axis=0, keepdims=True))
        sums.append(jnp.sum(du * centred, axis=0, keepdims=True))
    packed = pack_rows(sums)
    row_of = iota((8, 128), 0)

    def pick(rows, k):
        return jnp.sum(jnp.where(row_of == k, rows, 0.0), axis=0, keepdims=True)

    answer = jnp.zeros((1, 128), F32)
    for f in range(2):
        k = 2 + 2 * core + f
        mean_k, inv_k, n_k = pick(averaged, k), pick(inv_std, k), pick(counted, k)
        sum_du = pltpu.roll(packed, 64, 1) if f else packed
        dr = pltpu.roll(sum_du, 96, 1)
        cubed = inv_k * inv_k * inv_k
        dc1 = (dr * cubed * mean_k - inv_k * sum_du) / n_k
        dc2 = -0.5 * dr * cubed / n_k
        dc2 = pltpu.roll(dc2, 32, 1)
        pair = jnp.where(lanes < 32, dc1, jnp.where(lanes < 64, dc2, 0.0))
        answer = answer + (pltpu.roll(pair, 64, 1) if f else pair)
    dstat[pl.ds(tm, 1)] = answer.reshape(1, 1, 128)
    loop(GROUP, lambda d: first_copy(dstat, 2, d).start())

    def two_x(d):
        return pltpu.make_async_remote_copy(
            src_ref=sx2.at[lax.rem(y + d, ny)],
            dst_ref=rx2.at[d],
            send_sem=two_send.at[0, d],
            recv_sem=two_recv.at[0, d],
            device_id=at(tm, y_peer(d)),
            device_id_type=MESH,
        )

    def two_y(d):
        return pltpu.make_async_remote_copy(
            src_ref=sy2.at[lax.rem(x + d, NX)],
            dst_ref=ry2.at[d],
            send_sem=two_send.at[1, d],
            recv_sem=two_recv.at[1, d],
            device_id=at(x_peer(d)),
            device_id_type=MESH,
        )

    def three(d):
        return pltpu.make_async_remote_copy(
            src_ref=s3.at[lax.rem(z + d, nz)],
            dst_ref=r3.at[d],
            send_sem=three_send.at[d],
            recv_sem=three_recv.at[d],
            device_id=at(z_peer(d)),
            device_id_type=MESH,
        )

    loop(GROUP, lambda d: first_copy(dstat, 2, d).wait_recv())
    loop(nz, lambda d: second_copy(dstat, 3, d).start())

    for i in range(3):
        for d in range(1, NX):
            one_x(i, d).wait_recv()
    for p in range(4):
        rows = pl.ds(8 * p, 8)
        half = sx1[x, :, 16 * (p // 2) : 16 * (p // 2) + 16].astype(F32)
        for d in range(1, NX):
            half = half + rx1[d, :, 16 * (p // 2) : 16 * (p // 2) + 16].astype(F32)
        piece = half[:, 8 * (p % 2) : 8 * (p % 2) + 8]
        sx2[p] = piece.reshape(112, 256).astype(BF16)
    for d in (2, 1, 3):
        two_x(d).start()
    for i in range(3):
        for d in range(1, ny):
            one_y(i, d).wait_recv()
    for p in range(4):
        half = sy1[y, :, 16 * (p // 2) : 16 * (p // 2) + 16].astype(F32)
        for d in range(1, ny):
            half = half + ry1[d, :, 16 * (p // 2) : 16 * (p // 2) + 16].astype(F32)
        piece = half[:, 8 * (p % 2) : 8 * (p % 2) + 8].reshape(104, 256)
        sy2[p] = jnp.concatenate([piece, jnp.zeros((8, 256), F32)], axis=0).astype(BF16)
    for d in (2, 1, 3):
        two_y(d).start()

    loop(nz, lambda d: second_copy(dstat, 3, d).wait_recv())
    bounds = [(own + f, clip_end(starts, own + f, frames)) for f in range(2)]
    backs = masked_rows(dstat, bounds)
    back_one = spread(backs)
    back_two = spread(pltpu.roll(backs, 96, 1))
    for f in range(2):
        k = 2 + 2 * core + f
        values = xw[k].reshape(256, 256).astype(F32)
        result = (
            gwin[2 * core + f].reshape(256, 256).astype(F32)
            + da[f] * inv_rows[pl.ds(k, 1)]
            + back_one[f : f + 1]
            + values * (2.0 * back_two[f : f + 1])
        )
        grads_v[f] = result.reshape(16, 16, 256).astype(BF16)
    store_grads = pltpu.make_async_copy(grads_v, grads.at[0], store_sem.at[1])
    store_grads.start()

    for d in range(1, ny):
        two_x(d).wait_recv()
    summed = sx2[y].astype(F32)
    for d in range(1, ny):
        summed = summed + rx2[d].astype(F32)
    for h in range(2):
        total3[h, 0:112] = summed[:, 128 * h : 128 * h + 128]
    for d in range(1, NX):
        two_y(d).wait_recv()
    summed = sy2[x].astype(F32)
    for d in range(1, NX):
        summed = summed + ry2[d].astype(F32)
    for h in range(2):
        total3[h, 112:224] = summed[:, 128 * h : 128 * h + 128]
        total3[h, 224:256] = jnp.zeros((32, 128), F32)
        for q in range(nz):
            s3[q, :, 128 * h : 128 * h + 128] = total3[h, pl.ds(q, 32, stride=8)].astype(BF16)
    loop(nz, lambda d: three(d).start())
    loop(nz, lambda d: three(d).wait_recv())
    summed = s3[z].astype(F32)
    for d in range(1, nz):
        summed = summed + r3[d].astype(F32)
    summed = summed * scale
    for n in range(TAPS):
        i, lag, j = n // 9, n % 9 // 3, n % 3
        slot = n // 2 + 14 * (n % 2)
        to = 9 * lag + 3 * i + j
        wgrads[0, to : to + 1] = summed[slot : slot + 1]

    loop(GROUP, lambda d: first_copy(stat, 0, d).wait_send())
    loop(nz, lambda d: second_copy(stat, 1, d).wait_send())
    loop(GROUP, lambda d: first_copy(dstat, 2, d).wait_send())
    loop(nz, lambda d: second_copy(dstat, 3, d).wait_send())
    g_partner.wait_send()
    x_partner.wait_send()

    @pl.when(core == 0)
    def _():
        g_back[0].wait_send()
        g_back[1].wait_send()

    @pl.when(core == 1)
    def _():
        x_ahead.wait_send()

    for i in range(3):
        for d in range(1, 4):
            one_x(i, d).wait_send()
            one_y(i, d).wait_send()
    for d in range(1, 4):
        two_x(d).wait_send()
        two_y(d).wait_send()
    loop(nz, lambda d: three(d).wait_send())
    store_out.wait()
    store_grads.wait()


def local(nz, ny, scale, video_tile, clip_lengths, kernels, norm_gains, norm_shifts, cotangent):
    anywhere = pl.BlockSpec(memory_space=pl.ANY)
    vmem = pl.BlockSpec(memory_space=pltpu.VMEM)
    smem = pl.BlockSpec(memory_space=pltpu.SMEM)
    dma = pltpu.SemaphoreType.DMA
    return pl.pallas_call(
        functools.partial(kernel, nz, ny, scale),
        out_shape=(
            jax.ShapeDtypeStruct(video_tile.shape, BF16),
            jax.ShapeDtypeStruct(video_tile.shape, BF16),
            jax.ShapeDtypeStruct((1, TAPS, 256), F32),
        ),
        in_specs=[smem, vmem, vmem, anywhere, anywhere, anywhere],
        out_specs=(anywhere, anywhere, vmem),
        scratch_shapes=[
            pltpu.VMEM((6, 16, 16, 256), BF16),
            pltpu.VMEM((6, 16, 16, 256), BF16),
            pltpu.VMEM((3, 3, 3, 256, 256), BF16),
            pltpu.VMEM((6, 18, 16, 768), BF16),
            pltpu.VMEM((4, 18, 16, 768), BF16),
            pltpu.VMEM((6, 256, 256), BF16),
            pltpu.VMEM((384, 1536), BF16),
            pltpu.VMEM((nz * GROUP, 1, 128), F32),
            pltpu.VMEM((nz * GROUP, 1, 128), F32),
            pltpu.VMEM((8, 256), F32),
            pltpu.VMEM((8, 256), F32),
            pltpu.VMEM((8, 256), F32),
            pltpu.VMEM((2, 256, 256), F32),
            pltpu.VMEM((4, 14, 32, 256), BF16),
            pltpu.VMEM((4, 14, 32, 256), BF16),
            pltpu.VMEM((4, 13, 32, 256), BF16),
            pltpu.VMEM((4, 13, 32, 256), BF16),
            pltpu.VMEM((4, 112, 256), BF16),
            pltpu.VMEM((4, 112, 256), BF16),
            pltpu.VMEM((4, 112, 256), BF16),
            pltpu.VMEM((4, 112, 256), BF16),
            pltpu.VMEM((2, 256, 128), F32),
            pltpu.VMEM((8, 32, 256), BF16),
            pltpu.VMEM((8, 32, 256), BF16),
            pltpu.VMEM((2, 16, 16, 256), BF16),
            pltpu.VMEM((2, 16, 16, 256), BF16),
            dma((5,)),
            dma((5,)),
            dma((4,)),
            dma((4, 8)),
            dma((4, 8)),
            dma((2, 3, 4)),
            dma((2, 3, 4)),
            dma((2, 4)),
            dma((2, 4)),
            dma((8,)),
            dma((8,)),
            dma((2,)),
        ],
        compiler_params=pltpu.CompilerParams(
            collective_id=0, has_side_effects=True, vmem_limit_bytes=48 * 1024 * 1024
        ),
        cost_estimate=pl.CostEstimate(flops=5_500_000_000, bytes_accessed=5_000_000, transcendentals=400_000),
    )(clip_lengths, norm_gains, norm_shifts, video_tile, cotangent, kernels)


def solution(mesh):
    ny, tm = mesh.shape["dp"], mesh.shape["tm"]
    nz = tm // GROUP
    scale = 1.0 / math.sqrt(ny * tm * 2 * 256)
    placed = P("dp", "tm", None, None, None)
    return jax.shard_map(
        functools.partial(local, nz, ny, scale),
        mesh=mesh,
        in_specs=(placed, P("dp", None), P(), P(), P(), placed),
        out_specs=(placed, placed, P(None, None, ("dp", "tm"))),
        check_vma=False,
    )
```

```python
import functools
import math

import jax
import jax.numpy as jnp
from jax import lax
from jax.experimental import pallas as pl
from jax.experimental.pallas import tpu as pltpu
from jax.sharding import PartitionSpec as P

EPS = 1e-05
NX = 4
NC = 2
GROUP = NX * NC
TAPS = 27
REACH = 12
MESH = pl.DeviceIdType.MESH
F32 = jnp.float32
BF16 = jnp.bfloat16
Z_TAPS = 5
PIECES = ((0, 2), (2, 4), (6, 5))
HALVES = ((0, 6), (6, 5))


def place_of(n):
    if n < Z_TAPS:
        return "z", n
    return "xy"[(n - Z_TAPS) % 2], (n - Z_TAPS) // 2


def iota(shape, dim):
    return lax.broadcasted_iota(jnp.int32, shape, dim)


def clip_begin(starts, t):
    begin = jnp.int32(0)
    for start in starts:
        begin = jnp.where(start <= t, start, begin)
    return begin


def clip_end(starts, t, frames):
    end = jnp.int32(frames)
    for start in reversed(starts):
        end = jnp.where(start > t, start, end)
    return end


def flag(condition):
    return jnp.where(condition, jnp.float32(1.0), jnp.float32(0.0))


def dot(a, b, contract=(1, 0), precision=None):
    return lax.dot_general(
        a,
        b,
        (((contract[0],), (contract[1],)), ((), ())),
        preferred_element_type=F32,
        precision=precision,
    )


def sigmoid(z):
    return 0.5 * jnp.tanh(0.5 * z) + 0.5


def pack_rows(rows):
    place = iota((8, 256), 0)
    stacked = jnp.zeros((8, 256), F32)
    for k, row in enumerate(rows):
        stacked = jnp.where(place == k, row, stacked)
    gather = ((iota((256, 128), 0) >> 3) == (iota((256, 128), 1) & 31)).astype(F32)
    grouped = dot(stacked, gather, precision=lax.Precision.HIGHEST)
    mine = (iota((8, 128), 1) >> 5) == iota((8, 128), 0)
    return jnp.sum(jnp.where(mine, grouped, 0.0), axis=0, keepdims=True)


def spread(rows):
    lanes = iota((8, 128), 1)
    clean = jnp.where(lanes < 32, rows, 0.0)
    matrix = (iota((128, 256), 0) == (iota((128, 256), 1) >> 3)).astype(F32)
    return dot(clean, matrix, precision=lax.Precision.HIGHEST)


def masked_rows(buffer, bounds):
    values = buffer[...]
    frame = 2 * iota(values.shape, 0) + (iota(values.shape, 2) >> 6)
    place = iota((8, 128), 0)
    rows = jnp.zeros((8, 128), F32)
    for k, (low, high) in enumerate(bounds):
        inside = (frame >= low) & (frame < high)
        total = jnp.sum(jnp.where(inside, values, 0.0), axis=0)
        rows = jnp.where(place == k, total, rows)
    return rows + pltpu.roll(rows, 64, 1)


def kernel(
    nz,
    ny,
    scale,
    lens_hbm,
    gain_hbm,
    shift_hbm,
    video,
    cot,
    kern,
    out,
    grads,
    wgrads,
    lens,
    gain,
    shift,
    xw,
    gwin,
    kv,
    gim,
    aim,
    act,
    lhs,
    stat,
    dstat,
    mean_rows,
    scale_rows,
    inv_rows,
    da,
    sx1,
    rx1,
    sy1,
    ry1,
    sz1,
    rz1,
    sx2,
    rx2,
    sy2,
    ry2,
    sz2,
    rz2,
    sz3,
    rz3,
    kx2,
    ky2,
    turn,
    total3,
    s3,
    r3,
    out_v,
    grads_v,
    load_sem,
    halo_send,
    halo_recv,
    chain_send,
    chain_recv,
    one_send,
    one_recv,
    two_send,
    two_recv,
    three_send,
    three_recv,
    store_sem,
):
    y = lax.axis_index("dp")
    tm = lax.axis_index("tm")
    core = lax.rem(tm, NC)
    x = lax.rem(tm // NC, NX)
    z = tm // GROUP
    within = lax.rem(tm, GROUP)
    chip = tm // NC
    chips = nz * NX
    frames = 2 * nz * GROUP
    base = 4 * chip
    own = 2 * tm

    def at(tm_index, dp_index=None):
        return {"dp": y if dp_index is None else dp_index, "tm": tm_index}

    def x_peer(d):
        return z * GROUP + lax.rem(x + d, NX) * NC + core

    def z_peer(d):
        return lax.rem(z + d, nz) * GROUP + within

    def y_peer(d):
        return lax.rem(y + d, ny)

    def chip_peer(d):
        return lax.rem(chip + d, chips) * NC + core

    partner = chip * NC + 1 - core

    beside = lax.rem(tm + 2 * core - 1 + 2 * chips, 2 * chips)

    stat[...] = jnp.zeros(stat.shape, F32)
    dstat[...] = jnp.zeros(dstat.shape, F32)

    load_x = pltpu.make_async_copy(video.at[0], xw.at[pl.ds(2 + 2 * core, 2)], load_sem.at[0])
    load_g = pltpu.make_async_copy(cot.at[0], gwin.at[pl.ds(2 * core, 2)], load_sem.at[1])
    load_k = [
        pltpu.make_async_copy(kern.at[0, lag], kv.at[lag], load_sem.at[2 + lag]) for lag in range(3)
    ]
    load_small = [
        pltpu.make_async_copy(src, dst, load_sem.at[5 + k])
        for k, (src, dst) in enumerate(((lens_hbm, lens), (gain_hbm, gain), (shift_hbm, shift)))
    ]
    load_x.start()
    load_g.start()
    for copy in load_small:
        copy.start()

    barrier = pltpu.get_barrier_semaphore()

    def greet(device):
        pl.semaphore_signal(barrier, inc=1, device_id=device, device_id_type=MESH)

    def greet_chips(d, carry):
        greet(at(chip_peer(d)))
        greet(at(chip_peer(chips - d)))
        return carry

    lax.fori_loop(1, REACH + 1, greet_chips, 0)
    far = range(REACH // NX + 1, nz - REACH // NX)
    for d in far:
        greet(at(z_peer(d)))
    for d in range(1, ny):
        greet(at(tm, y_peer(d)))
    greet(at(partner))
    greet(at(beside))
    for copy in load_k:
        copy.start()

    for copy in load_small:
        copy.wait()
    starts = []
    begin = jnp.int32(0)
    for k in range(6):
        starts.append(begin)
        begin = begin + lens[0, k]

    load_x.wait()
    sums = []
    for f in range(2):
        values = xw[2 + 2 * core + f].reshape(256, 256).astype(F32)
        sums.append(jnp.sum(values, axis=0, keepdims=True))
        sums.append(jnp.sum(values * values, axis=0, keepdims=True))
    stat[pl.ds(tm, 1)] = pack_rows(sums).reshape(1, 1, 128)

    pl.semaphore_wait(barrier, 2 * REACH + len(far) + (ny - 1) + 2)

    def first_copy(buffer, kind):
        mine = buffer.at[pl.ds(tm, 1)]
        return pltpu.make_async_remote_copy(
            src_ref=mine,
            dst_ref=mine,
            send_sem=chain_send.at[kind, 0],
            recv_sem=chain_recv.at[kind, 0],
            device_id=at(partner),
            device_id_type=MESH,
        )

    def second_copy(buffer, kind, d):
        mine = buffer.at[pl.ds(NC * chip, NC)]
        step = d if kind == 0 else chips - d
        return pltpu.make_async_remote_copy(
            src_ref=mine,
            dst_ref=mine,
            send_sem=chain_send.at[kind, d],
            recv_sem=chain_recv.at[kind, d],
            device_id=at(chip_peer(step)),
            device_id_type=MESH,
        )

    def loop(count, act_on):
        def body(d, carry):
            act_on(d)
            return carry

        lax.fori_loop(1, count, body, 0)

    first_copy(stat, 0).start()

    def halo(src, dst, sent, received, device):
        return pltpu.make_async_remote_copy(
            src_ref=src,
            dst_ref=dst,
            send_sem=halo_send.at[sent],
            recv_sem=halo_recv.at[received],
            device_id=at(device),
            device_id_type=MESH,
        )

    own_g = gwin.at[pl.ds(2 * core, 2)]
    own_x = xw.at[pl.ds(2 + 2 * core, 2)]
    after_g = gwin.at[pl.ds(4, 2)]
    g_partner = halo(cot.at[0], own_g, 0, 0, partner)
    x_partner = halo(video.at[0], own_x, 1, 1, partner)
    g_back = halo(cot.at[0], after_g, 2, 2, beside)
    g_relay = halo(after_g, after_g, 2, 2, partner)
    x_ahead = halo(video.at[0], xw.at[pl.ds(0, 2)], 3, 3, beside)
    g_partner.start()
    x_partner.start()

    pixel, source = iota((256, 256), 0), iota((256, 256), 1)
    right = ((source == pixel + 1) & ((pixel & 15) != 15)).astype(BF16)
    left = ((source == pixel - 1) & ((pixel & 15) != 0)).astype(BF16)
    both = jnp.concatenate([right, left], axis=0)

    def widen(target, k, values, first, last):
        shifted = dot(both, values).astype(BF16)
        target[k, 1:17, :, 256 * first : 256 * first + 256] = shifted[:256].reshape(16, 16, 256)
        target[k, 1:17, :, 256:512] = values.reshape(16, 16, 256)
        target[k, 1:17, :, 256 * last : 256 * last + 256] = shifted[256:].reshape(16, 16, 256)
        target[k, 0:1] = jnp.zeros((1, 16, 768), BF16)
        target[k, 17:18] = jnp.zeros((1, 16, 768), BF16)

    def backward(lag):
        taken = jnp.concatenate(
            [
                gim[pl.ds(2 * core + lag, 2), 2 - i : 18 - i].reshape(512, 768)
                for i in range(3)
            ],
            axis=1,
        )
        weights = jnp.concatenate(
            [kv[lag, i, j] for i in range(3) for j in range(3)], axis=1
        )
        part = dot(taken, weights, (1, 1))
        for f in range(2):
            piece = part[256 * f : 256 * f + 256]
            if lag == 0:
                da[f] = piece
            else:
                keep = flag(own + f + lag < clip_end(starts, own + f, frames))
                da[f] = da[f] + keep * piece

    def widen_g(v, carry):
        widen(gim, v, gwin[v].reshape(256, 256), 0, 2)
        return carry

    load_g.wait()
    lax.fori_loop(0, 2, lambda v, carry: widen_g(2 * core + v, carry), 0)

    first_copy(stat, 0).wait_recv()
    loop(REACH + 1, lambda d: second_copy(stat, 0, d).start())

    @pl.when(core == 0)
    def _():
        g_back.start()

    load_k[0].wait()
    backward(0)
    g_partner.wait_recv()
    lax.fori_loop(0, 2, lambda v, carry: widen_g(2 - 2 * core + v, carry), 0)

    bounds, counted = [], jnp.zeros((8, 128), F32)
    for k in range(6):
        t = base - 2 + k
        b = clip_begin(starts, t)
        bounds.append((b, t + 1))
        count = jnp.maximum(t + 1 - b, 1).astype(F32)
        counted = jnp.where(iota((8, 128), 0) == k, count, counted)
    counted = jnp.maximum(counted, 1.0) * 2048.0
    row, channel = iota((128, 256), 0), iota((128, 256), 1)
    wanted = 64 * ((row >> 3) & 3) + 8 * (row & 7) + 2 * (row >> 5) + core
    select = (channel == wanted).astype(BF16)
    blank = jnp.zeros((128, 256), BF16)
    for lag, v in ((0, 4), (0, 5), (1, 0), (1, 5), (2, 0), (2, 1)):
        lhs[128 * lag : 128 * lag + 128, 256 * v : 256 * v + 256] = blank

    loop(REACH + 1, lambda d: second_copy(stat, 0, d).wait_recv())

    @pl.when(core == 1)
    def _():
        x_ahead.start()

    averaged = masked_rows(stat, bounds) / counted
    squares = pltpu.roll(averaged, 96, 1)
    inv_std = lax.rsqrt(squares - averaged * averaged + EPS)
    mean_rows[...] = spread(averaged)
    wide_inv = spread(inv_std)
    inv_rows[...] = wide_inv
    scale_rows[...] = wide_inv * gain[...]

    def activate(k, carry):
        values = xw[k].reshape(256, 256).astype(F32)
        normed = (values - mean_rows[pl.ds(k, 1)]) * scale_rows[pl.ds(k, 1)] + shift[...]
        act[k] = (normed * sigmoid(normed)).astype(BF16)
        return carry

    x_partner.wait_recv()
    lax.fori_loop(2, 6, activate, 0)

    for u in range(4):
        turned = dot(select, act[2 + u], (1, 1))
        end = clip_end(starts, base + u, frames)
        for lag in range(3):
            masked = turned if lag == 0 else turned * flag(base + u + lag < end)
            v = u + lag
            lhs[128 * lag : 128 * lag + 128, 256 * v : 256 * v + 256] = masked.astype(BF16)

    @pl.when(core == 1)
    def _():
        g_back.wait_recv()
        g_relay.start()

    @pl.when(core == 0)
    def _():
        g_relay.wait_recv()

    lax.fori_loop(4, 6, widen_g, 0)

    def one_x(i, d):
        low, count = PIECES[i]
        target = lax.rem(x + d, NX)
        return pltpu.make_async_remote_copy(
            src_ref=sx1.at[target, pl.ds(low, count)],
            dst_ref=rx1.at[d, pl.ds(low, count)],
            send_sem=one_send.at[0, i, d],
            recv_sem=one_recv.at[0, i, d],
            device_id=at(x_peer(d)),
            device_id_type=MESH,
        )

    def one_y(i, d):
        low, count = PIECES[i]
        target = lax.rem(y + d, ny)
        return pltpu.make_async_remote_copy(
            src_ref=sy1.at[target, pl.ds(low, count)],
            dst_ref=ry1.at[d, pl.ds(low, count)],
            send_sem=one_send.at[1, i, d],
            recv_sem=one_recv.at[1, i, d],
            device_id=at(tm, y_peer(d)),
            device_id_type=MESH,
        )

    def one_z(d):
        return pltpu.make_async_remote_copy(
            src_ref=sz1.at[lax.rem(z + d, nz)],
            dst_ref=rz1.at[d],
            send_sem=three_send.at[2, d],
            recv_sem=three_recv.at[2, d],
            device_id=at(z_peer(d)),
            device_id_type=MESH,
        )

    def put_total(buffer, first, rows):
        for h in range(2):
            buffer[h, first : first + rows.shape[0]] = rows[:, 128 * h : 128 * h + 128]

    def every(buffer, start, count, stride):
        rows = [buffer[h, pl.ds(start, count, stride=stride)] for h in range(2)]
        return jnp.concatenate(rows, axis=1)

    for i in range(3):
        terms = dot(lhs[...], gim[:, 2 - i : 18 - i].reshape(1536, 768))
        for lag in range(3):
            for j in range(3):
                axis, slot = place_of(9 * i + 3 * lag + j)
                block = terms[128 * lag : 128 * lag + 128, 256 * j : 256 * j + 256]
                if axis == "z":
                    put_total(turn, 128 * slot, block)
                    for q in range(nz):
                        sz1[q, slot] = every(turn, 128 * slot + q, 16, 8).astype(BF16)
                    continue
                for p in range(4):
                    if axis == "x":
                        sx1[p, slot] = block[32 * p : 32 * p + 32].astype(BF16)
                    else:
                        rows = [block[32 * q + 8 * p : 32 * q + 8 * p + 8] for q in range(4)]
                        sy1[p, slot] = jnp.concatenate(rows, axis=0).astype(BF16)
        if i == 0:
            loop(nz, lambda d: one_z(d).start())
        for d in (2, 1, 3):
            one_x(i, d).start()
            one_y(i, d).start()

    for lag in (1, 2):
        load_k[lag].wait()
        backward(lag)

    lanes = iota((1, 128), 1)
    sums = []
    for f in range(2):
        k = 2 + 2 * core + f
        centred = xw[k].reshape(256, 256).astype(F32) - mean_rows[pl.ds(k, 1)]
        normed = centred * scale_rows[pl.ds(k, 1)] + shift[...]
        sig = sigmoid(normed)
        du = da[f] * (sig * (1.0 + normed * (1.0 - sig))) * gain[...]
        da[f] = du
        sums.append(jnp.sum(du, axis=0, keepdims=True))
        sums.append(jnp.sum(du * centred, axis=0, keepdims=True))
    packed = pack_rows(sums)
    row_of = iota((8, 128), 0)

    def pick(rows, k):
        return jnp.sum(jnp.where(row_of == k, rows, 0.0), axis=0, keepdims=True)

    answer = jnp.zeros((1, 128), F32)
    for f in range(2):
        k = 2 + 2 * core + f
        mean_k, inv_k, n_k = pick(averaged, k), pick(inv_std, k), pick(counted, k)
        sum_du = pltpu.roll(packed, 64, 1) if f else packed
        dr = pltpu.roll(sum_du, 96, 1)
        cubed = inv_k * inv_k * inv_k
        dc1 = (dr * cubed * mean_k - inv_k * sum_du) / n_k
        dc2 = -0.5 * dr * cubed / n_k
        dc2 = pltpu.roll(dc2, 32, 1)
        pair = jnp.where(lanes < 32, dc1, jnp.where(lanes < 64, dc2, 0.0))
        answer = answer + (pltpu.roll(pair, 64, 1) if f else pair)
    dstat[pl.ds(tm, 1)] = answer.reshape(1, 1, 128)
    first_copy(dstat, 1).start()

    @pl.when(core == 0)
    def _():
        x_ahead.wait_recv()
        lax.fori_loop(0, 2, activate, 0)

    def widen_a(k, carry):
        widen(aim, k, act[2 * core + k], 2, 0)
        return carry

    lax.fori_loop(0, 4, widen_a, 0)
    first_copy(dstat, 1).wait_recv()
    loop(REACH + 1, lambda d: second_copy(dstat, 1, d).start())
    for lag in range(3):
        taken = jnp.concatenate(
            [aim[2 - lag : 4 - lag, i : i + 16].reshape(512, 768) for i in range(3)], axis=1
        )
        part = dot(taken, kv[lag].reshape(2304, 256))
        for f in range(2):
            piece = part[256 * f : 256 * f + 256]
            if lag == 0:
                total = xw[2 + 2 * core + f].reshape(256, 256).astype(F32) + piece
            else:
                keep = flag(own + f - lag >= clip_begin(starts, own + f))
                total = total_f[f] + keep * piece
            if f == 0:
                first = total
            else:
                total_f = [first, total]
    for f in range(2):
        out_v[f] = total_f[f].reshape(16, 16, 256).astype(BF16)
    store_out = pltpu.make_async_copy(out_v, out.at[0], store_sem.at[0])
    store_out.start()

    def two(c, kind, d):
        mine, got = ((sx2, rx2), (sy2, ry2), (sz2, rz2), (sz3, rz3))[kind]
        along_y = kind in (0, 2)
        target = lax.rem(y + d, ny) if along_y else lax.rem(x + d, NX)
        src, dst = mine.at[target], got.at[d]
        if kind < 2:
            src, dst = src.at[pl.ds(48 * c, 48)], dst.at[pl.ds(48 * c, 48)]
        return pltpu.make_async_remote_copy(
            src_ref=src,
            dst_ref=dst,
            send_sem=two_send.at[kind, c, d],
            recv_sem=two_recv.at[kind, c, d],
            device_id=at(tm, y_peer(d)) if along_y else at(x_peer(d)),
            device_id_type=MESH,
        )

    def three(c, d):
        return pltpu.make_async_remote_copy(
            src_ref=s3.at[lax.rem(z + d, nz), pl.ds(16 * c, 16)],
            dst_ref=r3.at[d, pl.ds(16 * c, 16)],
            send_sem=three_send.at[c, d],
            recv_sem=three_recv.at[c, d],
            device_id=at(z_peer(d)),
            device_id_type=MESH,
        )

    total3[...] = jnp.zeros(total3.shape, F32)

    def gathered(c, mine, got, keep, staged, me):
        low, count = HALVES[c]
        first = 48 * c
        for p in range(4):
            some = pl.ds(16 * (p // 2), 16)
            half = mine[me, pl.ds(low, count), some].astype(F32)
            for d in range(1, 4):
                half = half + got[d, pl.ds(low, count), some].astype(F32)
            piece = half[:, 8 * (p % 2) : 8 * (p % 2) + 8].reshape(8 * count, 256)
            if 8 * count < 48:
                piece = jnp.concatenate([piece, jnp.zeros((48 - 8 * count, 256), F32)], axis=0)
            keep[p, first : first + 48] = piece
            staged[p, first : first + 48] = piece.astype(BF16)

    def to_two(c):
        pieces = (0, 1) if c == 0 else (2,)
        for kind, one, mine, got, keep, staged, me in (
            (0, one_x, sx1, rx1, kx2, sx2, x),
            (1, one_y, sy1, ry1, ky2, sy2, y),
        ):
            for i in pieces:
                for d in range(1, 4):
                    one(i, d).wait_recv()
            gathered(c, mine, got, keep, staged, me)
            for d in (2, 1, 3):
                two(c, kind, d).start()

    def to_three(c):
        some = pl.ds(48 * c, 48)
        for kind, keep, got, me in ((0, kx2, rx2, y), (1, ky2, ry2, x)):
            for d in range(1, 4):
                two(c, kind, d).wait_recv()
            total = keep[me, some]
            for d in range(1, 4):
                total = total + got[d, some].astype(F32)
            put_total(total3, 128 * c + 48 * kind, total)
        for q in range(nz):
            s3[q, 16 * c : 16 * c + 16] = every(total3, 128 * c + q, 16, 8).astype(BF16)
        loop(nz, lambda d: three(c, d).start())

    def finish(rows, taps):
        for n in range(TAPS):
            if place_of(n) in taps:
                k = taps.index(place_of(n))
                to = 9 * (n % 9 // 3) + 3 * (n // 9) + n % 3
                wgrads[to] = rows[k : k + 1] * scale

    to_two(0)
    to_two(1)

    loop(nz, lambda d: one_z(d).wait_recv())
    total = sz1[z].astype(F32)
    for d in range(1, nz):
        total = total + rz1[d].astype(F32)
    put_total(turn, 0, total.reshape(16 * Z_TAPS, 256))
    for p in range(4):
        sz2[p] = every(turn, p, 32, 4).astype(BF16)
    for d in (2, 1, 3):
        two(0, 2, d).start()

    to_three(0)
    to_three(1)

    for d in (1, 2, 3):
        two(0, 2, d).wait_recv()
    total = every(turn, y, 32, 4)
    for d in range(1, 4):
        total = total + rz2[d].astype(F32)
    put_total(turn, 128, total)
    for p in range(4):
        sz3[p] = every(turn, 128 + p, 16, 4).astype(BF16)
    for d in (2, 1, 3):
        two(0, 3, d).start()

    loop(REACH + 1, lambda d: second_copy(dstat, 1, d).wait_recv())
    bounds = [(own + f, clip_end(starts, own + f, frames)) for f in range(2)]
    backs = masked_rows(dstat, bounds)
    back_one = spread(backs)
    back_two = spread(pltpu.roll(backs, 96, 1))
    for f in range(2):
        k = 2 + 2 * core + f
        values = xw[k].reshape(256, 256).astype(F32)
        result = (
            gwin[2 * core + f].reshape(256, 256).astype(F32)
            + da[f] * inv_rows[pl.ds(k, 1)]
            + back_one[f : f + 1]
            + values * (2.0 * back_two[f : f + 1])
        )
        grads_v[f] = result.reshape(16, 16, 256).astype(BF16)
    store_grads = pltpu.make_async_copy(grads_v, grads.at[0], store_sem.at[1])
    store_grads.start()

    for c in range(2):
        loop(nz, lambda d: three(c, d).wait_recv())
        total = every(total3, 128 * c + z, 16, 8)
        for d in range(1, nz):
            total = total + r3[d, pl.ds(16 * c, 16)].astype(F32)
        low, count = HALVES[c]
        finish(total, [(axis, low + k) for axis in "xy" for k in range(6)])
    for d in (1, 2, 3):
        two(0, 3, d).wait_recv()
    total = every(turn, 128 + x, 16, 4)
    for d in range(1, 4):
        total = total + rz3[d].astype(F32)
    finish(total, [("z", k) for k in range(Z_TAPS)])

    first_copy(stat, 0).wait_send()
    loop(REACH + 1, lambda d: second_copy(stat, 0, d).wait_send())
    first_copy(dstat, 1).wait_send()
    loop(REACH + 1, lambda d: second_copy(dstat, 1, d).wait_send())
    g_partner.wait_send()
    x_partner.wait_send()

    x_or_g = ((g_back, 0), (g_relay, 1), (x_ahead, 1))
    for copy, sender in x_or_g:
        pl.when(core == sender)(copy.wait_send)
    for d in range(1, 4):
        for i in range(3):
            one_x(i, d).wait_send()
            one_y(i, d).wait_send()
        for c, kind in ((0, 0), (0, 1), (1, 0), (1, 1), (0, 2), (0, 3)):
            two(c, kind, d).wait_send()
    loop(nz, lambda d: one_z(d).wait_send())
    for c in range(2):
        loop(nz, lambda d: three(c, d).wait_send())
    store_out.wait()
    store_grads.wait()


def hand_over(*refs):
    sources, targets, held, sems = refs[:3], refs[3:6], refs[6:9], refs[9]
    into = [pltpu.make_async_copy(sources[k], held[k], sems.at[0, k]) for k in range(3)]
    out = [pltpu.make_async_copy(held[k], targets[k], sems.at[1, k]) for k in range(3)]
    for copy in into:
        copy.start()
    for k in range(3):
        into[k].wait()
        out[k].start()
    for copy in out:
        copy.wait()


def local(nz, ny, scale, video_tile, clip_lengths, kernels, norm_gains, norm_shifts, cotangent):
    hbm = pl.BlockSpec(memory_space=pltpu.HBM)
    vmem = pl.BlockSpec(memory_space=pltpu.VMEM)
    dma = pltpu.SemaphoreType.DMA
    made = pl.pallas_call(
        functools.partial(kernel, nz, ny, scale),
        out_shape=(
            jax.ShapeDtypeStruct(video_tile.shape, BF16),
            jax.ShapeDtypeStruct(video_tile.shape, BF16),
            jax.ShapeDtypeStruct((TAPS, 1, 256), F32),
        ),
        in_specs=[hbm] * 6,
        out_specs=(hbm, hbm, vmem),
        scratch_shapes=[
            pltpu.SMEM((1, 6), jnp.int32),
            pltpu.VMEM((1, 256), F32),
            pltpu.VMEM((1, 256), F32),
            pltpu.VMEM((6, 16, 16, 256), BF16),
            pltpu.VMEM((6, 16, 16, 256), BF16),
            pltpu.VMEM((3, 3, 3, 256, 256), BF16),
            pltpu.VMEM((6, 18, 16, 768), BF16),
            pltpu.VMEM((4, 18, 16, 768), BF16),
            pltpu.VMEM((6, 256, 256), BF16),
            pltpu.VMEM((384, 1536), BF16),
            pltpu.VMEM((nz * GROUP, 1, 128), F32),
            pltpu.VMEM((nz * GROUP, 1, 128), F32),
            pltpu.VMEM((8, 256), F32),
            pltpu.VMEM((8, 256), F32),
            pltpu.VMEM((8, 256), F32),
            pltpu.VMEM((2, 256, 256), F32),
            pltpu.VMEM((4, 11, 32, 256), BF16),
            pltpu.VMEM((4, 11, 32, 256), BF16),
            pltpu.VMEM((4, 11, 32, 256), BF16),
            pltpu.VMEM((4, 11, 32, 256), BF16),
            pltpu.VMEM((8, Z_TAPS, 16, 256), BF16),
            pltpu.VMEM((8, Z_TAPS, 16, 256), BF16),
            pltpu.VMEM((4, 96, 256), BF16),
            pltpu.VMEM((4, 96, 256), BF16),
            pltpu.VMEM((4, 96, 256), BF16),
            pltpu.VMEM((4, 96, 256), BF16),
            pltpu.VMEM((4, 32, 256), BF16),
            pltpu.VMEM((4, 32, 256), BF16),
            pltpu.VMEM((4, 16, 256), BF16),
            pltpu.VMEM((4, 16, 256), BF16),
            pltpu.VMEM((4, 96, 256), F32),
            pltpu.VMEM((4, 96, 256), F32),
            pltpu.VMEM((2, 128 * Z_TAPS, 128), F32),
            pltpu.VMEM((2, 256, 128), F32),
            pltpu.VMEM((8, 32, 256), BF16),
            pltpu.VMEM((8, 32, 256), BF16),
            pltpu.VMEM((2, 16, 16, 256), BF16),
            pltpu.VMEM((2, 16, 16, 256), BF16),
            dma((8,)),
            dma((4,)),
            dma((4,)),
            dma((2, REACH + 1)),
            dma((2, REACH + 1)),
            dma((2, 3, 4)),
            dma((2, 3, 4)),
            dma((4, 2, 4)),
            dma((4, 2, 4)),
            dma((3, 8)),
            dma((3, 8)),
            dma((2,)),
        ],
        compiler_params=pltpu.CompilerParams(
            collective_id=0, has_side_effects=True, vmem_limit_bytes=60 * 1024 * 1024
        ),
        cost_estimate=pl.CostEstimate(flops=5_500_000_000, bytes_accessed=5_000_000, transcendentals=400_000),
    )(clip_lengths, norm_gains, norm_shifts, video_tile, cotangent, kernels)
    results = pl.pallas_call(
        hand_over,
        out_shape=tuple(jax.ShapeDtypeStruct(part.shape, part.dtype) for part in made),
        in_specs=[hbm] * 3,
        out_specs=(hbm,) * 3,
        scratch_shapes=[pltpu.VMEM(part.shape, part.dtype) for part in made] + [dma((2, 3))],
        compiler_params=pltpu.CompilerParams(vmem_limit_bytes=60 * 1024 * 1024),
    )(*made)
    return (results[0], results[1], results[2].transpose(1, 0, 2))


def solution(mesh):
    ny, tm = mesh.shape["dp"], mesh.shape["tm"]
    nz = tm // GROUP
    scale = 1.0 / math.sqrt(ny * tm * 2 * 256)
    placed = P("dp", "tm", None, None, None)
    return jax.shard_map(
        functools.partial(local, nz, ny, scale),
        mesh=mesh,
        in_specs=(placed, P("dp", None), P(), P(), P(), placed),
        out_specs=(placed, placed, P(None, None, ("dp", "tm"))),
        check_vma=False,
    )
```

```python
import functools
import math

import jax
import jax.numpy as jnp
from jax import lax
from jax.experimental import pallas as pl
from jax.experimental.pallas import tpu as pltpu
from jax.sharding import PartitionSpec as P

EPS = 1e-05
NX = 4
NC = 2
GROUP = NX * NC
TAPS = 27
REACH = 12
MESH = pl.DeviceIdType.MESH
F32 = jnp.float32
BF16 = jnp.bfloat16
Z_TAPS = 5
Z_PIECES = {1: (0, 2), 4: (2, 3)}
PIECES = {0: (0, 1), 2: (1, 2), 4: (3, 2), 6: (5, 3), 8: (8, 3)}
HALVES = ((0, 8, 0, 64), (8, 3, 64, 32))


def place_of(n):
    step, lag = n // 3, n % 3
    if step < Z_TAPS:
        return ("xyz"[lag], step)
    k = n - Z_TAPS
    return "xy"[k % 2], k // 2


def iota(shape, dim):
    return lax.broadcasted_iota(jnp.int32, shape, dim)


def clip_begin(starts, t):
    begin = jnp.int32(0)
    for start in starts:
        begin = jnp.where(start <= t, start, begin)
    return begin


def clip_end(starts, t, frames):
    end = jnp.int32(frames)
    for start in reversed(starts):
        end = jnp.where(start > t, start, end)
    return end


def flag(condition):
    return jnp.where(condition, jnp.float32(1.0), jnp.float32(0.0))


def dot(a, b, contract=(1, 0), precision=None):
    return lax.dot_general(
        a,
        b,
        (((contract[0],), (contract[1],)), ((), ())),
        preferred_element_type=F32,
        precision=precision,
    )


def sigmoid(z):
    return 0.5 * jnp.tanh(0.5 * z) + 0.5


def pack_rows(rows):
    place = iota((8, 256), 0)
    stacked = jnp.zeros((8, 256), F32)
    for k, row in enumerate(rows):
        stacked = jnp.where(place == k, row, stacked)
    gather = ((iota((256, 128), 0) >> 3) == (iota((256, 128), 1) & 31)).astype(F32)
    grouped = dot(stacked, gather, precision=lax.Precision.HIGHEST)
    mine = (iota((8, 128), 1) >> 5) == iota((8, 128), 0)
    return jnp.sum(jnp.where(mine, grouped, 0.0), axis=0, keepdims=True)


def spread(*parts):
    rows = jnp.concatenate(parts, axis=0)
    clean = jnp.where(iota(rows.shape, 1) < 32, rows, 0.0)
    matrix = (iota((128, 256), 0) == (iota((128, 256), 1) >> 3)).astype(F32)
    wide = dot(clean, matrix, precision=lax.Precision.HIGHEST)
    return [wide[8 * k : 8 * k + 8] for k in range(len(parts))]


def masked_rows(buffer, bounds):
    values = buffer[...]
    frame = 2 * iota(values.shape, 0) + (iota(values.shape, 2) >> 6)
    place = iota((8, 128), 0)
    rows = jnp.zeros((8, 128), F32)
    for k, (low, high) in enumerate(bounds):
        inside = (frame >= low) & (frame < high)
        total = jnp.sum(jnp.where(inside, values, 0.0), axis=0)
        rows = jnp.where(place == k, total, rows)
    return rows + pltpu.roll(rows, 64, 1)


def kernel(
    nz,
    ny,
    lens_hbm,
    gain_hbm,
    shift_hbm,
    video,
    cot,
    kern,
    out,
    grads,
    own3,
    r3,
    rz3,
    lens,
    gain,
    shift,
    xw,
    gwin,
    kv,
    gim,
    aim,
    act,
    lhs,
    stat,
    dstat,
    mean_rows,
    scale_rows,
    inv_rows,
    da,
    sx1,
    rx1,
    sy1,
    ry1,
    sz1,
    rz1,
    sx2,
    rx2,
    sy2,
    ry2,
    sz2,
    rz2,
    sz3,
    kx2,
    ky2,
    turn,
    total3,
    s3,
    own_v,
    out_v,
    grads_v,
    load_sem,
    halo_send,
    halo_recv,
    chain_send,
    chain_recv,
    one_send,
    one_recv,
    two_send,
    two_recv,
    three_send,
    three_recv,
    store_sem,
):
    y = lax.axis_index("dp")
    tm = lax.axis_index("tm")
    core = lax.rem(tm, NC)
    x = lax.rem(tm // NC, NX)
    z = tm // GROUP
    within = lax.rem(tm, GROUP)
    chip = tm // NC
    chips = nz * NX
    frames = 2 * nz * GROUP
    base = 4 * chip
    own = 2 * tm

    def at(tm_index, dp_index=None):
        return {"dp": y if dp_index is None else dp_index, "tm": tm_index}

    def x_peer(d):
        return z * GROUP + lax.rem(x + d, NX) * NC + core

    def z_peer(d):
        return lax.rem(z + d, nz) * GROUP + within

    def y_peer(d):
        return lax.rem(y + d, ny)

    def chip_peer(d):
        return lax.rem(chip + d, chips) * NC + core

    partner = chip * NC + 1 - core

    beside = lax.rem(tm + 2 * core - 1 + 2 * chips, 2 * chips)

    stat[...] = jnp.zeros(stat.shape, F32)
    dstat[...] = jnp.zeros(dstat.shape, F32)

    load_x = pltpu.make_async_copy(video.at[0], xw.at[pl.ds(2 + 2 * core, 2)], load_sem.at[0])
    load_g = pltpu.make_async_copy(cot.at[0], gwin.at[pl.ds(2 * core, 2)], load_sem.at[1])
    load_k = [
        pltpu.make_async_copy(kern.at[0, lag], kv.at[lag], load_sem.at[2 + lag]) for lag in range(3)
    ]
    load_small = [
        pltpu.make_async_copy(src, dst, load_sem.at[5 + k])
        for k, (src, dst) in enumerate(((lens_hbm, lens), (gain_hbm, gain), (shift_hbm, shift)))
    ]
    load_x.start()
    load_g.start()
    for copy in load_small:
        copy.start()

    barrier = pltpu.get_barrier_semaphore()

    def greet(device):
        pl.semaphore_signal(barrier, inc=1, device_id=device, device_id_type=MESH)

    def greet_chips(d, carry):
        greet(at(chip_peer(d)))
        greet(at(chip_peer(chips - d)))
        return carry

    far = range(REACH // NX + 1, nz - REACH // NX)
    for d in far:
        greet(at(z_peer(d)))
    for d in range(1, ny):
        greet(at(tm, y_peer(d)))
    lax.fori_loop(0, REACH, lambda d, carry: greet_chips(REACH - d, carry), 0)
    greet(at(partner))
    greet(at(beside))
    for copy in load_k:
        copy.start()

    for copy in load_small:
        copy.wait()
    starts = []
    begin = jnp.int32(0)
    for k in range(6):
        starts.append(begin)
        begin = begin + lens[0, k]

    load_x.wait()
    sums = []
    for f in range(2):
        values = xw[2 + 2 * core + f].reshape(256, 256).astype(F32)
        sums.append(jnp.sum(values, axis=0, keepdims=True))
        sums.append(jnp.sum(values * values, axis=0, keepdims=True))
    stat[pl.ds(tm, 1)] = pack_rows(sums).reshape(1, 1, 128)

    pl.semaphore_wait(barrier, 2 * REACH + len(far) + (ny - 1) + 2)

    def first_copy(buffer, kind):
        mine = buffer.at[pl.ds(tm, 1)]
        return pltpu.make_async_remote_copy(
            src_ref=mine,
            dst_ref=mine,
            send_sem=chain_send.at[kind, 0],
            recv_sem=chain_recv.at[kind, 0],
            device_id=at(partner),
            device_id_type=MESH,
        )

    def second_copy(buffer, kind, d):
        mine = buffer.at[pl.ds(NC * chip, NC)]
        step = d if kind == 0 else chips - d
        return pltpu.make_async_remote_copy(
            src_ref=mine,
            dst_ref=mine,
            send_sem=chain_send.at[kind, d],
            recv_sem=chain_recv.at[kind, d],
            device_id=at(chip_peer(step)),
            device_id_type=MESH,
        )

    def loop(count, act_on):
        def body(d, carry):
            act_on(d)
            return carry

        lax.fori_loop(1, count, body, 0)

    first_copy(stat, 0).start()

    def halo(src, dst, sent, received, device):
        return pltpu.make_async_remote_copy(
            src_ref=src,
            dst_ref=dst,
            send_sem=halo_send.at[sent],
            recv_sem=halo_recv.at[received],
            device_id=at(device),
            device_id_type=MESH,
        )

    own_g = gwin.at[pl.ds(2 * core, 2)]
    own_x = xw.at[pl.ds(2 + 2 * core, 2)]
    g_partner = halo(cot.at[0], own_g, 0, 0, partner)
    x_partner = halo(video.at[0], own_x, 1, 1, partner)
    g_back = [halo(cot.at[0, f], gwin.at[4 + f], 2 + f, 2 + f, beside) for f in range(2)]
    g_relay = [halo(gwin.at[4 + f], gwin.at[4 + f], 2 + f, 2 + f, partner) for f in range(2)]
    x_ahead = halo(video.at[0], xw.at[pl.ds(0, 2)], 4, 4, beside)
    g_partner.start()
    x_partner.start()

    pixel, source = iota((256, 256), 0), iota((256, 256), 1)
    right = ((source == pixel + 1) & ((pixel & 15) != 15)).astype(BF16)
    left = ((source == pixel - 1) & ((pixel & 15) != 0)).astype(BF16)
    both = jnp.concatenate([right, left], axis=0)

    def widen(target, k, values, first, last):
        shifted = dot(both, values).astype(BF16)
        target[k, 1:17, :, 256 * first : 256 * first + 256] = shifted[:256].reshape(16, 16, 256)
        target[k, 1:17, :, 256:512] = values.reshape(16, 16, 256)
        target[k, 1:17, :, 256 * last : 256 * last + 256] = shifted[256:].reshape(16, 16, 256)
        target[k, 0:1] = jnp.zeros((1, 16, 768), BF16)
        target[k, 17:18] = jnp.zeros((1, 16, 768), BF16)

    def backward(lag):
        taken = jnp.concatenate(
            [
                gim[pl.ds(2 * core + lag, 2), 2 - i : 18 - i].reshape(512, 768)
                for i in range(3)
            ],
            axis=1,
        )
        weights = jnp.concatenate(
            [kv[lag, i, j] for i in range(3) for j in range(3)], axis=1
        )
        part = dot(taken, weights, (1, 1))
        for f in range(2):
            piece = part[256 * f : 256 * f + 256]
            if lag == 0:
                da[f] = piece
            else:
                keep = flag(own + f + lag < clip_end(starts, own + f, frames))
                da[f] = da[f] + keep * piece

    def widen_g(v, carry):
        widen(gim, v, gwin[v].reshape(256, 256), 0, 2)
        return carry

    load_g.wait()
    lax.fori_loop(0, 2, lambda v, carry: widen_g(2 * core + v, carry), 0)

    first_copy(stat, 0).wait_recv()
    loop(REACH + 1, lambda d: second_copy(stat, 0, REACH + 1 - d).start())

    @pl.when(core == 0)
    def _():
        g_back[0].start()
        g_back[1].start()

    load_k[0].wait()
    backward(0)
    g_partner.wait_recv()
    lax.fori_loop(0, 2, lambda v, carry: widen_g(2 - 2 * core + v, carry), 0)

    bounds, counted = [], jnp.zeros((8, 128), F32)
    for k in range(6):
        t = base - 2 + k
        b = clip_begin(starts, t)
        bounds.append((b, t + 1))
        count = jnp.maximum(t + 1 - b, 1).astype(F32)
        counted = jnp.where(iota((8, 128), 0) == k, count, counted)
    counted = jnp.maximum(counted, 1.0) * 2048.0
    row, channel = iota((128, 256), 0), iota((128, 256), 1)
    wanted = 64 * ((row >> 3) & 3) + 8 * (row & 7) + 2 * (row >> 5) + core
    select = (channel == wanted).astype(BF16)
    blank = jnp.zeros((128, 256), BF16)
    for lag, v in ((0, 4), (0, 5), (1, 0), (1, 5), (2, 0), (2, 1)):
        lhs[128 * lag : 128 * lag + 128, 256 * v : 256 * v + 256] = blank

    loop(REACH + 1, lambda d: second_copy(stat, 0, d).wait_recv())

    @pl.when(core == 1)
    def _():
        x_ahead.start()

    averaged = masked_rows(stat, bounds) / counted
    squares = pltpu.roll(averaged, 96, 1)
    inv_std = lax.rsqrt(squares - averaged * averaged + EPS)
    wide_mean, wide_inv = spread(averaged, inv_std)
    mean_rows[...] = wide_mean
    inv_rows[...] = wide_inv
    scale_rows[...] = wide_inv * gain[...]

    def activate(k, carry):
        values = xw[k].reshape(256, 256).astype(F32)
        normed = (values - mean_rows[pl.ds(k, 1)]) * scale_rows[pl.ds(k, 1)] + shift[...]
        act[k] = (normed * sigmoid(normed)).astype(BF16)
        return carry

    x_partner.wait_recv()

    for u in range(4):
        activate(2 + u, 0)
        turned = dot(select, act[2 + u], (1, 1))
        end = clip_end(starts, base + u, frames)
        for lag in range(3):
            masked = turned if lag == 0 else turned * flag(base + u + lag < end)
            v = u + lag
            lhs[128 * lag : 128 * lag + 128, 256 * v : 256 * v + 256] = masked.astype(BF16)

    for f in range(2):

        @pl.when(core == 1)
        def _():
            g_back[f].wait_recv()
            g_relay[f].start()

        @pl.when(core == 0)
        def _():
            g_relay[f].wait_recv()

        widen_g(4 + f, 0)

    def one_x(i, d):
        low, count = PIECES[i]
        target = lax.rem(x + d, NX)
        return pltpu.make_async_remote_copy(
            src_ref=sx1.at[target, pl.ds(low, count)],
            dst_ref=rx1.at[d, pl.ds(low, count)],
            send_sem=one_send.at[0, i // 2, d],
            recv_sem=one_recv.at[0, i // 2, d],
            device_id=at(x_peer(d)),
            device_id_type=MESH,
        )

    def one_y(i, d):
        low, count = PIECES[i]
        target = lax.rem(y + d, ny)
        return pltpu.make_async_remote_copy(
            src_ref=sy1.at[target, pl.ds(low, count)],
            dst_ref=ry1.at[d, pl.ds(low, count)],
            send_sem=one_send.at[1, i // 2, d],
            recv_sem=one_recv.at[1, i // 2, d],
            device_id=at(tm, y_peer(d)),
            device_id_type=MESH,
        )

    def one_z(i, d):
        low, count = Z_PIECES[i]
        return pltpu.make_async_remote_copy(
            src_ref=sz1.at[lax.rem(z + d, nz), pl.ds(low, count)],
            dst_ref=rz1.at[d, pl.ds(low, count)],
            send_sem=three_send.at[2 + i // 4, d],
            recv_sem=three_recv.at[2 + i // 4, d],
            device_id=at(z_peer(d)),
            device_id_type=MESH,
        )

    def put_total(buffer, first, rows):
        for h in range(2):
            buffer[h, first : first + rows.shape[0]] = rows[:, 128 * h : 128 * h + 128]

    def every(buffer, start, count, stride):
        rows = [buffer[h, pl.ds(start, count, stride=stride)] for h in range(2)]
        return jnp.concatenate(rows, axis=1)

    for step in range(9):
        i, j = step // 3, step % 3
        terms = dot(lhs[...], gim[:, 2 - i : 18 - i, :, 256 * j : 256 * j + 256].reshape(1536, 256))
        for lag in range(3):
            axis, slot = place_of(3 * step + lag)
            block = terms[128 * lag : 128 * lag + 128]
            if axis == "z":
                put_total(turn, 128 * slot, block)
                for q in range(nz):
                    sz1[q, slot] = every(turn, 128 * slot + q, 16, 8).astype(BF16)
                continue
            for p in range(4):
                if axis == "x":
                    sx1[p, slot] = block[32 * p : 32 * p + 32].astype(BF16)
                else:
                    rows = [block[32 * q + 8 * p : 32 * q + 8 * p + 8] for q in range(4)]
                    sy1[p, slot] = jnp.concatenate(rows, axis=0).astype(BF16)
        if step in PIECES:
            for d in (2, 1, 3):
                one_x(step, d).start()
                one_y(step, d).start()
        if step in Z_PIECES:
            loop(nz, lambda d: one_z(step, d).start())

    for lag in (1, 2):
        load_k[lag].wait()
        backward(lag)

    lanes = iota((1, 128), 1)
    sums = []
    for f in range(2):
        k = 2 + 2 * core + f
        centred = xw[k].reshape(256, 256).astype(F32) - mean_rows[pl.ds(k, 1)]
        normed = centred * scale_rows[pl.ds(k, 1)] + shift[...]
        sig = sigmoid(normed)
        du = da[f] * (sig * (1.0 + normed * (1.0 - sig))) * gain[...]
        da[f] = du
        sums.append(jnp.sum(du, axis=0, keepdims=True))
        sums.append(jnp.sum(du * centred, axis=0, keepdims=True))
    packed = pack_rows(sums)
    row_of = iota((8, 128), 0)

    def pick(rows, k):
        return jnp.sum(jnp.where(row_of == k, rows, 0.0), axis=0, keepdims=True)

    answer = jnp.zeros((1, 128), F32)
    for f in range(2):
        k = 2 + 2 * core + f
        mean_k, inv_k, n_k = pick(averaged, k), pick(inv_std, k), pick(counted, k)
        sum_du = pltpu.roll(packed, 64, 1) if f else packed
        dr = pltpu.roll(sum_du, 96, 1)
        cubed = inv_k * inv_k * inv_k
        dc1 = (dr * cubed * mean_k - inv_k * sum_du) / n_k
        dc2 = -0.5 * dr * cubed / n_k
        dc2 = pltpu.roll(dc2, 32, 1)
        pair = jnp.where(lanes < 32, dc1, jnp.where(lanes < 64, dc2, 0.0))
        answer = answer + (pltpu.roll(pair, 64, 1) if f else pair)
    dstat[pl.ds(tm, 1)] = answer.reshape(1, 1, 128)
    first_copy(dstat, 1).start()

    @pl.when(core == 0)
    def _():
        x_ahead.wait_recv()
        lax.fori_loop(0, 2, activate, 0)

    def widen_a(k, carry):
        widen(aim, k, act[2 * core + k], 2, 0)
        return carry

    lax.fori_loop(0, 4, widen_a, 0)
    for lag in range(3):
        taken = jnp.concatenate(
            [aim[2 - lag : 4 - lag, i : i + 16].reshape(512, 768) for i in range(3)], axis=1
        )
        part = dot(taken, kv[lag].reshape(2304, 256))
        for f in range(2):
            piece = part[256 * f : 256 * f + 256]
            if lag == 0:
                total = xw[2 + 2 * core + f].reshape(256, 256).astype(F32) + piece
            else:
                keep = flag(own + f - lag >= clip_begin(starts, own + f))
                total = total_f[f] + keep * piece
            if f == 0:
                first = total
            else:
                total_f = [first, total]
    for f in range(2):
        out_v[f] = total_f[f].reshape(16, 16, 256).astype(BF16)
    store_out = pltpu.make_async_copy(out_v, out.at[0], store_sem.at[0])
    store_out.start()

    def two(c, kind, d):
        mine, got = ((sx2, rx2), (sy2, ry2), (sz2, rz2), (sz3, rz3))[kind]
        along_y = kind in (0, 2)
        target = lax.rem(y + d, ny) if along_y else lax.rem(x + d, NX)
        src, dst = mine.at[target], got.at[d]
        if kind < 2:
            some = pl.ds(HALVES[c][2], HALVES[c][3])
            src, dst = src.at[some], dst.at[some]
        return pltpu.make_async_remote_copy(
            src_ref=src,
            dst_ref=dst,
            send_sem=two_send.at[kind, c, d],
            recv_sem=two_recv.at[kind, c, d],
            device_id=at(tm, y_peer(d)) if along_y else at(x_peer(d)),
            device_id_type=MESH,
        )

    def three(c, d):
        return pltpu.make_async_remote_copy(
            src_ref=s3.at[lax.rem(z + d, nz), pl.ds(16 * c, 16)],
            dst_ref=r3.at[d, pl.ds(16 * c, 16)],
            send_sem=three_send.at[c, d],
            recv_sem=three_recv.at[c, d],
            device_id=at(z_peer(d)),
            device_id_type=MESH,
        )

    total3[...] = jnp.zeros(total3.shape, F32)

    def gathered(c, mine, got, keep, staged, me):
        low, count, first, length = HALVES[c]
        for both_p in range(2):
            some = pl.ds(16 * both_p, 16)
            half = mine[me, pl.ds(low, count), some].astype(F32)
            for d in range(1, 4):
                half = half + got[d, pl.ds(low, count), some].astype(F32)
            for p in (2 * both_p, 2 * both_p + 1):
                piece = half[:, 8 * (p % 2) : 8 * (p % 2) + 8].reshape(8 * count, 256)
                if 8 * count < length:
                    blank = jnp.zeros((length - 8 * count, 256), F32)
                    piece = jnp.concatenate([piece, blank], axis=0)
                keep[p, first : first + length] = piece
                staged[p, first : first + length] = piece.astype(BF16)

    def to_two(c):
        pieces = (0, 2, 4, 6) if c == 0 else (8,)
        for kind, one, mine, got, keep, staged, me in (
            (0, one_x, sx1, rx1, kx2, sx2, x),
            (1, one_y, sy1, ry1, ky2, sy2, y),
        ):
            for i in pieces:
                for d in range(1, 4):
                    one(i, d).wait_recv()
            gathered(c, mine, got, keep, staged, me)
            for d in (2, 1, 3):
                two(c, kind, d).start()

    def to_three(c):
        low, count, first, length = HALVES[c]
        some = pl.ds(first, length)
        for kind, keep, got, me in ((0, kx2, rx2, y), (1, ky2, ry2, x)):
            for d in range(1, 4):
                two(c, kind, d).wait_recv()
            total = keep[me, some]
            for d in range(1, 4):
                total = total + got[d, some].astype(F32)
            put_total(total3, 128 * c + length * kind, total)
        for q in range(nz):
            s3[q, 16 * c : 16 * c + 16] = every(total3, 128 * c + q, 16, 8).astype(BF16)
        for d in sorted(range(1, nz), key=lambda d: -min(d, nz - d)):
            three(c, d).start()

    to_two(0)
    to_two(1)

    for i in Z_PIECES:
        loop(nz, lambda d: one_z(i, d).wait_recv())
    total = sz1[z].astype(F32)
    for d in range(1, nz):
        total = total + rz1[d].astype(F32)
    put_total(turn, 0, total.reshape(16 * Z_TAPS, 256))
    for p in range(4):
        sz2[p] = every(turn, p, 32, 4).astype(BF16)
    for d in (2, 1, 3):
        two(0, 2, d).start()

    first_copy(dstat, 1).wait_recv()
    loop(REACH + 1, lambda d: second_copy(dstat, 1, d).start())
    to_three(0)
    to_three(1)

    for d in (1, 2, 3):
        two(0, 2, d).wait_recv()
    total = every(turn, y, 32, 4)
    for d in range(1, 4):
        total = total + rz2[d].astype(F32)
    put_total(turn, 128, total)
    for p in range(4):
        sz3[p] = every(turn, 128 + p, 16, 4).astype(BF16)
    for d in (2, 1, 3):
        two(0, 3, d).start()

    loop(REACH + 1, lambda d: second_copy(dstat, 1, d).wait_recv())
    bounds = [(own + f, clip_end(starts, own + f, frames)) for f in range(2)]
    backs = masked_rows(dstat, bounds)
    back_one, back_two = spread(backs, pltpu.roll(backs, 96, 1))
    for f in range(2):
        k = 2 + 2 * core + f
        values = xw[k].reshape(256, 256).astype(F32)
        result = (
            gwin[2 * core + f].reshape(256, 256).astype(F32)
            + da[f] * inv_rows[pl.ds(k, 1)]
            + back_one[f : f + 1]
            + values * (2.0 * back_two[f : f + 1])
        )
        grads_v[f] = result.reshape(16, 16, 256).astype(BF16)
    store_grads = pltpu.make_async_copy(grads_v, grads.at[0], store_sem.at[1])
    store_grads.start()

    for c in range(2):
        own_v[16 * c : 16 * c + 16] = every(total3, 128 * c + z, 16, 8)
    own_v[32:48] = every(turn, 128 + x, 16, 4)
    store_own = pltpu.make_async_copy(own_v, own3, store_sem.at[2])
    store_own.start()

    for kind, buffer in ((0, stat), (1, dstat)):
        first_copy(buffer, kind).wait_send()
        loop(REACH + 1, lambda d: second_copy(buffer, kind, d).wait_send())
    g_partner.wait_send()
    x_partner.wait_send()
    for f in range(2):
        pl.when(core == 0)(g_back[f].wait_send)
        pl.when(core == 1)(g_relay[f].wait_send)
    pl.when(core == 1)(x_ahead.wait_send)
    for d in (1, 2, 3):
        for i in PIECES:
            one_x(i, d).wait_send()
            one_y(i, d).wait_send()
        for c, kind in ((0, 0), (0, 1), (1, 0), (1, 1), (0, 2)):
            two(c, kind, d).wait_send()
    for i in Z_PIECES:
        loop(nz, lambda d: one_z(i, d).wait_send())
    loop(nz, lambda d: three(0, d).wait_send())

    store_out.wait()
    store_grads.wait()
    store_own.wait()
    for c in range(2):
        loop(nz, lambda d: three(c, d).wait_recv())
    for d in (1, 2, 3):
        two(0, 3, d).wait_recv()

    for d in (1, 2, 3):
        two(0, 3, d).wait_send()
    loop(nz, lambda d: three(1, d).wait_send())


def last_sum(scale, out, grads, own3, r3, rz3, *refs):
    out_to, grads_to, wgrads, out_v, grads_v, own_v, r3_v, rz3_v, w_v, sems = refs

    def copy(src, dst, k):
        return pltpu.make_async_copy(src, dst, sems.at[k])

    into = [
        copy(own3, own_v, 0),
        copy(r3, r3_v, 1),
        copy(rz3, rz3_v, 2),
        copy(out, out_v, 3),
        copy(grads, grads_v, 4),
    ]
    for part in into:
        part.start()
    into[3].wait()
    outward = [copy(out_v, out_to, 5)]
    outward[0].start()
    into[4].wait()
    outward.append(copy(grads_v, grads_to, 6))
    outward[1].start()
    for part in into[:3]:
        part.wait()
    total = own_v[0:32]
    for d in range(1, r3_v.shape[0]):
        total = total + r3_v[d].astype(F32)
    along_z = own_v[32:48]
    for d in range(1, rz3_v.shape[0]):
        along_z = along_z + rz3_v[d].astype(F32)
    places = [("z", k) for k in range(16)]
    for c, (low, count, first, length) in enumerate(HALVES):
        taps = [(axis, low + k) for axis in "xy" for k in range(length // 8)]
        places = places + taps + [None] * (16 - len(taps))
    rows = jnp.concatenate([along_z, total], axis=0) * scale
    for n in range(TAPS):
        k = places.index(place_of(n))
        to = 9 * (n % 3) + n // 3
        w_v[to] = rows[k : k + 1]
    outward.append(copy(w_v, wgrads, 7))
    outward[2].start()
    for part in outward:
        part.wait()


def local(nz, ny, scale, video_tile, clip_lengths, kernels, norm_gains, norm_shifts, cotangent):
    hbm = pl.BlockSpec(memory_space=pltpu.HBM)
    dma = pltpu.SemaphoreType.DMA
    made = pl.pallas_call(
        functools.partial(kernel, nz, ny),
        out_shape=(
            jax.ShapeDtypeStruct(video_tile.shape, BF16),
            jax.ShapeDtypeStruct(video_tile.shape, BF16),
            jax.ShapeDtypeStruct((48, 256), F32),
            jax.ShapeDtypeStruct((nz, 32, 256), BF16),
            jax.ShapeDtypeStruct((NX, 16, 256), BF16),
        ),
        in_specs=[hbm] * 6,
        out_specs=(hbm,) * 5,
        scratch_shapes=[
            pltpu.SMEM((1, 6), jnp.int32),
            pltpu.VMEM((1, 256), F32),
            pltpu.VMEM((1, 256), F32),
            pltpu.VMEM((6, 16, 16, 256), BF16),
            pltpu.VMEM((6, 16, 16, 256), BF16),
            pltpu.VMEM((3, 3, 3, 256, 256), BF16),
            pltpu.VMEM((6, 18, 16, 768), BF16),
            pltpu.VMEM((4, 18, 16, 768), BF16),
            pltpu.VMEM((6, 256, 256), BF16),
            pltpu.VMEM((384, 1536), BF16),
            pltpu.VMEM((nz * GROUP, 1, 128), F32),
            pltpu.VMEM((nz * GROUP, 1, 128), F32),
            pltpu.VMEM((8, 256), F32),
            pltpu.VMEM((8, 256), F32),
            pltpu.VMEM((8, 256), F32),
            pltpu.VMEM((2, 256, 256), F32),
            pltpu.VMEM((4, 11, 32, 256), BF16),
            pltpu.VMEM((4, 11, 32, 256), BF16),
            pltpu.VMEM((4, 11, 32, 256), BF16),
            pltpu.VMEM((4, 11, 32, 256), BF16),
            pltpu.VMEM((8, Z_TAPS, 16, 256), BF16),
            pltpu.VMEM((8, Z_TAPS, 16, 256), BF16),
            pltpu.VMEM((4, 96, 256), BF16),
            pltpu.VMEM((4, 96, 256), BF16),
            pltpu.VMEM((4, 96, 256), BF16),
            pltpu.VMEM((4, 96, 256), BF16),
            pltpu.VMEM((4, 32, 256), BF16),
            pltpu.VMEM((4, 32, 256), BF16),
            pltpu.VMEM((4, 16, 256), BF16),
            pltpu.VMEM((4, 96, 256), F32),
            pltpu.VMEM((4, 96, 256), F32),
            pltpu.VMEM((2, 128 * Z_TAPS, 128), F32),
            pltpu.VMEM((2, 256, 128), F32),
            pltpu.VMEM((8, 32, 256), BF16),
            pltpu.VMEM((48, 256), F32),
            pltpu.VMEM((2, 16, 16, 256), BF16),
            pltpu.VMEM((2, 16, 16, 256), BF16),
            dma((8,)),
            dma((5,)),
            dma((5,)),
            dma((2, REACH + 1)),
            dma((2, REACH + 1)),
            dma((2, 5, 4)),
            dma((2, 5, 4)),
            dma((4, 2, 4)),
            dma((4, 2, 4)),
            dma((4, 8)),
            dma((4, 8)),
            dma((3,)),
        ],
        compiler_params=pltpu.CompilerParams(
            collective_id=0, has_side_effects=True, vmem_limit_bytes=60 * 1024 * 1024
        ),
        cost_estimate=pl.CostEstimate(flops=5_500_000_000, bytes_accessed=5_000_000, transcendentals=400_000),
    )(clip_lengths, norm_gains, norm_shifts, video_tile, cotangent, kernels)
    results = pl.pallas_call(
        functools.partial(last_sum, scale),
        out_shape=(
            jax.ShapeDtypeStruct(video_tile.shape, BF16),
            jax.ShapeDtypeStruct(video_tile.shape, BF16),
            jax.ShapeDtypeStruct((TAPS, 1, 256), F32),
        ),
        in_specs=[hbm] * 5,
        out_specs=(hbm,) * 3,
        scratch_shapes=[pltpu.VMEM(part.shape, part.dtype) for part in made]
        + [pltpu.VMEM((TAPS, 1, 256), F32), dma((8,))],
        compiler_params=pltpu.CompilerParams(vmem_limit_bytes=60 * 1024 * 1024),
    )(*made)
    return (results[0], results[1], results[2].transpose(1, 0, 2))


def solution(mesh):
    ny, tm = mesh.shape["dp"], mesh.shape["tm"]
    nz = tm // GROUP
    scale = 1.0 / math.sqrt(ny * tm * 2 * 256)
    placed = P("dp", "tm", None, None, None)
    return jax.shard_map(
        functools.partial(local, nz, ny, scale),
        mesh=mesh,
        in_specs=(placed, P("dp", None), P(), P(), P(), placed),
        out_specs=(placed, placed, P(None, None, ("dp", "tm"))),
        check_vma=False,
    )
```

```python
import functools
import math

import jax
import jax.numpy as jnp
from jax import lax
from jax.experimental import pallas as pl
from jax.experimental.pallas import tpu as pltpu
from jax.sharding import PartitionSpec as P

EPS = 1e-05
NX = 4
NC = 2
GROUP = NX * NC
TAPS = 27
REACH = 12
MESH = pl.DeviceIdType.MESH
F32 = jnp.float32
BF16 = jnp.bfloat16
Z_TAPS = 5
Z_PIECES = {1: (0, 2), 4: (2, 3)}
PIECES = {0: (0, 1), 2: (1, 2), 4: (3, 2), 6: (5, 3), 8: (8, 3)}
HALVES = ((0, 8, 0, 64), (8, 3, 64, 32))


def place_of(n):
    step, lag = n // 3, n % 3
    if step < Z_TAPS:
        return ("xyz"[lag], step)
    k = n - Z_TAPS
    return "xy"[k % 2], k // 2


def iota(shape, dim):
    return lax.broadcasted_iota(jnp.int32, shape, dim)


def clip_begin(starts, t):
    begin = jnp.int32(0)
    for start in starts:
        begin = jnp.where(start <= t, start, begin)
    return begin


def clip_end(starts, t, frames):
    end = jnp.int32(frames)
    for start in reversed(starts):
        end = jnp.where(start > t, start, end)
    return end


def flag(condition):
    return jnp.where(condition, jnp.float32(1.0), jnp.float32(0.0))


def dot(a, b, contract=(1, 0)):
    return lax.dot_general(
        a,
        b,
        (((contract[0],), (contract[1],)), ((), ())),
        preferred_element_type=F32,
    )


def sums_of(rows, matrix):
    high = rows.astype(BF16)
    rest = rows - high.astype(F32)
    middle = rest.astype(BF16)
    low = (rest - middle.astype(F32)).astype(BF16)
    n = rows.shape[0]
    parts = dot(jnp.concatenate([high, middle, low], axis=0), matrix.astype(BF16))
    return parts[:n] + (parts[n : 2 * n] + parts[2 * n :])


def sigmoid(z):
    return 0.5 * jnp.tanh(0.5 * z) + 0.5


def pack_rows(rows):
    place = iota((16, 256), 0)
    stacked = jnp.zeros((16, 256), F32)
    for k, row in enumerate(rows):
        stacked = jnp.where(place == k, row, stacked)
    gather = ((iota((256, 128), 0) >> 3) == (iota((256, 128), 1) & 31)).astype(F32)
    grouped = sums_of(stacked, gather)[:8]
    mine = (iota((8, 128), 1) >> 5) == iota((8, 128), 0)
    return jnp.sum(jnp.where(mine, grouped, 0.0), axis=0, keepdims=True)


def spread(*parts):
    rows = jnp.concatenate(parts, axis=0)
    clean = jnp.where(iota(rows.shape, 1) < 32, rows, 0.0)
    matrix = (iota((128, 256), 0) == (iota((128, 256), 1) >> 3)).astype(F32)
    wide = sums_of(clean, matrix)
    return [wide[8 * k : 8 * k + 8] for k in range(len(parts))]


def masked_rows(buffer, bounds):
    values = buffer[...]
    frame = 2 * iota(values.shape, 0) + (iota(values.shape, 2) >> 6)
    place = iota((8, 128), 0)
    rows = jnp.zeros((8, 128), F32)
    for k, (low, high) in enumerate(bounds):
        inside = (frame >= low) & (frame < high)
        total = jnp.sum(jnp.where(inside, values, 0.0), axis=0)
        rows = jnp.where(place == k, total, rows)
    return rows + pltpu.roll(rows, 64, 1)


def kernel(
    nz,
    ny,
    lens_hbm,
    gain_hbm,
    shift_hbm,
    video,
    cot,
    kern,
    out,
    grads,
    own3,
    r3,
    rz3,
    lens,
    gain,
    shift,
    xw,
    gwin,
    kv,
    gim,
    aim,
    act,
    lhs,
    stat,
    dstat,
    mean_rows,
    scale_rows,
    inv_rows,
    da,
    sx1,
    rx1,
    sy1,
    ry1,
    sz1,
    rz1,
    sx2,
    rx2,
    sy2,
    ry2,
    sz2,
    rz2,
    sz3,
    kx2,
    ky2,
    turn,
    total3,
    s3,
    own_v,
    out_v,
    grads_v,
    load_sem,
    halo_send,
    halo_recv,
    chain_send,
    chain_recv,
    one_send,
    one_recv,
    two_send,
    two_recv,
    three_send,
    three_recv,
    store_sem,
):
    y = lax.axis_index("dp")
    tm = lax.axis_index("tm")
    core = lax.rem(tm, NC)
    x = lax.rem(tm // NC, NX)
    z = tm // GROUP
    within = lax.rem(tm, GROUP)
    chip = tm // NC
    chips = nz * NX
    frames = 2 * nz * GROUP
    base = 4 * chip
    own = 2 * tm

    def at(tm_index, dp_index=None):
        return {"dp": y if dp_index is None else dp_index, "tm": tm_index}

    def x_peer(d):
        return z * GROUP + lax.rem(x + d, NX) * NC + core

    def z_peer(d):
        return lax.rem(z + d, nz) * GROUP + within

    def y_peer(d):
        return lax.rem(y + d, ny)

    def chip_peer(d):
        return lax.rem(chip + d, chips) * NC + core

    partner = chip * NC + 1 - core

    beside = lax.rem(tm + 2 * core - 1 + 2 * chips, 2 * chips)

    stat[...] = jnp.zeros(stat.shape, F32)
    dstat[...] = jnp.zeros(dstat.shape, F32)

    load_x = pltpu.make_async_copy(video.at[0], xw.at[pl.ds(2 + 2 * core, 2)], load_sem.at[0])
    load_g = pltpu.make_async_copy(cot.at[0], gwin.at[pl.ds(2 * core, 2)], load_sem.at[1])
    load_k = [
        pltpu.make_async_copy(kern.at[0, lag], kv.at[lag], load_sem.at[2 + lag]) for lag in range(3)
    ]
    load_small = [
        pltpu.make_async_copy(src, dst, load_sem.at[5 + k])
        for k, (src, dst) in enumerate(((lens_hbm, lens), (gain_hbm, gain), (shift_hbm, shift)))
    ]
    load_x.start()

    barrier = pltpu.get_barrier_semaphore()

    def greet(device):
        pl.semaphore_signal(barrier, inc=1, device_id=device, device_id_type=MESH)

    def greet_before(d, carry):
        greet(at(chip_peer(chips - REACH + d)))
        return carry

    def greet_after(d, carry):
        greet(at(chip_peer(d)))
        return carry

    greet(at(partner))
    greet(at(beside))
    lax.fori_loop(0, REACH, greet_before, 0)
    far = range(REACH // NX + 1, nz - REACH // NX)
    for d in range(1, ny):
        greet(at(tm, y_peer(d)))
    for d in far:
        greet(at(z_peer(d)))
    lax.fori_loop(1, REACH + 1, greet_after, 0)
    load_g.start()
    for copy in load_small:
        copy.start()
    for copy in load_k:
        copy.start()

    for copy in load_small:
        copy.wait()
    starts = []
    begin = jnp.int32(0)
    for k in range(6):
        starts.append(begin)
        begin = begin + lens[0, k]

    load_x.wait()
    sums = []
    for f in range(2):
        values = xw[2 + 2 * core + f].reshape(256, 256).astype(F32)
        sums.append(jnp.sum(values, axis=0, keepdims=True))
        sums.append(jnp.sum(values * values, axis=0, keepdims=True))
    stat[pl.ds(tm, 1)] = pack_rows(sums).reshape(1, 1, 128)

    pl.semaphore_wait(barrier, 2 * REACH + len(far) + (ny - 1) + 2)

    def first_copy(buffer, kind):
        mine = buffer.at[pl.ds(tm, 1)]
        return pltpu.make_async_remote_copy(
            src_ref=mine,
            dst_ref=mine,
            send_sem=chain_send.at[kind, 0],
            recv_sem=chain_recv.at[kind, 0],
            device_id=at(partner),
            device_id_type=MESH,
        )

    def second_copy(buffer, kind, d):
        mine = buffer.at[pl.ds(NC * chip, NC)]
        step = d if kind == 0 else chips - d
        return pltpu.make_async_remote_copy(
            src_ref=mine,
            dst_ref=mine,
            send_sem=chain_send.at[kind, d],
            recv_sem=chain_recv.at[kind, d],
            device_id=at(chip_peer(step)),
            device_id_type=MESH,
        )

    def loop(count, act_on):
        def body(d, carry):
            act_on(d)
            return carry

        lax.fori_loop(1, count, body, 0)

    first_copy(stat, 0).start()

    def halo(src, dst, sent, received, device):
        return pltpu.make_async_remote_copy(
            src_ref=src,
            dst_ref=dst,
            send_sem=halo_send.at[sent],
            recv_sem=halo_recv.at[received],
            device_id=at(device),
            device_id_type=MESH,
        )

    own_g = gwin.at[pl.ds(2 * core, 2)]
    own_x = xw.at[pl.ds(2 + 2 * core, 2)]
    g_partner = halo(cot.at[0], own_g, 0, 0, partner)
    x_partner = halo(video.at[0], own_x, 1, 1, partner)
    g_back = [halo(cot.at[0, f], gwin.at[4 + f], 2 + f, 2 + f, beside) for f in range(2)]
    g_relay = [halo(gwin.at[4 + f], gwin.at[4 + f], 2 + f, 2 + f, partner) for f in range(2)]
    x_ahead = halo(video.at[0], xw.at[pl.ds(0, 2)], 4, 4, beside)
    g_partner.start()
    x_partner.start()

    @pl.when(core == 0)
    def _():
        g_back[0].start()
        g_back[1].start()


    pixel, source = iota((256, 256), 0), iota((256, 256), 1)
    right = ((source == pixel + 1) & ((pixel & 15) != 15)).astype(BF16)
    left = ((source == pixel - 1) & ((pixel & 15) != 0)).astype(BF16)
    both = jnp.concatenate([right, left], axis=0)

    def widen(target, k, values, first, last):
        shifted = dot(both, values).astype(BF16)
        target[k, 1:17, :, 256 * first : 256 * first + 256] = shifted[:256].reshape(16, 16, 256)
        target[k, 1:17, :, 256:512] = values.reshape(16, 16, 256)
        target[k, 1:17, :, 256 * last : 256 * last + 256] = shifted[256:].reshape(16, 16, 256)
        target[k, 0:1] = jnp.zeros((1, 16, 768), BF16)
        target[k, 17:18] = jnp.zeros((1, 16, 768), BF16)

    def backward(lag):
        taken = jnp.concatenate(
            [
                gim[pl.ds(2 * core + lag, 2), 2 - i : 18 - i].reshape(512, 768)
                for i in range(3)
            ],
            axis=1,
        )
        weights = jnp.concatenate(
            [kv[lag, i, j] for i in range(3) for j in range(3)], axis=1
        )
        part = dot(taken, weights, (1, 1))
        for f in range(2):
            piece = part[256 * f : 256 * f + 256]
            if lag == 0:
                da[f] = piece
            else:
                keep = flag(own + f + lag < clip_end(starts, own + f, frames))
                da[f] = da[f] + keep * piece

    def widen_g(v, carry):
        widen(gim, v, gwin[v].reshape(256, 256), 0, 2)
        return carry

    load_g.wait()
    lax.fori_loop(0, 2, lambda v, carry: widen_g(2 * core + v, carry), 0)

    first_copy(stat, 0).wait_recv()
    loop(REACH + 1, lambda d: second_copy(stat, 0, REACH + 1 - d).start())

    load_k[0].wait()
    backward(0)
    g_partner.wait_recv()
    lax.fori_loop(0, 2, lambda v, carry: widen_g(2 - 2 * core + v, carry), 0)

    bounds, counted = [], jnp.zeros((8, 128), F32)
    for k in range(6):
        t = base - 2 + k
        b = clip_begin(starts, t)
        bounds.append((b, t + 1))
        count = jnp.maximum(t + 1 - b, 1).astype(F32)
        counted = jnp.where(iota((8, 128), 0) == k, count, counted)
    counted = jnp.maximum(counted, 1.0) * 2048.0
    row, channel = iota((128, 256), 0), iota((128, 256), 1)
    wanted = 64 * ((row >> 3) & 3) + 8 * (row & 7) + 2 * (row >> 5) + core
    select = (channel == wanted).astype(BF16)
    blank = jnp.zeros((128, 256), BF16)
    for lag, v in ((0, 4), (0, 5), (1, 0), (1, 5), (2, 0), (2, 1)):
        lhs[128 * lag : 128 * lag + 128, 256 * v : 256 * v + 256] = blank

    loop(REACH + 1, lambda d: second_copy(stat, 0, d).wait_recv())

    @pl.when(core == 1)
    def _():
        x_ahead.start()

    averaged = masked_rows(stat, bounds) / counted
    squares = pltpu.roll(averaged, 96, 1)
    inv_std = lax.rsqrt(squares - averaged * averaged + EPS)
    wide_mean, wide_inv = spread(averaged, inv_std)
    mean_rows[...] = wide_mean
    inv_rows[...] = wide_inv
    scale_rows[...] = wide_inv * gain[...]

    def activate(k, carry):
        values = xw[k].reshape(256, 256).astype(F32)
        normed = (values - mean_rows[pl.ds(k, 1)]) * scale_rows[pl.ds(k, 1)] + shift[...]
        act[k] = (normed * sigmoid(normed)).astype(BF16)
        return carry

    x_partner.wait_recv()

    for u in range(4):
        activate(2 + u, 0)
        turned = dot(select, act[2 + u], (1, 1))
        end = clip_end(starts, base + u, frames)
        for lag in range(3):
            masked = turned if lag == 0 else turned * flag(base + u + lag < end)
            v = u + lag
            lhs[128 * lag : 128 * lag + 128, 256 * v : 256 * v + 256] = masked.astype(BF16)

    for f in range(2):

        @pl.when(core == 1)
        def _():
            g_back[f].wait_recv()
            g_relay[f].start()

        @pl.when(core == 0)
        def _():
            g_relay[f].wait_recv()

        widen_g(4 + f, 0)

    def one_x(i, d):
        low, count = PIECES[i]
        target = lax.rem(x + d, NX)
        return pltpu.make_async_remote_copy(
            src_ref=sx1.at[target, pl.ds(low, count)],
            dst_ref=rx1.at[d, pl.ds(low, count)],
            send_sem=one_send.at[0, i // 2, d],
            recv_sem=one_recv.at[0, i // 2, d],
            device_id=at(x_peer(d)),
            device_id_type=MESH,
        )

    def one_y(i, d):
        low, count = PIECES[i]
        target = lax.rem(y + d, ny)
        return pltpu.make_async_remote_copy(
            src_ref=sy1.at[target, pl.ds(low, count)],
            dst_ref=ry1.at[d, pl.ds(low, count)],
            send_sem=one_send.at[1, i // 2, d],
            recv_sem=one_recv.at[1, i // 2, d],
            device_id=at(tm, y_peer(d)),
            device_id_type=MESH,
        )

    def one_z(i, d):
        low, count = Z_PIECES[i]
        return pltpu.make_async_remote_copy(
            src_ref=sz1.at[lax.rem(z + d, nz), pl.ds(low, count)],
            dst_ref=rz1.at[d, pl.ds(low, count)],
            send_sem=three_send.at[2 + i // 4, d],
            recv_sem=three_recv.at[2 + i // 4, d],
            device_id=at(z_peer(d)),
            device_id_type=MESH,
        )

    def put_total(buffer, first, rows):
        for h in range(2):
            buffer[h, first : first + rows.shape[0]] = rows[:, 128 * h : 128 * h + 128]

    def every(buffer, start, count, stride):
        rows = [buffer[h, pl.ds(start, count, stride=stride)] for h in range(2)]
        return jnp.concatenate(rows, axis=1)

    for step in range(9):
        i, j = step // 3, step % 3
        terms = dot(lhs[...], gim[:, 2 - i : 18 - i, :, 256 * j : 256 * j + 256].reshape(1536, 256))
        for lag in range(3):
            axis, slot = place_of(3 * step + lag)
            block = terms[128 * lag : 128 * lag + 128]
            if axis == "z":
                put_total(turn, 128 * slot, block)
                for q in range(nz):
                    sz1[q, slot] = every(turn, 128 * slot + q, 16, 8).astype(BF16)
                continue
            for p in range(4):
                if axis == "x":
                    sx1[p, slot] = block[32 * p : 32 * p + 32].astype(BF16)
                else:
                    rows = [block[32 * q + 8 * p : 32 * q + 8 * p + 8] for q in range(4)]
                    sy1[p, slot] = jnp.concatenate(rows, axis=0).astype(BF16)
        if step in PIECES:
            for d in (2, 1, 3):
                one_x(step, d).start()
                one_y(step, d).start()
        if step in Z_PIECES:
            loop(nz, lambda d: one_z(step, d).start())

    for lag in (1, 2):
        load_k[lag].wait()
        backward(lag)

    lanes = iota((1, 128), 1)
    sums = []
    for f in range(2):
        k = 2 + 2 * core + f
        centred = xw[k].reshape(256, 256).astype(F32) - mean_rows[pl.ds(k, 1)]
        normed = centred * scale_rows[pl.ds(k, 1)] + shift[...]
        sig = sigmoid(normed)
        du = da[f] * (sig * (1.0 + normed * (1.0 - sig))) * gain[...]
        da[f] = du
        sums.append(jnp.sum(du, axis=0, keepdims=True))
        sums.append(jnp.sum(du * centred, axis=0, keepdims=True))
    packed = pack_rows(sums)
    row_of = iota((8, 128), 0)

    def pick(rows, k):
        return jnp.sum(jnp.where(row_of == k, rows, 0.0), axis=0, keepdims=True)

    answer = jnp.zeros((1, 128), F32)
    for f in range(2):
        k = 2 + 2 * core + f
        mean_k, inv_k, n_k = pick(averaged, k), pick(inv_std, k), pick(counted, k)
        sum_du = pltpu.roll(packed, 64, 1) if f else packed
        dr = pltpu.roll(sum_du, 96, 1)
        cubed = inv_k * inv_k * inv_k
        dc1 = (dr * cubed * mean_k - inv_k * sum_du) / n_k
        dc2 = -0.5 * dr * cubed / n_k
        dc2 = pltpu.roll(dc2, 32, 1)
        pair = jnp.where(lanes < 32, dc1, jnp.where(lanes < 64, dc2, 0.0))
        answer = answer + (pltpu.roll(pair, 64, 1) if f else pair)
    dstat[pl.ds(tm, 1)] = answer.reshape(1, 1, 128)
    first_copy(dstat, 1).start()

    @pl.when(core == 0)
    def _():
        x_ahead.wait_recv()
        lax.fori_loop(0, 2, activate, 0)

    def widen_a(k, carry):
        widen(aim, k, act[2 * core + k], 2, 0)
        return carry

    lax.fori_loop(0, 4, widen_a, 0)
    for lag in range(3):
        taken = jnp.concatenate(
            [aim[2 - lag : 4 - lag, i : i + 16].reshape(512, 768) for i in range(3)], axis=1
        )
        part = dot(taken, kv[lag].reshape(2304, 256))
        for f in range(2):
            piece = part[256 * f : 256 * f + 256]
            if lag == 0:
                total = xw[2 + 2 * core + f].reshape(256, 256).astype(F32) + piece
            else:
                keep = flag(own + f - lag >= clip_begin(starts, own + f))
                total = total_f[f] + keep * piece
            if f == 0:
                first = total
            else:
                total_f = [first, total]
    for f in range(2):
        out_v[f] = total_f[f].reshape(16, 16, 256).astype(BF16)
    store_out = pltpu.make_async_copy(out_v, out.at[0], store_sem.at[0])
    store_out.start()

    def two(c, kind, d):
        mine, got = ((sx2, rx2), (sy2, ry2), (sz2, rz2), (sz3, rz3))[kind]
        along_y = kind in (0, 2)
        target = lax.rem(y + d, ny) if along_y else lax.rem(x + d, NX)
        src, dst = mine.at[target], got.at[d]
        if kind < 2:
            some = pl.ds(HALVES[c][2], HALVES[c][3])
            src, dst = src.at[some], dst.at[some]
        return pltpu.make_async_remote_copy(
            src_ref=src,
            dst_ref=dst,
            send_sem=two_send.at[kind, c, d],
            recv_sem=two_recv.at[kind, c, d],
            device_id=at(tm, y_peer(d)) if along_y else at(x_peer(d)),
            device_id_type=MESH,
        )

    def three(c, d):
        return pltpu.make_async_remote_copy(
            src_ref=s3.at[lax.rem(z + d, nz), pl.ds(16 * c, 16)],
            dst_ref=r3.at[d, pl.ds(16 * c, 16)],
            send_sem=three_send.at[c, d],
            recv_sem=three_recv.at[c, d],
            device_id=at(z_peer(d)),
            device_id_type=MESH,
        )

    total3[...] = jnp.zeros(total3.shape, F32)

    def gathered(c, mine, got, keep, staged, me):
        low, count, first, length = HALVES[c]
        for both_p in range(2):
            some = pl.ds(16 * both_p, 16)
            half = mine[me, pl.ds(low, count), some].astype(F32)
            for d in range(1, 4):
                half = half + got[d, pl.ds(low, count), some].astype(F32)
            for p in (2 * both_p, 2 * both_p + 1):
                piece = half[:, 8 * (p % 2) : 8 * (p % 2) + 8].reshape(8 * count, 256)
                if 8 * count < length:
                    blank = jnp.zeros((length - 8 * count, 256), F32)
                    piece = jnp.concatenate([piece, blank], axis=0)
                keep[p, first : first + length] = piece
                staged[p, first : first + length] = piece.astype(BF16)

    def to_two(c):
        pieces = (0, 2, 4, 6) if c == 0 else (8,)
        for kind, one, mine, got, keep, staged, me in (
            (0, one_x, sx1, rx1, kx2, sx2, x),
            (1, one_y, sy1, ry1, ky2, sy2, y),
        ):
            for i in pieces:
                for d in range(1, 4):
                    one(i, d).wait_recv()
            gathered(c, mine, got, keep, staged, me)
            for d in (2, 1, 3):
                two(c, kind, d).start()

    def to_three(c):
        low, count, first, length = HALVES[c]
        some = pl.ds(first, length)
        for kind, keep, got, me in ((0, kx2, rx2, y), (1, ky2, ry2, x)):
            for d in range(1, 4):
                two(c, kind, d).wait_recv()
            total = keep[me, some]
            for d in range(1, 4):
                total = total + got[d, some].astype(F32)
            put_total(total3, 128 * c + length * kind, total)
        for q in range(nz):
            s3[q, 16 * c : 16 * c + 16] = every(total3, 128 * c + q, 16, 8).astype(BF16)
        for d in sorted(range(1, nz), key=lambda d: -min(d, nz - d)):
            three(c, d).start()

    to_two(0)
    to_two(1)

    for i in Z_PIECES:
        loop(nz, lambda d: one_z(i, d).wait_recv())
    total = sz1[z].astype(F32)
    for d in range(1, nz):
        total = total + rz1[d].astype(F32)
    put_total(turn, 0, total.reshape(16 * Z_TAPS, 256))
    for p in range(4):
        sz2[p] = every(turn, p, 32, 4).astype(BF16)
    for d in (2, 1, 3):
        two(0, 2, d).start()

    first_copy(dstat, 1).wait_recv()
    loop(REACH + 1, lambda d: second_copy(dstat, 1, d).start())
    to_three(0)
    to_three(1)

    for d in (1, 2, 3):
        two(0, 2, d).wait_recv()
    total = every(turn, y, 32, 4)
    for d in range(1, 4):
        total = total + rz2[d].astype(F32)
    put_total(turn, 128, total)
    for p in range(4):
        sz3[p] = every(turn, 128 + p, 16, 4).astype(BF16)
    for d in (2, 1, 3):
        two(0, 3, d).start()

    loop(REACH + 1, lambda d: second_copy(dstat, 1, d).wait_recv())
    bounds = [(own + f, clip_end(starts, own + f, frames)) for f in range(2)]
    backs = masked_rows(dstat, bounds)
    back_one, back_two = spread(backs, pltpu.roll(backs, 96, 1))
    for f in range(2):
        k = 2 + 2 * core + f
        values = xw[k].reshape(256, 256).astype(F32)
        result = (
            gwin[2 * core + f].reshape(256, 256).astype(F32)
            + da[f] * inv_rows[pl.ds(k, 1)]
            + back_one[f : f + 1]
            + values * (2.0 * back_two[f : f + 1])
        )
        grads_v[f] = result.reshape(16, 16, 256).astype(BF16)
    store_grads = pltpu.make_async_copy(grads_v, grads.at[0], store_sem.at[1])
    store_grads.start()

    for c in range(2):
        own_v[16 * c : 16 * c + 16] = every(total3, 128 * c + z, 16, 8)
    own_v[32:48] = every(turn, 128 + x, 16, 4)
    store_own = pltpu.make_async_copy(own_v, own3, store_sem.at[2])
    store_own.start()

    for kind, buffer in ((0, stat), (1, dstat)):
        first_copy(buffer, kind).wait_send()
        loop(REACH + 1, lambda d: second_copy(buffer, kind, d).wait_send())
    g_partner.wait_send()
    x_partner.wait_send()
    for f in range(2):
        pl.when(core == 0)(g_back[f].wait_send)
        pl.when(core == 1)(g_relay[f].wait_send)
    pl.when(core == 1)(x_ahead.wait_send)
    for d in (1, 2, 3):
        for i in PIECES:
            one_x(i, d).wait_send()
            one_y(i, d).wait_send()
        for c, kind in ((0, 0), (0, 1), (1, 0), (1, 1), (0, 2)):
            two(c, kind, d).wait_send()
    for i in Z_PIECES:
        loop(nz, lambda d: one_z(i, d).wait_send())
    loop(nz, lambda d: three(0, d).wait_send())

    store_out.wait()
    store_grads.wait()
    store_own.wait()
    for c in range(2):
        loop(nz, lambda d: three(c, d).wait_recv())
    for d in (1, 2, 3):
        two(0, 3, d).wait_recv()

    for d in (1, 2, 3):
        two(0, 3, d).wait_send()
    loop(nz, lambda d: three(1, d).wait_send())


def last_sum(scale, out, grads, own3, r3, rz3, *refs):
    out_to, grads_to, wgrads, out_v, grads_v, own_v, r3_v, rz3_v, w_v, sems = refs

    def copy(src, dst, k):
        return pltpu.make_async_copy(src, dst, sems.at[k])

    into = [
        copy(own3, own_v, 0),
        copy(r3, r3_v, 1),
        copy(rz3, rz3_v, 2),
        copy(out, out_v, 3),
        copy(grads, grads_v, 4),
    ]
    for part in into:
        part.start()
    into[3].wait()
    outward = [copy(out_v, out_to, 5)]
    outward[0].start()
    into[4].wait()
    outward.append(copy(grads_v, grads_to, 6))
    outward[1].start()
    for part in into[:3]:
        part.wait()
    total = own_v[0:32]
    for d in range(1, r3_v.shape[0]):
        total = total + r3_v[d].astype(F32)
    along_z = own_v[32:48]
    for d in range(1, rz3_v.shape[0]):
        along_z = along_z + rz3_v[d].astype(F32)
    places = [("z", k) for k in range(16)]
    for c, (low, count, first, length) in enumerate(HALVES):
        taps = [(axis, low + k) for axis in "xy" for k in range(length // 8)]
        places = places + taps + [None] * (16 - len(taps))
    rows = jnp.concatenate([along_z, total], axis=0) * scale
    for n in range(TAPS):
        k = places.index(place_of(n))
        to = 9 * (n % 3) + n // 3
        w_v[to] = rows[k : k + 1]
    outward.append(copy(w_v, wgrads, 7))
    outward[2].start()
    for part in outward:
        part.wait()


def local(nz, ny, scale, video_tile, clip_lengths, kernels, norm_gains, norm_shifts, cotangent):
    hbm = pl.BlockSpec(memory_space=pltpu.HBM)
    dma = pltpu.SemaphoreType.DMA
    made = pl.pallas_call(
        functools.partial(kernel, nz, ny),
        out_shape=(
            jax.ShapeDtypeStruct(video_tile.shape, BF16),
            jax.ShapeDtypeStruct(video_tile.shape, BF16),
            jax.ShapeDtypeStruct((48, 256), F32),
            jax.ShapeDtypeStruct((nz, 32, 256), BF16),
            jax.ShapeDtypeStruct((NX, 16, 256), BF16),
        ),
        in_specs=[hbm] * 6,
        out_specs=(hbm,) * 5,
        scratch_shapes=[
            pltpu.SMEM((1, 6), jnp.int32),
            pltpu.VMEM((1, 256), F32),
            pltpu.VMEM((1, 256), F32),
            pltpu.VMEM((6, 16, 16, 256), BF16),
            pltpu.VMEM((6, 16, 16, 256), BF16),
            pltpu.VMEM((3, 3, 3, 256, 256), BF16),
            pltpu.VMEM((6, 18, 16, 768), BF16),
            pltpu.VMEM((4, 18, 16, 768), BF16),
            pltpu.VMEM((6, 256, 256), BF16),
            pltpu.VMEM((384, 1536), BF16),
            pltpu.VMEM((nz * GROUP, 1, 128), F32),
            pltpu.VMEM((nz * GROUP, 1, 128), F32),
            pltpu.VMEM((8, 256), F32),
            pltpu.VMEM((8, 256), F32),
            pltpu.VMEM((8, 256), F32),
            pltpu.VMEM((2, 256, 256), F32),
            pltpu.VMEM((4, 11, 32, 256), BF16),
            pltpu.VMEM((4, 11, 32, 256), BF16),
            pltpu.VMEM((4, 11, 32, 256), BF16),
            pltpu.VMEM((4, 11, 32, 256), BF16),
            pltpu.VMEM((8, Z_TAPS, 16, 256), BF16),
            pltpu.VMEM((8, Z_TAPS, 16, 256), BF16),
            pltpu.VMEM((4, 96, 256), BF16),
            pltpu.VMEM((4, 96, 256), BF16),
            pltpu.VMEM((4, 96, 256), BF16),
            pltpu.VMEM((4, 96, 256), BF16),
            pltpu.VMEM((4, 32, 256), BF16),
            pltpu.VMEM((4, 32, 256), BF16),
            pltpu.VMEM((4, 16, 256), BF16),
            pltpu.VMEM((4, 96, 256), F32),
            pltpu.VMEM((4, 96, 256), F32),
            pltpu.VMEM((2, 128 * Z_TAPS, 128), F32),
            pltpu.VMEM((2, 256, 128), F32),
            pltpu.VMEM((8, 32, 256), BF16),
            pltpu.VMEM((48, 256), F32),
            pltpu.VMEM((2, 16, 16, 256), BF16),
            pltpu.VMEM((2, 16, 16, 256), BF16),
            dma((8,)),
            dma((5,)),
            dma((5,)),
            dma((2, REACH + 1)),
            dma((2, REACH + 1)),
            dma((2, 5, 4)),
            dma((2, 5, 4)),
            dma((4, 2, 4)),
            dma((4, 2, 4)),
            dma((4, 8)),
            dma((4, 8)),
            dma((3,)),
        ],
        compiler_params=pltpu.CompilerParams(
            collective_id=0, has_side_effects=True, vmem_limit_bytes=60 * 1024 * 1024
        ),
        cost_estimate=pl.CostEstimate(flops=5_500_000_000, bytes_accessed=5_000_000, transcendentals=400_000),
    )(clip_lengths, norm_gains, norm_shifts, video_tile, cotangent, kernels)
    results = pl.pallas_call(
        functools.partial(last_sum, scale),
        out_shape=(
            jax.ShapeDtypeStruct(video_tile.shape, BF16),
            jax.ShapeDtypeStruct(video_tile.shape, BF16),
            jax.ShapeDtypeStruct((TAPS, 1, 256), F32),
        ),
        in_specs=[hbm] * 5,
        out_specs=(hbm,) * 3,
        scratch_shapes=[pltpu.VMEM(part.shape, part.dtype) for part in made]
        + [pltpu.VMEM((TAPS, 1, 256), F32), dma((8,))],
        compiler_params=pltpu.CompilerParams(vmem_limit_bytes=60 * 1024 * 1024),
    )(*made)
    return (results[0], results[1], results[2].transpose(1, 0, 2))


def solution(mesh):
    ny, tm = mesh.shape["dp"], mesh.shape["tm"]
    nz = tm // GROUP
    scale = 1.0 / math.sqrt(ny * tm * 2 * 256)
    placed = P("dp", "tm", None, None, None)
    return jax.shard_map(
        functools.partial(local, nz, ny, scale),
        mesh=mesh,
        in_specs=(placed, P("dp", None), P(), P(), P(), placed),
        out_specs=(placed, placed, P(None, None, ("dp", "tm"))),
        check_vma=False,
    )
```

```python
import functools
import math

import jax
import jax.numpy as jnp
from jax import lax
from jax.experimental import pallas as pl
from jax.experimental.pallas import tpu as pltpu
from jax.sharding import PartitionSpec as P

EPS = 1e-05
NX = 4
NC = 2
GROUP = NX * NC
TAPS = 27
REACH = 12
MESH = pl.DeviceIdType.MESH
F32 = jnp.float32
BF16 = jnp.bfloat16
Z_TAPS = 5
Z_PIECES = {1: (0, 2), 4: (2, 3)}
PIECES = {0: (0, 1), 2: (1, 2), 4: (3, 2), 6: (5, 3), 8: (8, 3)}
HALVES = ((0, 8, 0, 64), (8, 3, 64, 32))


def place_of(n):
    step, lag = n // 3, n % 3
    if step < Z_TAPS:
        return ("xyz"[lag], step)
    k = n - Z_TAPS
    return "xy"[k % 2], k // 2


def iota(shape, dim):
    return lax.broadcasted_iota(jnp.int32, shape, dim)


def clip_begin(starts, t):
    begin = jnp.int32(0)
    for start in starts:
        begin = jnp.where(start <= t, start, begin)
    return begin


def clip_end(starts, t, frames):
    end = jnp.int32(frames)
    for start in reversed(starts):
        end = jnp.where(start > t, start, end)
    return end


def flag(condition):
    return jnp.where(condition, jnp.float32(1.0), jnp.float32(0.0))


def dot(a, b, contract=(1, 0)):
    return lax.dot_general(
        a,
        b,
        (((contract[0],), (contract[1],)), ((), ())),
        preferred_element_type=F32,
    )


def sums_of(rows, matrix):
    high = rows.astype(BF16)
    rest = rows - high.astype(F32)
    middle = rest.astype(BF16)
    low = (rest - middle.astype(F32)).astype(BF16)
    n = rows.shape[0]
    parts = dot(jnp.concatenate([high, middle, low], axis=0), matrix.astype(BF16))
    return parts[:n] + (parts[n : 2 * n] + parts[2 * n :])


def sigmoid(z):
    return 0.5 * jnp.tanh(0.5 * z) + 0.5


def pack_rows(rows):
    place = iota((16, 256), 0)
    stacked = jnp.zeros((16, 256), F32)
    for k, row in enumerate(rows):
        stacked = jnp.where(place == k, row, stacked)
    gather = ((iota((256, 128), 0) >> 3) == (iota((256, 128), 1) & 31)).astype(F32)
    grouped = sums_of(stacked, gather)[:8]
    mine = (iota((8, 128), 1) >> 5) == iota((8, 128), 0)
    return jnp.sum(jnp.where(mine, grouped, 0.0), axis=0, keepdims=True)


def spread(*parts):
    rows = jnp.concatenate(parts, axis=0)
    clean = jnp.where(iota(rows.shape, 1) < 32, rows, 0.0)
    matrix = (iota((128, 256), 0) == (iota((128, 256), 1) >> 3)).astype(F32)
    wide = sums_of(clean, matrix)
    return [wide[8 * k : 8 * k + 8] for k in range(len(parts))]


def masked_rows(buffer, bounds):
    values = buffer[...]
    frame = 2 * iota(values.shape, 0) + (iota(values.shape, 2) >> 6)
    place = iota((8, 128), 0)
    rows = jnp.zeros((8, 128), F32)
    for k, (low, high) in enumerate(bounds):
        inside = (frame >= low) & (frame < high)
        total = jnp.sum(jnp.where(inside, values, 0.0), axis=0)
        rows = jnp.where(place == k, total, rows)
    return rows + pltpu.roll(rows, 64, 1)


def kernel(
    nz,
    ny,
    lens_hbm,
    gain_hbm,
    shift_hbm,
    video,
    cot,
    kern,
    out,
    grads,
    own3,
    r3,
    rz3,
    lens,
    gain,
    shift,
    xw,
    gwin,
    kv,
    gim,
    aim,
    act,
    lhs,
    stat,
    dstat,
    mean_rows,
    scale_rows,
    inv_rows,
    da,
    sx1,
    rx1,
    sy1,
    ry1,
    sz1,
    rz1,
    sx2,
    rx2,
    sy2,
    ry2,
    sz2,
    rz2,
    sz3,
    kx2,
    ky2,
    turn,
    total3,
    s3,
    own_v,
    out_v,
    grads_v,
    load_sem,
    halo_send,
    halo_recv,
    chain_send,
    chain_recv,
    one_send,
    one_recv,
    two_send,
    two_recv,
    three_send,
    three_recv,
    store_sem,
):
    y = lax.axis_index("dp")
    tm = lax.axis_index("tm")
    core = lax.rem(tm, NC)
    x = lax.rem(tm // NC, NX)
    z = tm // GROUP
    within = lax.rem(tm, GROUP)
    chip = tm // NC
    chips = nz * NX
    frames = 2 * nz * GROUP
    base = 4 * chip
    own = 2 * tm

    def at(tm_index, dp_index=None):
        return {"dp": y if dp_index is None else dp_index, "tm": tm_index}

    def x_peer(d):
        return z * GROUP + lax.rem(x + d, NX) * NC + core

    def z_peer(d):
        return lax.rem(z + d, nz) * GROUP + within

    def y_peer(d):
        return lax.rem(y + d, ny)

    def chip_peer(d):
        return lax.rem(chip + d, chips) * NC + core

    partner = chip * NC + 1 - core

    beside = lax.rem(tm + 2 * core - 1 + 2 * chips, 2 * chips)

    stat[...] = jnp.zeros(stat.shape, F32)
    dstat[...] = jnp.zeros(dstat.shape, F32)

    load_x = pltpu.make_async_copy(video.at[0], xw.at[pl.ds(2 + 2 * core, 2)], load_sem.at[0])
    load_g = pltpu.make_async_copy(cot.at[0], gwin.at[pl.ds(2 * core, 2)], load_sem.at[1])
    load_k = [
        pltpu.make_async_copy(kern.at[0, lag], kv.at[lag], load_sem.at[2 + lag]) for lag in range(3)
    ]
    load_small = [
        pltpu.make_async_copy(src, dst, load_sem.at[5 + k])
        for k, (src, dst) in enumerate(((lens_hbm, lens), (gain_hbm, gain), (shift_hbm, shift)))
    ]
    load_x.start()

    barrier = pltpu.get_barrier_semaphore()

    def greet(device):
        pl.semaphore_signal(barrier, inc=1, device_id=device, device_id_type=MESH)

    def greet_before(d, carry):
        greet(at(chip_peer(chips - REACH + d)))
        return carry

    greet(at(partner))
    greet(at(beside))
    lax.fori_loop(0, REACH, greet_before, 0)
    far = range(REACH // NX + 1, nz - REACH // NX)
    for d in range(1, ny):
        greet(at(tm, y_peer(d)))
    for d in far:
        greet(at(z_peer(d)))
    load_g.start()
    for copy in load_small:
        copy.start()
    for copy in load_k:
        copy.start()

    for copy in load_small:
        copy.wait()
    starts = []
    begin = jnp.int32(0)
    for k in range(6):
        starts.append(begin)
        begin = begin + lens[0, k]

    load_x.wait()
    sums = []
    for f in range(2):
        values = xw[2 + 2 * core + f].reshape(256, 256).astype(F32)
        sums.append(jnp.sum(values, axis=0, keepdims=True))
        sums.append(jnp.sum(values * values, axis=0, keepdims=True))
    stat[pl.ds(tm, 1)] = pack_rows(sums).reshape(1, 1, 128)

    pl.semaphore_wait(barrier, REACH + len(far) + (ny - 1) + 2)

    def first_copy(buffer, kind):
        mine = buffer.at[pl.ds(tm, 1)]
        return pltpu.make_async_remote_copy(
            src_ref=mine,
            dst_ref=mine,
            send_sem=chain_send.at[kind, 0],
            recv_sem=chain_recv.at[kind, 0],
            device_id=at(partner),
            device_id_type=MESH,
        )

    def second_copy(buffer, kind, d):
        mine = buffer.at[pl.ds(NC * chip, NC)]
        step = d if kind == 0 else chips - d
        return pltpu.make_async_remote_copy(
            src_ref=mine,
            dst_ref=mine,
            send_sem=chain_send.at[kind, d],
            recv_sem=chain_recv.at[kind, d],
            device_id=at(chip_peer(step)),
            device_id_type=MESH,
        )

    def loop(count, act_on):
        def body(d, carry):
            act_on(d)
            return carry

        lax.fori_loop(1, count, body, 0)

    first_copy(stat, 0).start()

    def halo(src, dst, sent, received, device):
        return pltpu.make_async_remote_copy(
            src_ref=src,
            dst_ref=dst,
            send_sem=halo_send.at[sent],
            recv_sem=halo_recv.at[received],
            device_id=at(device),
            device_id_type=MESH,
        )

    own_g = gwin.at[pl.ds(2 * core, 2)]
    own_x = xw.at[pl.ds(2 + 2 * core, 2)]
    g_partner = halo(cot.at[0], own_g, 0, 0, partner)
    x_partner = halo(video.at[0], own_x, 1, 1, partner)
    g_back = [halo(cot.at[0, f], gwin.at[4 + f], 2 + f, 2 + f, beside) for f in range(2)]
    g_relay = [halo(gwin.at[4 + f], gwin.at[4 + f], 2 + f, 2 + f, partner) for f in range(2)]
    x_ahead = halo(video.at[0], xw.at[pl.ds(0, 2)], 4, 4, beside)
    g_partner.start()
    x_partner.start()

    @pl.when(core == 0)
    def _():
        g_back[0].start()
        g_back[1].start()


    pixel, source = iota((256, 256), 0), iota((256, 256), 1)
    right = ((source == pixel + 1) & ((pixel & 15) != 15)).astype(BF16)
    left = ((source == pixel - 1) & ((pixel & 15) != 0)).astype(BF16)
    both = jnp.concatenate([right, left], axis=0)

    def widen(target, k, values, first, last):
        shifted = dot(both, values).astype(BF16)
        target[k, 1:17, :, 256 * first : 256 * first + 256] = shifted[:256].reshape(16, 16, 256)
        target[k, 1:17, :, 256:512] = values.reshape(16, 16, 256)
        target[k, 1:17, :, 256 * last : 256 * last + 256] = shifted[256:].reshape(16, 16, 256)
        target[k, 0:1] = jnp.zeros((1, 16, 768), BF16)
        target[k, 17:18] = jnp.zeros((1, 16, 768), BF16)

    def backward(lag):
        taken = jnp.concatenate(
            [
                gim[pl.ds(2 * core + lag, 2), 2 - i : 18 - i].reshape(512, 768)
                for i in range(3)
            ],
            axis=1,
        )
        weights = jnp.concatenate(
            [kv[lag, i, j] for i in range(3) for j in range(3)], axis=1
        )
        part = dot(taken, weights, (1, 1))
        for f in range(2):
            piece = part[256 * f : 256 * f + 256]
            if lag == 0:
                da[f] = piece
            else:
                keep = flag(own + f + lag < clip_end(starts, own + f, frames))
                da[f] = da[f] + keep * piece

    def widen_g(v, carry):
        widen(gim, v, gwin[v].reshape(256, 256), 0, 2)
        return carry

    load_g.wait()
    lax.fori_loop(0, 2, lambda v, carry: widen_g(2 * core + v, carry), 0)

    first_copy(stat, 0).wait_recv()
    loop(REACH + 1, lambda d: second_copy(stat, 0, REACH + 1 - d).start())

    load_k[0].wait()
    backward(0)
    g_partner.wait_recv()
    lax.fori_loop(0, 2, lambda v, carry: widen_g(2 - 2 * core + v, carry), 0)

    bounds, counted = [], jnp.zeros((8, 128), F32)
    for k in range(6):
        t = base - 2 + k
        b = clip_begin(starts, t)
        bounds.append((b, t + 1))
        count = jnp.maximum(t + 1 - b, 1).astype(F32)
        counted = jnp.where(iota((8, 128), 0) == k, count, counted)
    counted = jnp.maximum(counted, 1.0) * 2048.0
    row, channel = iota((128, 256), 0), iota((128, 256), 1)
    wanted = 64 * ((row >> 3) & 3) + 8 * (row & 7) + 2 * (row >> 5) + core
    select = (channel == wanted).astype(BF16)
    blank = jnp.zeros((128, 256), BF16)
    for lag, v in ((0, 4), (0, 5), (1, 0), (1, 5), (2, 0), (2, 1)):
        lhs[128 * lag : 128 * lag + 128, 256 * v : 256 * v + 256] = blank

    loop(REACH + 1, lambda d: second_copy(stat, 0, d).wait_recv())

    @pl.when(core == 1)
    def _():
        x_ahead.start()

    averaged = masked_rows(stat, bounds) / counted
    squares = pltpu.roll(averaged, 96, 1)
    inv_std = lax.rsqrt(squares - averaged * averaged + EPS)
    wide_mean, wide_inv = spread(averaged, inv_std)
    mean_rows[...] = wide_mean
    inv_rows[...] = wide_inv
    scale_rows[...] = wide_inv * gain[...]

    def activate(k, carry):
        values = xw[k].reshape(256, 256).astype(F32)
        normed = (values - mean_rows[pl.ds(k, 1)]) * scale_rows[pl.ds(k, 1)] + shift[...]
        act[k] = (normed * sigmoid(normed)).astype(BF16)
        return carry

    x_partner.wait_recv()

    for u in range(4):
        activate(2 + u, 0)
        turned = dot(select, act[2 + u], (1, 1))
        end = clip_end(starts, base + u, frames)
        for lag in range(3):
            masked = turned if lag == 0 else turned * flag(base + u + lag < end)
            v = u + lag
            lhs[128 * lag : 128 * lag + 128, 256 * v : 256 * v + 256] = masked.astype(BF16)

    for f in range(2):

        @pl.when(core == 1)
        def _():
            g_back[f].wait_recv()
            g_relay[f].start()

        @pl.when(core == 0)
        def _():
            g_relay[f].wait_recv()

        widen_g(4 + f, 0)

    def one_x(i, d):
        low, count = PIECES[i]
        target = lax.rem(x + d, NX)
        return pltpu.make_async_remote_copy(
            src_ref=sx1.at[target, pl.ds(low, count)],
            dst_ref=rx1.at[d, pl.ds(low, count)],
            send_sem=one_send.at[0, i // 2, d],
            recv_sem=one_recv.at[0, i // 2, d],
            device_id=at(x_peer(d)),
            device_id_type=MESH,
        )

    def one_y(i, d):
        low, count = PIECES[i]
        target = lax.rem(y + d, ny)
        return pltpu.make_async_remote_copy(
            src_ref=sy1.at[target, pl.ds(low, count)],
            dst_ref=ry1.at[d, pl.ds(low, count)],
            send_sem=one_send.at[1, i // 2, d],
            recv_sem=one_recv.at[1, i // 2, d],
            device_id=at(tm, y_peer(d)),
            device_id_type=MESH,
        )

    def one_z(i, d):
        low, count = Z_PIECES[i]
        return pltpu.make_async_remote_copy(
            src_ref=sz1.at[lax.rem(z + d, nz), pl.ds(low, count)],
            dst_ref=rz1.at[d, pl.ds(low, count)],
            send_sem=three_send.at[2 + i // 4, d],
            recv_sem=three_recv.at[2 + i // 4, d],
            device_id=at(z_peer(d)),
            device_id_type=MESH,
        )

    def put_total(buffer, first, rows):
        for h in range(2):
            buffer[h, first : first + rows.shape[0]] = rows[:, 128 * h : 128 * h + 128]

    def every(buffer, start, count, stride):
        rows = [buffer[h, pl.ds(start, count, stride=stride)] for h in range(2)]
        return jnp.concatenate(rows, axis=1)

    for step in range(9):
        i, j = step // 3, step % 3
        terms = dot(lhs[...], gim[:, 2 - i : 18 - i, :, 256 * j : 256 * j + 256].reshape(1536, 256))
        for lag in range(3):
            axis, slot = place_of(3 * step + lag)
            block = terms[128 * lag : 128 * lag + 128]
            if axis == "z":
                put_total(turn, 128 * slot, block)
                for q in range(nz):
                    sz1[q, slot] = every(turn, 128 * slot + q, 16, 8).astype(BF16)
                continue
            for p in range(4):
                if axis == "x":
                    sx1[p, slot] = block[32 * p : 32 * p + 32].astype(BF16)
                else:
                    rows = [block[32 * q + 8 * p : 32 * q + 8 * p + 8] for q in range(4)]
                    sy1[p, slot] = jnp.concatenate(rows, axis=0).astype(BF16)
        if step in PIECES:
            for d in (2, 1, 3):
                one_x(step, d).start()
                one_y(step, d).start()
        if step in Z_PIECES:
            loop(nz, lambda d: one_z(step, d).start())

    for lag in (1, 2):
        load_k[lag].wait()
        backward(lag)

    lanes = iota((1, 128), 1)
    sums = []
    for f in range(2):
        k = 2 + 2 * core + f
        centred = xw[k].reshape(256, 256).astype(F32) - mean_rows[pl.ds(k, 1)]
        normed = centred * scale_rows[pl.ds(k, 1)] + shift[...]
        sig = sigmoid(normed)
        du = da[f] * (sig * (1.0 + normed * (1.0 - sig))) * gain[...]
        da[f] = du
        sums.append(jnp.sum(du, axis=0, keepdims=True))
        sums.append(jnp.sum(du * centred, axis=0, keepdims=True))
    packed = pack_rows(sums)
    row_of = iota((8, 128), 0)

    def pick(rows, k):
        return jnp.sum(jnp.where(row_of == k, rows, 0.0), axis=0, keepdims=True)

    answer = jnp.zeros((1, 128), F32)
    for f in range(2):
        k = 2 + 2 * core + f
        mean_k, inv_k, n_k = pick(averaged, k), pick(inv_std, k), pick(counted, k)
        sum_du = pltpu.roll(packed, 64, 1) if f else packed
        dr = pltpu.roll(sum_du, 96, 1)
        cubed = inv_k * inv_k * inv_k
        dc1 = (dr * cubed * mean_k - inv_k * sum_du) / n_k
        dc2 = -0.5 * dr * cubed / n_k
        dc2 = pltpu.roll(dc2, 32, 1)
        pair = jnp.where(lanes < 32, dc1, jnp.where(lanes < 64, dc2, 0.0))
        answer = answer + (pltpu.roll(pair, 64, 1) if f else pair)
    dstat[pl.ds(tm, 1)] = answer.reshape(1, 1, 128)
    first_copy(dstat, 1).start()

    @pl.when(core == 0)
    def _():
        x_ahead.wait_recv()
        lax.fori_loop(0, 2, activate, 0)

    def widen_a(k, carry):
        widen(aim, k, act[2 * core + k], 2, 0)
        return carry

    lax.fori_loop(0, 4, widen_a, 0)
    for lag in range(3):
        taken = jnp.concatenate(
            [aim[2 - lag : 4 - lag, i : i + 16].reshape(512, 768) for i in range(3)], axis=1
        )
        part = dot(taken, kv[lag].reshape(2304, 256))
        for f in range(2):
            piece = part[256 * f : 256 * f + 256]
            if lag == 0:
                total = xw[2 + 2 * core + f].reshape(256, 256).astype(F32) + piece
            else:
                keep = flag(own + f - lag >= clip_begin(starts, own + f))
                total = total_f[f] + keep * piece
            if f == 0:
                first = total
            else:
                total_f = [first, total]
    for f in range(2):
        out_v[f] = total_f[f].reshape(16, 16, 256).astype(BF16)
    store_out = pltpu.make_async_copy(out_v, out.at[0], store_sem.at[0])
    store_out.start()

    def two(c, kind, d):
        mine, got = ((sx2, rx2), (sy2, ry2), (sz2, rz2), (sz3, rz3))[kind]
        along_y = kind in (0, 2)
        target = lax.rem(y + d, ny) if along_y else lax.rem(x + d, NX)
        src, dst = mine.at[target], got.at[d]
        if kind < 2:
            some = pl.ds(HALVES[c][2], HALVES[c][3])
            src, dst = src.at[some], dst.at[some]
        return pltpu.make_async_remote_copy(
            src_ref=src,
            dst_ref=dst,
            send_sem=two_send.at[kind, c, d],
            recv_sem=two_recv.at[kind, c, d],
            device_id=at(tm, y_peer(d)) if along_y else at(x_peer(d)),
            device_id_type=MESH,
        )

    def three(c, d):
        return pltpu.make_async_remote_copy(
            src_ref=s3.at[lax.rem(z + d, nz), pl.ds(16 * c, 16)],
            dst_ref=r3.at[d, pl.ds(16 * c, 16)],
            send_sem=three_send.at[c, d],
            recv_sem=three_recv.at[c, d],
            device_id=at(z_peer(d)),
            device_id_type=MESH,
        )

    total3[...] = jnp.zeros(total3.shape, F32)

    def gathered(c, mine, got, keep, staged, me):
        low, count, first, length = HALVES[c]
        for both_p in range(2):
            some = pl.ds(16 * both_p, 16)
            half = mine[me, pl.ds(low, count), some].astype(F32)
            for d in range(1, 4):
                half = half + got[d, pl.ds(low, count), some].astype(F32)
            for p in (2 * both_p, 2 * both_p + 1):
                piece = half[:, 8 * (p % 2) : 8 * (p % 2) + 8].reshape(8 * count, 256)
                if 8 * count < length:
                    blank = jnp.zeros((length - 8 * count, 256), F32)
                    piece = jnp.concatenate([piece, blank], axis=0)
                keep[p, first : first + length] = piece
                staged[p, first : first + length] = piece.astype(BF16)

    def to_two(c):
        pieces = (0, 2, 4, 6) if c == 0 else (8,)
        for kind, one, mine, got, keep, staged, me in (
            (0, one_x, sx1, rx1, kx2, sx2, x),
            (1, one_y, sy1, ry1, ky2, sy2, y),
        ):
            for i in pieces:
                for d in range(1, 4):
                    one(i, d).wait_recv()
            gathered(c, mine, got, keep, staged, me)
            for d in (2, 1, 3):
                two(c, kind, d).start()

    def to_three(c):
        low, count, first, length = HALVES[c]
        some = pl.ds(first, length)
        for kind, keep, got, me in ((0, kx2, rx2, y), (1, ky2, ry2, x)):
            for d in range(1, 4):
                two(c, kind, d).wait_recv()
            total = keep[me, some]
            for d in range(1, 4):
                total = total + got[d, some].astype(F32)
            put_total(total3, 128 * c + length * kind, total)
        for q in range(nz):
            s3[q, 16 * c : 16 * c + 16] = every(total3, 128 * c + q, 16, 8).astype(BF16)
        for d in sorted(range(1, nz), key=lambda d: -min(d, nz - d)):
            three(c, d).start()

    to_two(0)
    to_two(1)

    for i in Z_PIECES:
        loop(nz, lambda d: one_z(i, d).wait_recv())
    total = sz1[z].astype(F32)
    for d in range(1, nz):
        total = total + rz1[d].astype(F32)
    put_total(turn, 0, total.reshape(16 * Z_TAPS, 256))
    for p in range(4):
        sz2[p] = every(turn, p, 32, 4).astype(BF16)
    for d in (2, 1, 3):
        two(0, 2, d).start()

    first_copy(dstat, 1).wait_recv()
    loop(REACH + 1, lambda d: second_copy(dstat, 1, d).start())
    to_three(0)
    to_three(1)

    for d in (1, 2, 3):
        two(0, 2, d).wait_recv()
    total = every(turn, y, 32, 4)
    for d in range(1, 4):
        total = total + rz2[d].astype(F32)
    put_total(turn, 128, total)
    for p in range(4):
        sz3[p] = every(turn, 128 + p, 16, 4).astype(BF16)
    for d in (2, 1, 3):
        two(0, 3, d).start()

    loop(REACH + 1, lambda d: second_copy(dstat, 1, d).wait_recv())
    bounds = [(own + f, clip_end(starts, own + f, frames)) for f in range(2)]
    backs = masked_rows(dstat, bounds)
    back_one, back_two = spread(backs, pltpu.roll(backs, 96, 1))
    for f in range(2):
        k = 2 + 2 * core + f
        values = xw[k].reshape(256, 256).astype(F32)
        result = (
            gwin[2 * core + f].reshape(256, 256).astype(F32)
            + da[f] * inv_rows[pl.ds(k, 1)]
            + back_one[f : f + 1]
            + values * (2.0 * back_two[f : f + 1])
        )
        grads_v[f] = result.reshape(16, 16, 256).astype(BF16)
    store_grads = pltpu.make_async_copy(grads_v, grads.at[0], store_sem.at[1])
    store_grads.start()

    for c in range(2):
        own_v[16 * c : 16 * c + 16] = every(total3, 128 * c + z, 16, 8)
    own_v[32:48] = every(turn, 128 + x, 16, 4)
    store_own = pltpu.make_async_copy(own_v, own3, store_sem.at[2])
    store_own.start()

    for kind, buffer in ((0, stat), (1, dstat)):
        first_copy(buffer, kind).wait_send()
        loop(REACH + 1, lambda d: second_copy(buffer, kind, d).wait_send())
    g_partner.wait_send()
    x_partner.wait_send()
    for f in range(2):
        pl.when(core == 0)(g_back[f].wait_send)
        pl.when(core == 1)(g_relay[f].wait_send)
    pl.when(core == 1)(x_ahead.wait_send)
    for d in (1, 2, 3):
        for i in PIECES:
            one_x(i, d).wait_send()
            one_y(i, d).wait_send()
        for c, kind in ((0, 0), (0, 1), (1, 0), (1, 1), (0, 2)):
            two(c, kind, d).wait_send()
    for i in Z_PIECES:
        loop(nz, lambda d: one_z(i, d).wait_send())
    loop(nz, lambda d: three(0, d).wait_send())

    store_out.wait()
    store_grads.wait()
    store_own.wait()
    for c in range(2):
        loop(nz, lambda d: three(c, d).wait_recv())
    for d in (1, 2, 3):
        two(0, 3, d).wait_recv()

    for d in (1, 2, 3):
        two(0, 3, d).wait_send()
    loop(nz, lambda d: three(1, d).wait_send())


def last_sum(scale, out, grads, own3, r3, rz3, *refs):
    out_to, grads_to, wgrads, out_v, grads_v, own_v, r3_v, rz3_v, w_v, sems = refs

    def copy(src, dst, k):
        return pltpu.make_async_copy(src, dst, sems.at[k])

    into = [
        copy(own3, own_v, 0),
        copy(r3, r3_v, 1),
        copy(rz3, rz3_v, 2),
        copy(out, out_v, 3),
        copy(grads, grads_v, 4),
    ]
    for part in into:
        part.start()
    into[3].wait()
    outward = [copy(out_v, out_to, 5)]
    outward[0].start()
    into[4].wait()
    outward.append(copy(grads_v, grads_to, 6))
    outward[1].start()
    for part in into[:3]:
        part.wait()
    total = own_v[0:32]
    for d in range(1, r3_v.shape[0]):
        total = total + r3_v[d].astype(F32)
    along_z = own_v[32:48]
    for d in range(1, rz3_v.shape[0]):
        along_z = along_z + rz3_v[d].astype(F32)
    places = [("z", k) for k in range(16)]
    for c, (low, count, first, length) in enumerate(HALVES):
        taps = [(axis, low + k) for axis in "xy" for k in range(length // 8)]
        places = places + taps + [None] * (16 - len(taps))
    rows = jnp.concatenate([along_z, total], axis=0) * scale
    for n in range(TAPS):
        k = places.index(place_of(n))
        to = 9 * (n % 3) + n // 3
        w_v[to] = rows[k : k + 1]
    outward.append(copy(w_v, wgrads, 7))
    outward[2].start()
    for part in outward:
        part.wait()


def local(nz, ny, scale, video_tile, clip_lengths, kernels, norm_gains, norm_shifts, cotangent):
    hbm = pl.BlockSpec(memory_space=pltpu.HBM)
    dma = pltpu.SemaphoreType.DMA
    made = pl.pallas_call(
        functools.partial(kernel, nz, ny),
        out_shape=(
            jax.ShapeDtypeStruct(video_tile.shape, BF16),
            jax.ShapeDtypeStruct(video_tile.shape, BF16),
            jax.ShapeDtypeStruct((48, 256), F32),
            jax.ShapeDtypeStruct((nz, 32, 256), BF16),
            jax.ShapeDtypeStruct((NX, 16, 256), BF16),
        ),
        in_specs=[hbm] * 6,
        out_specs=(hbm,) * 5,
        scratch_shapes=[
            pltpu.SMEM((1, 6), jnp.int32),
            pltpu.VMEM((1, 256), F32),
            pltpu.VMEM((1, 256), F32),
            pltpu.VMEM((6, 16, 16, 256), BF16),
            pltpu.VMEM((6, 16, 16, 256), BF16),
            pltpu.VMEM((3, 3, 3, 256, 256), BF16),
            pltpu.VMEM((6, 18, 16, 768), BF16),
            pltpu.VMEM((4, 18, 16, 768), BF16),
            pltpu.VMEM((6, 256, 256), BF16),
            pltpu.VMEM((384, 1536), BF16),
            pltpu.VMEM((nz * GROUP, 1, 128), F32),
            pltpu.VMEM((nz * GROUP, 1, 128), F32),
            pltpu.VMEM((8, 256), F32),
            pltpu.VMEM((8, 256), F32),
            pltpu.VMEM((8, 256), F32),
            pltpu.VMEM((2, 256, 256), F32),
            pltpu.VMEM((4, 11, 32, 256), BF16),
            pltpu.VMEM((4, 11, 32, 256), BF16),
            pltpu.VMEM((4, 11, 32, 256), BF16),
            pltpu.VMEM((4, 11, 32, 256), BF16),
            pltpu.VMEM((8, Z_TAPS, 16, 256), BF16),
            pltpu.VMEM((8, Z_TAPS, 16, 256), BF16),
            pltpu.VMEM((4, 96, 256), BF16),
            pltpu.VMEM((4, 96, 256), BF16),
            pltpu.VMEM((4, 96, 256), BF16),
            pltpu.VMEM((4, 96, 256), BF16),
            pltpu.VMEM((4, 32, 256), BF16),
            pltpu.VMEM((4, 32, 256), BF16),
            pltpu.VMEM((4, 16, 256), BF16),
            pltpu.VMEM((4, 96, 256), F32),
            pltpu.VMEM((4, 96, 256), F32),
            pltpu.VMEM((2, 128 * Z_TAPS, 128), F32),
            pltpu.VMEM((2, 256, 128), F32),
            pltpu.VMEM((8, 32, 256), BF16),
            pltpu.VMEM((48, 256), F32),
            pltpu.VMEM((2, 16, 16, 256), BF16),
            pltpu.VMEM((2, 16, 16, 256), BF16),
            dma((8,)),
            dma((5,)),
            dma((5,)),
            dma((2, REACH + 1)),
            dma((2, REACH + 1)),
            dma((2, 5, 4)),
            dma((2, 5, 4)),
            dma((4, 2, 4)),
            dma((4, 2, 4)),
            dma((4, 8)),
            dma((4, 8)),
            dma((3,)),
        ],
        compiler_params=pltpu.CompilerParams(
            collective_id=0, has_side_effects=True, vmem_limit_bytes=60 * 1024 * 1024
        ),
        cost_estimate=pl.CostEstimate(flops=5_500_000_000, bytes_accessed=5_000_000, transcendentals=400_000),
    )(clip_lengths, norm_gains, norm_shifts, video_tile, cotangent, kernels)
    results = pl.pallas_call(
        functools.partial(last_sum, scale),
        out_shape=(
            jax.ShapeDtypeStruct(video_tile.shape, BF16),
            jax.ShapeDtypeStruct(video_tile.shape, BF16),
            jax.ShapeDtypeStruct((TAPS, 1, 256), F32),
        ),
        in_specs=[hbm] * 5,
        out_specs=(hbm,) * 3,
        scratch_shapes=[pltpu.VMEM(part.shape, part.dtype) for part in made]
        + [pltpu.VMEM((TAPS, 1, 256), F32), dma((8,))],
        compiler_params=pltpu.CompilerParams(vmem_limit_bytes=60 * 1024 * 1024),
    )(*made)
    return (results[0], results[1], results[2].transpose(1, 0, 2))


def solution(mesh):
    ny, tm = mesh.shape["dp"], mesh.shape["tm"]
    nz = tm // GROUP
    scale = 1.0 / math.sqrt(ny * tm * 2 * 256)
    placed = P("dp", "tm", None, None, None)
    return jax.shard_map(
        functools.partial(local, nz, ny, scale),
        mesh=mesh,
        in_specs=(placed, P("dp", None), P(), P(), P(), placed),
        out_specs=(placed, placed, P(None, None, ("dp", "tm"))),
        check_vma=False,
    )
```

```python
import functools
import math

import jax
import jax.numpy as jnp
from jax import lax
from jax.experimental import pallas as pl
from jax.experimental.pallas import tpu as pltpu
from jax.sharding import PartitionSpec as P

EPS = 1e-05
NX = 4
NC = 2
GROUP = NX * NC
TAPS = 27
REACH = 12
MESH = pl.DeviceIdType.MESH
F32 = jnp.float32
BF16 = jnp.bfloat16
Z_TAPS = 5
Z_PIECES = {0: (0, 1), 2: (1, 2), 4: (3, 2)}
PIECES = {0: (0, 1), 2: (1, 2), 4: (3, 2), 6: (5, 3), 8: (8, 3)}
HALVES = ((0, 8, 0, 64), (8, 3, 64, 32))


def place_of(n):
    step, lag = n // 3, n % 3
    if step < Z_TAPS:
        return ("xyz"[lag], step)
    k = n - Z_TAPS
    return "xy"[k % 2], k // 2


def iota(shape, dim):
    return lax.broadcasted_iota(jnp.int32, shape, dim)


def clip_begin(starts, t):
    begin = jnp.int32(0)
    for start in starts:
        begin = jnp.where(start <= t, start, begin)
    return begin


def clip_end(starts, t, frames):
    end = jnp.int32(frames)
    for start in reversed(starts):
        end = jnp.where(start > t, start, end)
    return end


def flag(condition):
    return jnp.where(condition, jnp.float32(1.0), jnp.float32(0.0))


def dot(a, b, contract=(1, 0)):
    return lax.dot_general(
        a,
        b,
        (((contract[0],), (contract[1],)), ((), ())),
        preferred_element_type=F32,
    )


def sums_of(rows, matrix):
    high = rows.astype(BF16)
    rest = rows - high.astype(F32)
    middle = rest.astype(BF16)
    low = (rest - middle.astype(F32)).astype(BF16)
    n = rows.shape[0]
    parts = dot(jnp.concatenate([high, middle, low], axis=0), matrix.astype(BF16))
    return parts[:n] + (parts[n : 2 * n] + parts[2 * n :])


def sigmoid(z):
    return 0.5 * jnp.tanh(0.5 * z) + 0.5


def pack_rows(rows):
    place = iota((16, 256), 0)
    stacked = jnp.zeros((16, 256), F32)
    for k, row in enumerate(rows):
        stacked = jnp.where(place == k, row, stacked)
    gather = ((iota((256, 128), 0) >> 3) == (iota((256, 128), 1) & 31)).astype(F32)
    grouped = sums_of(stacked, gather)[:8]
    mine = (iota((8, 128), 1) >> 5) == iota((8, 128), 0)
    return jnp.sum(jnp.where(mine, grouped, 0.0), axis=0, keepdims=True)


def spread(*parts):
    rows = jnp.concatenate(parts, axis=0)
    clean = jnp.where(iota(rows.shape, 1) < 32, rows, 0.0)
    matrix = (iota((128, 256), 0) == (iota((128, 256), 1) >> 3)).astype(F32)
    wide = sums_of(clean, matrix)
    return [wide[8 * k : 8 * k + 8] for k in range(len(parts))]


def masked_rows(buffer, bounds):
    values = buffer[...]
    frame = 2 * iota(values.shape, 0) + (iota(values.shape, 2) >> 6)
    place = iota((8, 128), 0)
    rows = jnp.zeros((8, 128), F32)
    for k, (low, high) in enumerate(bounds):
        inside = (frame >= low) & (frame < high)
        total = jnp.sum(jnp.where(inside, values, 0.0), axis=0)
        rows = jnp.where(place == k, total, rows)
    return rows + pltpu.roll(rows, 64, 1)


def kernel(
    nz,
    ny,
    lens_hbm,
    gain_hbm,
    shift_hbm,
    video,
    cot,
    kern,
    out,
    grads,
    own3,
    r3,
    rz3,
    lens,
    gain,
    shift,
    xw,
    gwin,
    kv,
    gim,
    aim,
    act,
    lhs,
    stat,
    dstat,
    mean_rows,
    scale_rows,
    inv_rows,
    da,
    sx1,
    rx1,
    sy1,
    ry1,
    sz1,
    rz1,
    sx2,
    rx2,
    sy2,
    ry2,
    sz2,
    rz2,
    sz3,
    kx2,
    ky2,
    turn,
    total3,
    s3,
    own_v,
    out_v,
    grads_v,
    load_sem,
    halo_send,
    halo_recv,
    chain_send,
    chain_recv,
    one_send,
    one_recv,
    two_send,
    two_recv,
    three_send,
    three_recv,
    store_sem,
):
    y = lax.axis_index("dp")
    tm = lax.axis_index("tm")
    core = lax.rem(tm, NC)
    x = lax.rem(tm // NC, NX)
    z = tm // GROUP
    within = lax.rem(tm, GROUP)
    chip = tm // NC
    chips = nz * NX
    frames = 2 * nz * GROUP
    base = 4 * chip
    own = 2 * tm

    def at(tm_index, dp_index=None):
        return {"dp": y if dp_index is None else dp_index, "tm": tm_index}

    def x_peer(d):
        return z * GROUP + lax.rem(x + d, NX) * NC + core

    def z_peer(d):
        return lax.rem(z + d, nz) * GROUP + within

    def y_peer(d):
        return lax.rem(y + d, ny)

    def chip_peer(d):
        return lax.rem(chip + d, chips) * NC + core

    partner = chip * NC + 1 - core

    beside = lax.rem(tm + 2 * core - 1 + 2 * chips, 2 * chips)

    stat[...] = jnp.zeros(stat.shape, F32)
    dstat[...] = jnp.zeros(dstat.shape, F32)

    load_x = pltpu.make_async_copy(video.at[0], xw.at[pl.ds(2 + 2 * core, 2)], load_sem.at[0])
    load_g = pltpu.make_async_copy(cot.at[0], gwin.at[pl.ds(2 * core, 2)], load_sem.at[1])
    load_k = [
        pltpu.make_async_copy(kern.at[0, lag], kv.at[lag], load_sem.at[2 + lag]) for lag in range(3)
    ]
    load_small = [
        pltpu.make_async_copy(src, dst, load_sem.at[5 + k])
        for k, (src, dst) in enumerate(((lens_hbm, lens), (gain_hbm, gain), (shift_hbm, shift)))
    ]
    load_x.start()

    barrier = pltpu.get_barrier_semaphore()

    def greet(device):
        pl.semaphore_signal(barrier, inc=1, device_id=device, device_id_type=MESH)

    def greet_before(d, carry):
        greet(at(chip_peer(chips - REACH + d)))
        return carry

    greet(at(partner))
    greet(at(beside))
    lax.fori_loop(0, REACH, greet_before, 0)
    far = range(REACH // NX + 1, nz - REACH // NX)
    for d in range(1, ny):
        greet(at(tm, y_peer(d)))
    for d in far:
        greet(at(z_peer(d)))
    load_g.start()
    for copy in load_small:
        copy.start()
    for copy in load_k:
        copy.start()

    for copy in load_small:
        copy.wait()
    starts = []
    begin = jnp.int32(0)
    for k in range(6):
        starts.append(begin)
        begin = begin + lens[0, k]

    load_x.wait()
    sums = []
    for f in range(2):
        values = xw[2 + 2 * core + f].reshape(256, 256).astype(F32)
        sums.append(jnp.sum(values, axis=0, keepdims=True))
        sums.append(jnp.sum(values * values, axis=0, keepdims=True))
    stat[pl.ds(tm, 1)] = pack_rows(sums).reshape(1, 1, 128)

    pl.semaphore_wait(barrier, REACH + len(far) + (ny - 1) + 2)

    def first_copy(buffer, kind):
        mine = buffer.at[pl.ds(tm, 1)]
        return pltpu.make_async_remote_copy(
            src_ref=mine,
            dst_ref=mine,
            send_sem=chain_send.at[kind, 0],
            recv_sem=chain_recv.at[kind, 0],
            device_id=at(partner),
            device_id_type=MESH,
        )

    def second_copy(buffer, kind, d):
        mine = buffer.at[pl.ds(NC * chip, NC)]
        step = d if kind == 0 else chips - d
        return pltpu.make_async_remote_copy(
            src_ref=mine,
            dst_ref=mine,
            send_sem=chain_send.at[kind, d],
            recv_sem=chain_recv.at[kind, d],
            device_id=at(chip_peer(step)),
            device_id_type=MESH,
        )

    def loop(count, act_on):
        def body(d, carry):
            act_on(d)
            return carry

        lax.fori_loop(1, count, body, 0)

    first_copy(stat, 0).start()

    def halo(src, dst, sent, received, device):
        return pltpu.make_async_remote_copy(
            src_ref=src,
            dst_ref=dst,
            send_sem=halo_send.at[sent],
            recv_sem=halo_recv.at[received],
            device_id=at(device),
            device_id_type=MESH,
        )

    own_g = gwin.at[pl.ds(2 * core, 2)]
    own_x = xw.at[pl.ds(2 + 2 * core, 2)]
    g_partner = halo(cot.at[0], own_g, 0, 0, partner)
    x_partner = halo(video.at[0], own_x, 1, 1, partner)
    g_back = [halo(cot.at[0, f], gwin.at[4 + f], 2 + f, 2 + f, beside) for f in range(2)]
    g_relay = [halo(gwin.at[4 + f], gwin.at[4 + f], 2 + f, 2 + f, partner) for f in range(2)]
    x_ahead = halo(video.at[0], xw.at[pl.ds(0, 2)], 4, 4, beside)
    g_partner.start()
    x_partner.start()

    @pl.when(core == 0)
    def _():
        g_back[0].start()
        g_back[1].start()


    pixel, source = iota((256, 256), 0), iota((256, 256), 1)
    right = ((source == pixel + 1) & ((pixel & 15) != 15)).astype(BF16)
    left = ((source == pixel - 1) & ((pixel & 15) != 0)).astype(BF16)
    both = jnp.concatenate([right, left], axis=0)

    def widen(target, k, values, first, last):
        shifted = dot(both, values).astype(BF16)
        target[k, 1:17, :, 256 * first : 256 * first + 256] = shifted[:256].reshape(16, 16, 256)
        target[k, 1:17, :, 256:512] = values.reshape(16, 16, 256)
        target[k, 1:17, :, 256 * last : 256 * last + 256] = shifted[256:].reshape(16, 16, 256)
        target[k, 0:1] = jnp.zeros((1, 16, 768), BF16)
        target[k, 17:18] = jnp.zeros((1, 16, 768), BF16)

    def backward(lag):
        taken = jnp.concatenate(
            [
                gim[pl.ds(2 * core + lag, 2), 2 - i : 18 - i].reshape(512, 768)
                for i in range(3)
            ],
            axis=1,
        )
        weights = jnp.concatenate(
            [kv[lag, i, j] for i in range(3) for j in range(3)], axis=1
        )
        part = dot(taken, weights, (1, 1))
        for f in range(2):
            piece = part[256 * f : 256 * f + 256]
            if lag == 0:
                da[f] = piece
            else:
                keep = flag(own + f + lag < clip_end(starts, own + f, frames))
                da[f] = da[f] + keep * piece

    def widen_g(v, carry):
        widen(gim, v, gwin[v].reshape(256, 256), 0, 2)
        return carry

    load_g.wait()
    lax.fori_loop(0, 2, lambda v, carry: widen_g(2 * core + v, carry), 0)

    first_copy(stat, 0).wait_recv()
    loop(REACH + 1, lambda d: second_copy(stat, 0, REACH + 1 - d).start())

    load_k[0].wait()
    backward(0)
    g_partner.wait_recv()
    lax.fori_loop(0, 2, lambda v, carry: widen_g(2 - 2 * core + v, carry), 0)

    bounds, counted = [], jnp.zeros((8, 128), F32)
    for k in range(6):
        t = base - 2 + k
        b = clip_begin(starts, t)
        bounds.append((b, t + 1))
        count = jnp.maximum(t + 1 - b, 1).astype(F32)
        counted = jnp.where(iota((8, 128), 0) == k, count, counted)
    counted = jnp.maximum(counted, 1.0) * 2048.0
    row, channel = iota((128, 256), 0), iota((128, 256), 1)
    wanted = 64 * ((row >> 3) & 3) + 8 * (row & 7) + 2 * (row >> 5) + core
    select = (channel == wanted).astype(BF16)
    blank = jnp.zeros((128, 256), BF16)
    for lag, v in ((0, 4), (0, 5), (1, 0), (1, 5), (2, 0), (2, 1)):
        lhs[128 * lag : 128 * lag + 128, 256 * v : 256 * v + 256] = blank

    loop(REACH + 1, lambda d: second_copy(stat, 0, d).wait_recv())

    @pl.when(core == 1)
    def _():
        x_ahead.start()

    averaged = masked_rows(stat, bounds) / counted
    squares = pltpu.roll(averaged, 96, 1)
    inv_std = lax.rsqrt(squares - averaged * averaged + EPS)
    wide_mean, wide_inv = spread(averaged, inv_std)
    mean_rows[...] = wide_mean
    inv_rows[...] = wide_inv
    scale_rows[...] = wide_inv * gain[...]

    def activate(k, carry):
        values = xw[k].reshape(256, 256).astype(F32)
        normed = (values - mean_rows[pl.ds(k, 1)]) * scale_rows[pl.ds(k, 1)] + shift[...]
        act[k] = (normed * sigmoid(normed)).astype(BF16)
        return carry

    x_partner.wait_recv()

    for u in range(4):
        activate(2 + u, 0)
        turned = dot(select, act[2 + u], (1, 1))
        end = clip_end(starts, base + u, frames)
        for lag in range(3):
            masked = turned if lag == 0 else turned * flag(base + u + lag < end)
            v = u + lag
            lhs[128 * lag : 128 * lag + 128, 256 * v : 256 * v + 256] = masked.astype(BF16)

    for f in range(2):

        @pl.when(core == 1)
        def _():
            g_back[f].wait_recv()
            g_relay[f].start()

        @pl.when(core == 0)
        def _():
            g_relay[f].wait_recv()

        widen_g(4 + f, 0)

    def one_x(i, d):
        low, count = PIECES[i]
        target = lax.rem(x + d, NX)
        return pltpu.make_async_remote_copy(
            src_ref=sx1.at[target, pl.ds(low, count)],
            dst_ref=rx1.at[d, pl.ds(low, count)],
            send_sem=one_send.at[0, i // 2, d],
            recv_sem=one_recv.at[0, i // 2, d],
            device_id=at(x_peer(d)),
            device_id_type=MESH,
        )

    def one_y(i, d):
        low, count = PIECES[i]
        target = lax.rem(y + d, ny)
        return pltpu.make_async_remote_copy(
            src_ref=sy1.at[target, pl.ds(low, count)],
            dst_ref=ry1.at[d, pl.ds(low, count)],
            send_sem=one_send.at[1, i // 2, d],
            recv_sem=one_recv.at[1, i // 2, d],
            device_id=at(tm, y_peer(d)),
            device_id_type=MESH,
        )

    def one_z(i, d):
        low, count = Z_PIECES[i]
        return pltpu.make_async_remote_copy(
            src_ref=sz1.at[lax.rem(z + d, nz), pl.ds(low, count)],
            dst_ref=rz1.at[d, pl.ds(low, count)],
            send_sem=three_send.at[2 + i // 2, d],
            recv_sem=three_recv.at[2 + i // 2, d],
            device_id=at(z_peer(d)),
            device_id_type=MESH,
        )

    def put_total(buffer, first, rows):
        for h in range(2):
            buffer[h, first : first + rows.shape[0]] = rows[:, 128 * h : 128 * h + 128]

    def every(buffer, start, count, stride):
        rows = [buffer[h, pl.ds(start, count, stride=stride)] for h in range(2)]
        return jnp.concatenate(rows, axis=1)

    for step in range(9):
        i, j = step // 3, step % 3
        terms = dot(lhs[...], gim[:, 2 - i : 18 - i, :, 256 * j : 256 * j + 256].reshape(1536, 256))
        for lag in range(3):
            axis, slot = place_of(3 * step + lag)
            block = terms[128 * lag : 128 * lag + 128]
            if axis == "z":
                put_total(turn, 128 * slot, block)
                for q in range(nz):
                    sz1[q, slot] = every(turn, 128 * slot + q, 16, 8).astype(BF16)
                continue
            for p in range(4):
                if axis == "x":
                    sx1[p, slot] = block[32 * p : 32 * p + 32].astype(BF16)
                else:
                    rows = [block[32 * q + 8 * p : 32 * q + 8 * p + 8] for q in range(4)]
                    sy1[p, slot] = jnp.concatenate(rows, axis=0).astype(BF16)
        if step in Z_PIECES:
            loop(nz, lambda d: one_z(step, d).start())
        if step in PIECES:
            for d in (2, 1, 3):
                one_x(step, d).start()
                one_y(step, d).start()

    for lag in (1, 2):
        load_k[lag].wait()
        backward(lag)

    lanes = iota((1, 128), 1)
    sums = []
    for f in range(2):
        k = 2 + 2 * core + f
        centred = xw[k].reshape(256, 256).astype(F32) - mean_rows[pl.ds(k, 1)]
        normed = centred * scale_rows[pl.ds(k, 1)] + shift[...]
        sig = sigmoid(normed)
        du = da[f] * (sig * (1.0 + normed * (1.0 - sig))) * gain[...]
        da[f] = du
        sums.append(jnp.sum(du, axis=0, keepdims=True))
        sums.append(jnp.sum(du * centred, axis=0, keepdims=True))
    packed = pack_rows(sums)
    row_of = iota((8, 128), 0)

    def pick(rows, k):
        return jnp.sum(jnp.where(row_of == k, rows, 0.0), axis=0, keepdims=True)

    answer = jnp.zeros((1, 128), F32)
    for f in range(2):
        k = 2 + 2 * core + f
        mean_k, inv_k, n_k = pick(averaged, k), pick(inv_std, k), pick(counted, k)
        sum_du = pltpu.roll(packed, 64, 1) if f else packed
        dr = pltpu.roll(sum_du, 96, 1)
        cubed = inv_k * inv_k * inv_k
        dc1 = (dr * cubed * mean_k - inv_k * sum_du) / n_k
        dc2 = -0.5 * dr * cubed / n_k
        dc2 = pltpu.roll(dc2, 32, 1)
        pair = jnp.where(lanes < 32, dc1, jnp.where(lanes < 64, dc2, 0.0))
        answer = answer + (pltpu.roll(pair, 64, 1) if f else pair)
    dstat[pl.ds(tm, 1)] = answer.reshape(1, 1, 128)
    first_copy(dstat, 1).start()

    @pl.when(core == 0)
    def _():
        x_ahead.wait_recv()
        lax.fori_loop(0, 2, activate, 0)

    def widen_a(k, carry):
        widen(aim, k, act[2 * core + k], 2, 0)
        return carry

    lax.fori_loop(0, 4, widen_a, 0)
    for lag in range(3):
        taken = jnp.concatenate(
            [aim[2 - lag : 4 - lag, i : i + 16].reshape(512, 768) for i in range(3)], axis=1
        )
        part = dot(taken, kv[lag].reshape(2304, 256))
        for f in range(2):
            piece = part[256 * f : 256 * f + 256]
            if lag == 0:
                total = xw[2 + 2 * core + f].reshape(256, 256).astype(F32) + piece
            else:
                keep = flag(own + f - lag >= clip_begin(starts, own + f))
                total = total_f[f] + keep * piece
            if f == 0:
                first = total
            else:
                total_f = [first, total]
    for f in range(2):
        out_v[f] = total_f[f].reshape(16, 16, 256).astype(BF16)
    store_out = pltpu.make_async_copy(out_v, out.at[0], store_sem.at[0])
    store_out.start()

    def two(c, kind, d):
        mine, got = ((sx2, rx2), (sy2, ry2), (sz2, rz2), (sz3, rz3))[kind]
        along_y = kind in (0, 2)
        target = lax.rem(y + d, ny) if along_y else lax.rem(x + d, NX)
        src, dst = mine.at[target], got.at[d]
        if kind < 2:
            some = pl.ds(HALVES[c][2], HALVES[c][3])
            src, dst = src.at[some], dst.at[some]
        return pltpu.make_async_remote_copy(
            src_ref=src,
            dst_ref=dst,
            send_sem=two_send.at[kind, c, d],
            recv_sem=two_recv.at[kind, c, d],
            device_id=at(tm, y_peer(d)) if along_y else at(x_peer(d)),
            device_id_type=MESH,
        )

    def three(c, d):
        return pltpu.make_async_remote_copy(
            src_ref=s3.at[lax.rem(z + d, nz), pl.ds(16 * c, 16)],
            dst_ref=r3.at[d, pl.ds(16 * c, 16)],
            send_sem=three_send.at[c, d],
            recv_sem=three_recv.at[c, d],
            device_id=at(z_peer(d)),
            device_id_type=MESH,
        )

    total3[...] = jnp.zeros(total3.shape, F32)

    def gathered(c, mine, got, keep, staged, me):
        low, count, first, length = HALVES[c]
        for both_p in range(2):
            some = pl.ds(16 * both_p, 16)
            half = mine[me, pl.ds(low, count), some].astype(F32)
            for d in range(1, 4):
                half = half + got[d, pl.ds(low, count), some].astype(F32)
            for p in (2 * both_p, 2 * both_p + 1):
                piece = half[:, 8 * (p % 2) : 8 * (p % 2) + 8].reshape(8 * count, 256)
                if 8 * count < length:
                    blank = jnp.zeros((length - 8 * count, 256), F32)
                    piece = jnp.concatenate([piece, blank], axis=0)
                keep[p, first : first + length] = piece
                staged[p, first : first + length] = piece.astype(BF16)

    def to_two(c):
        pieces = (0, 2, 4, 6) if c == 0 else (8,)
        for kind, one, mine, got, keep, staged, me in (
            (0, one_x, sx1, rx1, kx2, sx2, x),
            (1, one_y, sy1, ry1, ky2, sy2, y),
        ):
            for i in pieces:
                for d in range(1, 4):
                    one(i, d).wait_recv()
            gathered(c, mine, got, keep, staged, me)
            for d in (2, 1, 3):
                two(c, kind, d).start()

    def to_three(c):
        low, count, first, length = HALVES[c]
        some = pl.ds(first, length)
        for kind, keep, got, me in ((0, kx2, rx2, y), (1, ky2, ry2, x)):
            for d in range(1, 4):
                two(c, kind, d).wait_recv()
            total = keep[me, some]
            for d in range(1, 4):
                total = total + got[d, some].astype(F32)
            put_total(total3, 128 * c + length * kind, total)
        for q in range(nz):
            s3[q, 16 * c : 16 * c + 16] = every(total3, 128 * c + q, 16, 8).astype(BF16)
        for d in sorted(range(1, nz), key=lambda d: -min(d, nz - d)):
            three(c, d).start()

    to_two(0)
    to_two(1)

    for i in Z_PIECES:
        loop(nz, lambda d: one_z(i, d).wait_recv())
    total = sz1[z].astype(F32)
    for d in range(1, nz):
        total = total + rz1[d].astype(F32)
    put_total(turn, 0, total.reshape(16 * Z_TAPS, 256))
    for p in range(4):
        sz2[p] = every(turn, p, 32, 4).astype(BF16)
    for d in (2, 1, 3):
        two(0, 2, d).start()

    first_copy(dstat, 1).wait_recv()
    loop(REACH + 1, lambda d: second_copy(dstat, 1, d).start())
    to_three(0)
    to_three(1)

    for d in (1, 2, 3):
        two(0, 2, d).wait_recv()
    total = every(turn, y, 32, 4)
    for d in range(1, 4):
        total = total + rz2[d].astype(F32)
    put_total(turn, 128, total)
    for p in range(4):
        sz3[p] = every(turn, 128 + p, 16, 4).astype(BF16)
    for d in (2, 1, 3):
        two(0, 3, d).start()

    loop(REACH + 1, lambda d: second_copy(dstat, 1, d).wait_recv())
    bounds = [(own + f, clip_end(starts, own + f, frames)) for f in range(2)]
    backs = masked_rows(dstat, bounds)
    back_one, back_two = spread(backs, pltpu.roll(backs, 96, 1))
    for f in range(2):
        k = 2 + 2 * core + f
        values = xw[k].reshape(256, 256).astype(F32)
        result = (
            gwin[2 * core + f].reshape(256, 256).astype(F32)
            + da[f] * inv_rows[pl.ds(k, 1)]
            + back_one[f : f + 1]
            + values * (2.0 * back_two[f : f + 1])
        )
        grads_v[f] = result.reshape(16, 16, 256).astype(BF16)
    store_grads = pltpu.make_async_copy(grads_v, grads.at[0], store_sem.at[1])
    store_grads.start()

    for c in range(2):
        own_v[16 * c : 16 * c + 16] = every(total3, 128 * c + z, 16, 8)
    own_v[32:48] = every(turn, 128 + x, 16, 4)
    store_own = pltpu.make_async_copy(own_v, own3, store_sem.at[2])
    store_own.start()

    for kind, buffer in ((0, stat), (1, dstat)):
        first_copy(buffer, kind).wait_send()
        loop(REACH + 1, lambda d: second_copy(buffer, kind, d).wait_send())
    g_partner.wait_send()
    x_partner.wait_send()
    for f in range(2):
        pl.when(core == 0)(g_back[f].wait_send)
        pl.when(core == 1)(g_relay[f].wait_send)
    pl.when(core == 1)(x_ahead.wait_send)
    for d in (1, 2, 3):
        for i in PIECES:
            one_x(i, d).wait_send()
            one_y(i, d).wait_send()
        for c, kind in ((0, 0), (0, 1), (1, 0), (1, 1), (0, 2)):
            two(c, kind, d).wait_send()
    for i in Z_PIECES:
        loop(nz, lambda d: one_z(i, d).wait_send())
    loop(nz, lambda d: three(0, d).wait_send())

    store_out.wait()
    store_grads.wait()
    store_own.wait()
    for c in range(2):
        loop(nz, lambda d: three(c, d).wait_recv())
    for d in (1, 2, 3):
        two(0, 3, d).wait_recv()

    for d in (1, 2, 3):
        two(0, 3, d).wait_send()
    loop(nz, lambda d: three(1, d).wait_send())


def last_sum(scale, out, grads, own3, r3, rz3, *refs):
    out_to, grads_to, wgrads, out_v, grads_v, own_v, r3_v, rz3_v, w_v, sems = refs

    def copy(src, dst, k):
        return pltpu.make_async_copy(src, dst, sems.at[k])

    into = [
        copy(own3, own_v, 0),
        copy(r3, r3_v, 1),
        copy(rz3, rz3_v, 2),
        copy(out, out_v, 3),
        copy(grads, grads_v, 4),
    ]
    for part in into:
        part.start()
    into[3].wait()
    outward = [copy(out_v, out_to, 5)]
    outward[0].start()
    into[4].wait()
    outward.append(copy(grads_v, grads_to, 6))
    outward[1].start()
    for part in into[:3]:
        part.wait()
    total = own_v[0:32]
    for d in range(1, r3_v.shape[0]):
        total = total + r3_v[d].astype(F32)
    along_z = own_v[32:48]
    for d in range(1, rz3_v.shape[0]):
        along_z = along_z + rz3_v[d].astype(F32)
    places = [("z", k) for k in range(16)]
    for c, (low, count, first, length) in enumerate(HALVES):
        taps = [(axis, low + k) for axis in "xy" for k in range(length // 8)]
        places = places + taps + [None] * (16 - len(taps))
    rows = jnp.concatenate([along_z, total], axis=0) * scale
    for n in range(TAPS):
        k = places.index(place_of(n))
        to = 9 * (n % 3) + n // 3
        w_v[to] = rows[k : k + 1]
    outward.append(copy(w_v, wgrads, 7))
    outward[2].start()
    for part in outward:
        part.wait()


def local(nz, ny, scale, video_tile, clip_lengths, kernels, norm_gains, norm_shifts, cotangent):
    hbm = pl.BlockSpec(memory_space=pltpu.HBM)
    dma = pltpu.SemaphoreType.DMA
    made = pl.pallas_call(
        functools.partial(kernel, nz, ny),
        out_shape=(
            jax.ShapeDtypeStruct(video_tile.shape, BF16),
            jax.ShapeDtypeStruct(video_tile.shape, BF16),
            jax.ShapeDtypeStruct((48, 256), F32),
            jax.ShapeDtypeStruct((nz, 32, 256), BF16),
            jax.ShapeDtypeStruct((NX, 16, 256), BF16),
        ),
        in_specs=[hbm] * 6,
        out_specs=(hbm,) * 5,
        scratch_shapes=[
            pltpu.SMEM((1, 6), jnp.int32),
            pltpu.VMEM((1, 256), F32),
            pltpu.VMEM((1, 256), F32),
            pltpu.VMEM((6, 16, 16, 256), BF16),
            pltpu.VMEM((6, 16, 16, 256), BF16),
            pltpu.VMEM((3, 3, 3, 256, 256), BF16),
            pltpu.VMEM((6, 18, 16, 768), BF16),
            pltpu.VMEM((4, 18, 16, 768), BF16),
            pltpu.VMEM((6, 256, 256), BF16),
            pltpu.VMEM((384, 1536), BF16),
            pltpu.VMEM((nz * GROUP, 1, 128), F32),
            pltpu.VMEM((nz * GROUP, 1, 128), F32),
            pltpu.VMEM((8, 256), F32),
            pltpu.VMEM((8, 256), F32),
            pltpu.VMEM((8, 256), F32),
            pltpu.VMEM((2, 256, 256), F32),
            pltpu.VMEM((4, 11, 32, 256), BF16),
            pltpu.VMEM((4, 11, 32, 256), BF16),
            pltpu.VMEM((4, 11, 32, 256), BF16),
            pltpu.VMEM((4, 11, 32, 256), BF16),
            pltpu.VMEM((8, Z_TAPS, 16, 256), BF16),
            pltpu.VMEM((8, Z_TAPS, 16, 256), BF16),
            pltpu.VMEM((4, 96, 256), BF16),
            pltpu.VMEM((4, 96, 256), BF16),
            pltpu.VMEM((4, 96, 256), BF16),
            pltpu.VMEM((4, 96, 256), BF16),
            pltpu.VMEM((4, 32, 256), BF16),
            pltpu.VMEM((4, 32, 256), BF16),
            pltpu.VMEM((4, 16, 256), BF16),
            pltpu.VMEM((4, 96, 256), F32),
            pltpu.VMEM((4, 96, 256), F32),
            pltpu.VMEM((2, 128 * Z_TAPS, 128), F32),
            pltpu.VMEM((2, 256, 128), F32),
            pltpu.VMEM((8, 32, 256), BF16),
            pltpu.VMEM((48, 256), F32),
            pltpu.VMEM((2, 16, 16, 256), BF16),
            pltpu.VMEM((2, 16, 16, 256), BF16),
            dma((8,)),
            dma((5,)),
            dma((5,)),
            dma((2, REACH + 1)),
            dma((2, REACH + 1)),
            dma((2, 5, 4)),
            dma((2, 5, 4)),
            dma((4, 2, 4)),
            dma((4, 2, 4)),
            dma((5, 8)),
            dma((5, 8)),
            dma((3,)),
        ],
        compiler_params=pltpu.CompilerParams(
            collective_id=0, has_side_effects=True, vmem_limit_bytes=60 * 1024 * 1024
        ),
        cost_estimate=pl.CostEstimate(flops=5_500_000_000, bytes_accessed=5_000_000, transcendentals=400_000),
    )(clip_lengths, norm_gains, norm_shifts, video_tile, cotangent, kernels)
    results = pl.pallas_call(
        functools.partial(last_sum, scale),
        out_shape=(
            jax.ShapeDtypeStruct(video_tile.shape, BF16),
            jax.ShapeDtypeStruct(video_tile.shape, BF16),
            jax.ShapeDtypeStruct((TAPS, 1, 256), F32),
        ),
        in_specs=[hbm] * 5,
        out_specs=(hbm,) * 3,
        scratch_shapes=[pltpu.VMEM(part.shape, part.dtype) for part in made]
        + [pltpu.VMEM((TAPS, 1, 256), F32), dma((8,))],
        compiler_params=pltpu.CompilerParams(vmem_limit_bytes=60 * 1024 * 1024),
    )(*made)
    return (results[0], results[1], results[2].transpose(1, 0, 2))


def solution(mesh):
    ny, tm = mesh.shape["dp"], mesh.shape["tm"]
    nz = tm // GROUP
    scale = 1.0 / math.sqrt(ny * tm * 2 * 256)
    placed = P("dp", "tm", None, None, None)
    return jax.shard_map(
        functools.partial(local, nz, ny, scale),
        mesh=mesh,
        in_specs=(placed, P("dp", None), P(), P(), P(), placed),
        out_specs=(placed, placed, P(None, None, ("dp", "tm"))),
        check_vma=False,
    )
```

```python
import functools
import math

import jax
import jax.numpy as jnp
from jax import lax
from jax.experimental import pallas as pl
from jax.experimental.pallas import tpu as pltpu
from jax.sharding import PartitionSpec as P

EPS = 1e-05
NX = 4
NC = 2
GROUP = NX * NC
TAPS = 27
REACH = 12
MESH = pl.DeviceIdType.MESH
F32 = jnp.float32
BF16 = jnp.bfloat16
Z_TAPS = 5
Z_PIECES = {0: (0, 1), 2: (1, 2), 4: (3, 2)}
PIECES = {0: (0, 1), 2: (1, 2), 4: (3, 2), 6: (5, 3), 8: (8, 3)}
HALVES = ((0, 8, 0, 64), (8, 3, 64, 32))


def place_of(n):
    step, lag = n // 3, n % 3
    if step < Z_TAPS:
        return ("xyz"[lag], step)
    k = n - Z_TAPS
    return "xy"[k % 2], k // 2


def iota(shape, dim):
    return lax.broadcasted_iota(jnp.int32, shape, dim)


def clip_begin(starts, t):
    begin = jnp.int32(0)
    for start in starts:
        begin = jnp.where(start <= t, start, begin)
    return begin


def clip_end(starts, t, frames):
    end = jnp.int32(frames)
    for start in reversed(starts):
        end = jnp.where(start > t, start, end)
    return end


def flag(condition):
    return jnp.where(condition, jnp.float32(1.0), jnp.float32(0.0))


def dot(a, b, contract=(1, 0)):
    return lax.dot_general(
        a,
        b,
        (((contract[0],), (contract[1],)), ((), ())),
        preferred_element_type=F32,
    )


def sums_of(rows, matrix):
    high = rows.astype(BF16)
    rest = rows - high.astype(F32)
    middle = rest.astype(BF16)
    low = (rest - middle.astype(F32)).astype(BF16)
    n = rows.shape[0]
    parts = dot(jnp.concatenate([high, middle, low], axis=0), matrix.astype(BF16))
    return parts[:n] + (parts[n : 2 * n] + parts[2 * n :])


def sigmoid(z):
    return 0.5 * jnp.tanh(0.5 * z) + 0.5


def pack_rows(rows):
    place = iota((16, 256), 0)
    stacked = jnp.zeros((16, 256), F32)
    for k, row in enumerate(rows):
        stacked = jnp.where(place == k, row, stacked)
    gather = ((iota((256, 128), 0) >> 3) == (iota((256, 128), 1) & 31)).astype(F32)
    grouped = sums_of(stacked, gather)[:8]
    mine = (iota((8, 128), 1) >> 5) == iota((8, 128), 0)
    return jnp.sum(jnp.where(mine, grouped, 0.0), axis=0, keepdims=True)


def spread(*parts):
    rows = jnp.concatenate(parts, axis=0)
    clean = jnp.where(iota(rows.shape, 1) < 32, rows, 0.0)
    matrix = (iota((128, 256), 0) == (iota((128, 256), 1) >> 3)).astype(F32)
    wide = sums_of(clean, matrix)
    return [wide[8 * k : 8 * k + 8] for k in range(len(parts))]


def masked_rows(buffer, bounds):
    values = buffer[...]
    frame = 2 * iota(values.shape, 0) + (iota(values.shape, 2) >> 6)
    place = iota((8, 128), 0)
    rows = jnp.zeros((8, 128), F32)
    for k, (low, high) in enumerate(bounds):
        inside = (frame >= low) & (frame < high)
        total = jnp.sum(jnp.where(inside, values, 0.0), axis=0)
        rows = jnp.where(place == k, total, rows)
    return rows + pltpu.roll(rows, 64, 1)


def kernel(
    nz,
    ny,
    lens_hbm,
    gain_hbm,
    shift_hbm,
    video,
    cot,
    kern,
    out,
    grads,
    own3,
    r3,
    rz3,
    lens,
    gain,
    shift,
    xw,
    gwin,
    kv,
    gim,
    aim,
    act,
    lhs,
    stat,
    dstat,
    mean_rows,
    scale_rows,
    inv_rows,
    da,
    sx1,
    rx1,
    sy1,
    ry1,
    sz1,
    rz1,
    sx2,
    rx2,
    sy2,
    ry2,
    sz2,
    rz2,
    sz3,
    kx2,
    ky2,
    turn,
    total3,
    s3,
    own_v,
    out_v,
    grads_v,
    load_sem,
    halo_send,
    halo_recv,
    chain_send,
    chain_recv,
    one_send,
    one_recv,
    two_send,
    two_recv,
    three_send,
    three_recv,
    store_sem,
):
    y = lax.axis_index("dp")
    tm = lax.axis_index("tm")
    core = lax.rem(tm, NC)
    x = lax.rem(tm // NC, NX)
    z = tm // GROUP
    within = lax.rem(tm, GROUP)
    chip = tm // NC
    chips = nz * NX
    frames = 2 * nz * GROUP
    base = 4 * chip
    own = 2 * tm

    def at(tm_index, dp_index=None):
        return {"dp": y if dp_index is None else dp_index, "tm": tm_index}

    def x_peer(d):
        return z * GROUP + lax.rem(x + d, NX) * NC + core

    def z_peer(d):
        return lax.rem(z + d, nz) * GROUP + within

    def y_peer(d):
        return lax.rem(y + d, ny)

    def chip_peer(d):
        return lax.rem(chip + d, chips) * NC + core

    partner = chip * NC + 1 - core

    beside = lax.rem(tm + 2 * core - 1 + 2 * chips, 2 * chips)

    stat[...] = jnp.zeros(stat.shape, F32)
    dstat[...] = jnp.zeros(dstat.shape, F32)

    load_x = pltpu.make_async_copy(video.at[0], xw.at[pl.ds(2 + 2 * core, 2)], load_sem.at[0])
    load_g = pltpu.make_async_copy(cot.at[0], gwin.at[pl.ds(2 * core, 2)], load_sem.at[1])
    load_k = [
        pltpu.make_async_copy(kern.at[0, lag], kv.at[lag], load_sem.at[2 + lag]) for lag in range(3)
    ]
    load_small = [
        pltpu.make_async_copy(src, dst, load_sem.at[5 + k])
        for k, (src, dst) in enumerate(((lens_hbm, lens), (gain_hbm, gain), (shift_hbm, shift)))
    ]
    load_x.start()

    barrier = pltpu.get_barrier_semaphore()

    def greet(device):
        pl.semaphore_signal(barrier, inc=1, device_id=device, device_id_type=MESH)

    def greet_before(d, carry):
        greet(at(chip_peer(chips - REACH + d)))
        return carry

    greet(at(partner))
    greet(at(beside))
    lax.fori_loop(0, REACH, greet_before, 0)
    far = range(REACH // NX + 1, nz - REACH // NX)
    for d in range(1, ny):
        greet(at(tm, y_peer(d)))
    for d in far:
        greet(at(z_peer(d)))
    load_g.start()
    for copy in load_small:
        copy.start()
    for copy in load_k:
        copy.start()

    for copy in load_small:
        copy.wait()
    starts = []
    begin = jnp.int32(0)
    for k in range(6):
        starts.append(begin)
        begin = begin + lens[0, k]

    load_x.wait()
    sums = []
    for f in range(2):
        values = xw[2 + 2 * core + f].reshape(256, 256).astype(F32)
        sums.append(jnp.sum(values, axis=0, keepdims=True))
        sums.append(jnp.sum(values * values, axis=0, keepdims=True))
    stat[pl.ds(tm, 1)] = pack_rows(sums).reshape(1, 1, 128)

    pl.semaphore_wait(barrier, REACH + len(far) + (ny - 1) + 2)

    def first_copy(buffer, kind):
        mine = buffer.at[pl.ds(tm, 1)]
        return pltpu.make_async_remote_copy(
            src_ref=mine,
            dst_ref=mine,
            send_sem=chain_send.at[kind, 0],
            recv_sem=chain_recv.at[kind, 0],
            device_id=at(partner),
            device_id_type=MESH,
        )

    def second_copy(buffer, kind, d):
        mine = buffer.at[pl.ds(NC * chip, NC)]
        step = d if kind == 0 else chips - d
        return pltpu.make_async_remote_copy(
            src_ref=mine,
            dst_ref=mine,
            send_sem=chain_send.at[kind, d],
            recv_sem=chain_recv.at[kind, d],
            device_id=at(chip_peer(step)),
            device_id_type=MESH,
        )

    def loop(count, act_on):
        def body(d, carry):
            act_on(d)
            return carry

        lax.fori_loop(1, count, body, 0)

    first_copy(stat, 0).start()

    def halo(src, dst, sent, received, device):
        return pltpu.make_async_remote_copy(
            src_ref=src,
            dst_ref=dst,
            send_sem=halo_send.at[sent],
            recv_sem=halo_recv.at[received],
            device_id=at(device),
            device_id_type=MESH,
        )

    own_g = gwin.at[pl.ds(2 * core, 2)]
    own_x = xw.at[pl.ds(2 + 2 * core, 2)]
    g_partner = halo(cot.at[0], own_g, 0, 0, partner)
    x_partner = halo(video.at[0], own_x, 1, 1, partner)
    g_back = [halo(cot.at[0, f], gwin.at[4 + f], 2 + f, 2 + f, beside) for f in range(2)]
    g_relay = [halo(gwin.at[4 + f], gwin.at[4 + f], 2 + f, 2 + f, partner) for f in range(2)]
    x_ahead = halo(video.at[0], xw.at[pl.ds(0, 2)], 4, 4, beside)
    g_partner.start()
    x_partner.start()

    @pl.when(core == 0)
    def _():
        g_back[0].start()
        g_back[1].start()


    pixel, source = iota((256, 256), 0), iota((256, 256), 1)
    right = ((source == pixel + 1) & ((pixel & 15) != 15)).astype(BF16)
    left = ((source == pixel - 1) & ((pixel & 15) != 0)).astype(BF16)
    both = jnp.concatenate([right, left], axis=0)

    def widen(target, k, values, first, last):
        shifted = dot(both, values).astype(BF16)
        target[k, 1:17, :, 256 * first : 256 * first + 256] = shifted[:256].reshape(16, 16, 256)
        target[k, 1:17, :, 256:512] = values.reshape(16, 16, 256)
        target[k, 1:17, :, 256 * last : 256 * last + 256] = shifted[256:].reshape(16, 16, 256)
        target[k, 0:1] = jnp.zeros((1, 16, 768), BF16)
        target[k, 17:18] = jnp.zeros((1, 16, 768), BF16)

    def backward(lag):
        taken = jnp.concatenate(
            [
                gim[pl.ds(2 * core + lag, 2), 2 - i : 18 - i].reshape(512, 768)
                for i in range(3)
            ],
            axis=1,
        )
        weights = jnp.concatenate(
            [kv[lag, i, j] for i in range(3) for j in range(3)], axis=1
        )
        part = dot(taken, weights, (1, 1))
        for f in range(2):
            piece = part[256 * f : 256 * f + 256]
            if lag == 0:
                da[f] = piece
            else:
                keep = flag(own + f + lag < clip_end(starts, own + f, frames))
                da[f] = da[f] + keep * piece

    def widen_g(v, carry):
        widen(gim, v, gwin[v].reshape(256, 256), 0, 2)
        return carry

    load_g.wait()
    lax.fori_loop(0, 2, lambda v, carry: widen_g(2 * core + v, carry), 0)

    first_copy(stat, 0).wait_recv()
    loop(REACH + 1, lambda d: second_copy(stat, 0, REACH + 1 - d).start())

    load_k[0].wait()
    backward(0)
    g_partner.wait_recv()
    lax.fori_loop(0, 2, lambda v, carry: widen_g(2 - 2 * core + v, carry), 0)

    bounds, counted = [], jnp.zeros((8, 128), F32)
    for k in range(6):
        t = base - 2 + k
        b = clip_begin(starts, t)
        bounds.append((b, t + 1))
        count = jnp.maximum(t + 1 - b, 1).astype(F32)
        counted = jnp.where(iota((8, 128), 0) == k, count, counted)
    counted = jnp.maximum(counted, 1.0) * 2048.0
    row, channel = iota((128, 256), 0), iota((128, 256), 1)
    wanted = 64 * ((row >> 3) & 3) + 8 * (row & 7) + 2 * (row >> 5) + core
    select = (channel == wanted).astype(BF16)
    blank = jnp.zeros((128, 256), BF16)
    for lag, v in ((0, 4), (0, 5), (1, 0), (1, 5), (2, 0), (2, 1)):
        lhs[128 * lag : 128 * lag + 128, 256 * v : 256 * v + 256] = blank

    loop(REACH + 1, lambda d: second_copy(stat, 0, d).wait_recv())

    @pl.when(core == 1)
    def _():
        x_ahead.start()

    averaged = masked_rows(stat, bounds) / counted
    squares = pltpu.roll(averaged, 96, 1)
    inv_std = lax.rsqrt(squares - averaged * averaged + EPS)
    wide_mean, wide_inv = spread(averaged, inv_std)
    mean_rows[...] = wide_mean
    inv_rows[...] = wide_inv
    scale_rows[...] = wide_inv * gain[...]

    def activate(k, carry):
        values = xw[k].reshape(256, 256).astype(F32)
        normed = (values - mean_rows[pl.ds(k, 1)]) * scale_rows[pl.ds(k, 1)] + shift[...]
        act[k] = (normed * sigmoid(normed)).astype(BF16)
        return carry

    x_partner.wait_recv()

    for u in range(4):
        activate(2 + u, 0)
        turned = dot(select, act[2 + u], (1, 1))
        end = clip_end(starts, base + u, frames)
        for lag in range(3):
            masked = turned if lag == 0 else turned * flag(base + u + lag < end)
            v = u + lag
            lhs[128 * lag : 128 * lag + 128, 256 * v : 256 * v + 256] = masked.astype(BF16)

    for f in range(2):

        @pl.when(core == 1)
        def _():
            g_back[f].wait_recv()
            g_relay[f].start()

        @pl.when(core == 0)
        def _():
            g_relay[f].wait_recv()

        widen_g(4 + f, 0)

    def one_x(i, d):
        low, count = PIECES[i]
        target = lax.rem(x + d, NX)
        return pltpu.make_async_remote_copy(
            src_ref=sx1.at[target, pl.ds(low, count)],
            dst_ref=rx1.at[d, pl.ds(low, count)],
            send_sem=one_send.at[0, i // 2, d],
            recv_sem=one_recv.at[0, i // 2, d],
            device_id=at(x_peer(d)),
            device_id_type=MESH,
        )

    def one_y(i, d):
        low, count = PIECES[i]
        target = lax.rem(y + d, ny)
        return pltpu.make_async_remote_copy(
            src_ref=sy1.at[target, pl.ds(low, count)],
            dst_ref=ry1.at[d, pl.ds(low, count)],
            send_sem=one_send.at[1, i // 2, d],
            recv_sem=one_recv.at[1, i // 2, d],
            device_id=at(tm, y_peer(d)),
            device_id_type=MESH,
        )

    def one_z(i, d):
        low, count = Z_PIECES[i]
        return pltpu.make_async_remote_copy(
            src_ref=sz1.at[lax.rem(z + d, nz), pl.ds(low, count)],
            dst_ref=rz1.at[d, pl.ds(low, count)],
            send_sem=three_send.at[2 + i // 2, d],
            recv_sem=three_recv.at[2 + i // 2, d],
            device_id=at(z_peer(d)),
            device_id_type=MESH,
        )

    def put_total(buffer, first, rows):
        for h in range(2):
            buffer[h, first : first + rows.shape[0]] = rows[:, 128 * h : 128 * h + 128]

    def every(buffer, start, count, stride):
        rows = [buffer[h, pl.ds(start, count, stride=stride)] for h in range(2)]
        return jnp.concatenate(rows, axis=1)

    for step in range(9):
        i, j = step // 3, step % 3
        terms = dot(lhs[...], gim[:, 2 - i : 18 - i, :, 256 * j : 256 * j + 256].reshape(1536, 256))
        for lag in range(3):
            axis, slot = place_of(3 * step + lag)
            block = terms[128 * lag : 128 * lag + 128]
            if axis == "z":
                put_total(turn, 128 * slot, block)
                for q in range(nz):
                    sz1[q, slot] = every(turn, 128 * slot + q, 16, 8).astype(BF16)
                continue
            for p in range(4):
                if axis == "x":
                    sx1[p, slot] = block[32 * p : 32 * p + 32].astype(BF16)
                else:
                    rows = [block[32 * q + 8 * p : 32 * q + 8 * p + 8] for q in range(4)]
                    sy1[p, slot] = jnp.concatenate(rows, axis=0).astype(BF16)
        if step in Z_PIECES:
            loop(nz, lambda d: one_z(step, d).start())
        if step in PIECES:
            for d in (2, 1, 3):
                one_x(step, d).start()
                one_y(step, d).start()

    for lag in (1, 2):
        load_k[lag].wait()
        backward(lag)

    lanes = iota((1, 128), 1)
    sums = []
    for f in range(2):
        k = 2 + 2 * core + f
        centred = xw[k].reshape(256, 256).astype(F32) - mean_rows[pl.ds(k, 1)]
        normed = centred * scale_rows[pl.ds(k, 1)] + shift[...]
        sig = sigmoid(normed)
        du = da[f] * (sig * (1.0 + normed * (1.0 - sig))) * gain[...]
        da[f] = du
        sums.append(jnp.sum(du, axis=0, keepdims=True))
        sums.append(jnp.sum(du * centred, axis=0, keepdims=True))
    packed = pack_rows(sums)
    row_of = iota((8, 128), 0)

    def pick(rows, k):
        return jnp.sum(jnp.where(row_of == k, rows, 0.0), axis=0, keepdims=True)

    answer = jnp.zeros((1, 128), F32)
    for f in range(2):
        k = 2 + 2 * core + f
        mean_k, inv_k, n_k = pick(averaged, k), pick(inv_std, k), pick(counted, k)
        sum_du = pltpu.roll(packed, 64, 1) if f else packed
        dr = pltpu.roll(sum_du, 96, 1)
        cubed = inv_k * inv_k * inv_k
        dc1 = (dr * cubed * mean_k - inv_k * sum_du) / n_k
        dc2 = -0.5 * dr * cubed / n_k
        dc2 = pltpu.roll(dc2, 32, 1)
        pair = jnp.where(lanes < 32, dc1, jnp.where(lanes < 64, dc2, 0.0))
        answer = answer + (pltpu.roll(pair, 64, 1) if f else pair)
    dstat[pl.ds(tm, 1)] = answer.reshape(1, 1, 128)
    first_copy(dstat, 1).start()

    @pl.when(core == 0)
    def _():
        x_ahead.wait_recv()
        lax.fori_loop(0, 2, activate, 0)

    def widen_a(k, carry):
        widen(aim, k, act[2 * core + k], 2, 0)
        return carry

    lax.fori_loop(0, 4, widen_a, 0)
    for lag in range(3):
        taken = jnp.concatenate(
            [aim[2 - lag : 4 - lag, i : i + 16].reshape(512, 768) for i in range(3)], axis=1
        )
        part = dot(taken, kv[lag].reshape(2304, 256))
        for f in range(2):
            piece = part[256 * f : 256 * f + 256]
            if lag == 0:
                total = xw[2 + 2 * core + f].reshape(256, 256).astype(F32) + piece
            else:
                keep = flag(own + f - lag >= clip_begin(starts, own + f))
                total = total_f[f] + keep * piece
            if f == 0:
                first = total
            else:
                total_f = [first, total]
    for f in range(2):
        out_v[f] = total_f[f].reshape(16, 16, 256).astype(BF16)
    store_out = pltpu.make_async_copy(out_v, out.at[0], store_sem.at[0])
    store_out.start()

    def two(c, kind, d):
        mine, got = ((sx2, rx2), (sy2, ry2), (sz2, rz2), (sz3, rz3))[kind]
        along_y = kind in (0, 2)
        target = lax.rem(y + d, ny) if along_y else lax.rem(x + d, NX)
        src, dst = mine.at[target], got.at[d]
        if kind < 2:
            some = pl.ds(HALVES[c][2], HALVES[c][3])
            src, dst = src.at[some], dst.at[some]
        return pltpu.make_async_remote_copy(
            src_ref=src,
            dst_ref=dst,
            send_sem=two_send.at[kind, c, d],
            recv_sem=two_recv.at[kind, c, d],
            device_id=at(tm, y_peer(d)) if along_y else at(x_peer(d)),
            device_id_type=MESH,
        )

    def three(c, d):
        return pltpu.make_async_remote_copy(
            src_ref=s3.at[lax.rem(z + d, nz), pl.ds(16 * c, 16)],
            dst_ref=r3.at[d, pl.ds(16 * c, 16)],
            send_sem=three_send.at[c, d],
            recv_sem=three_recv.at[c, d],
            device_id=at(z_peer(d)),
            device_id_type=MESH,
        )

    total3[...] = jnp.zeros(total3.shape, F32)

    def gathered(c, mine, got, keep, staged, me):
        low, count, first, length = HALVES[c]
        for both_p in range(2):
            some = pl.ds(16 * both_p, 16)
            half = mine[me, pl.ds(low, count), some].astype(F32)
            for d in range(1, 4):
                half = half + got[d, pl.ds(low, count), some].astype(F32)
            for p in (2 * both_p, 2 * both_p + 1):
                piece = half[:, 8 * (p % 2) : 8 * (p % 2) + 8].reshape(8 * count, 256)
                if 8 * count < length:
                    blank = jnp.zeros((length - 8 * count, 256), F32)
                    piece = jnp.concatenate([piece, blank], axis=0)
                keep[p, first : first + length] = piece
                staged[p, first : first + length] = piece.astype(BF16)

    def to_two(c):
        pieces = (0, 2, 4, 6) if c == 0 else (8,)
        for kind, one, mine, got, keep, staged, me in (
            (0, one_x, sx1, rx1, kx2, sx2, x),
            (1, one_y, sy1, ry1, ky2, sy2, y),
        ):
            for i in pieces:
                for d in range(1, 4):
                    one(i, d).wait_recv()
            gathered(c, mine, got, keep, staged, me)
            for d in (2, 1, 3):
                two(c, kind, d).start()

    def to_three(c):
        low, count, first, length = HALVES[c]
        some = pl.ds(first, length)
        for kind, keep, got, me in ((0, kx2, rx2, y), (1, ky2, ry2, x)):
            for d in range(1, 4):
                two(c, kind, d).wait_recv()
            total = keep[me, some]
            for d in range(1, 4):
                total = total + got[d, some].astype(F32)
            put_total(total3, 128 * c + length * kind, total)
        for q in range(nz):
            s3[q, 16 * c : 16 * c + 16] = every(total3, 128 * c + q, 16, 8).astype(BF16)
        for d in sorted(range(1, nz), key=lambda d: -min(d, nz - d)):
            three(c, d).start()

    to_two(0)
    to_two(1)

    for i in Z_PIECES:
        loop(nz, lambda d: one_z(i, d).wait_recv())
    total = sz1[z].astype(F32)
    for d in range(1, nz):
        total = total + rz1[d].astype(F32)
    put_total(turn, 0, total.reshape(16 * Z_TAPS, 256))
    for p in range(4):
        sz2[p] = every(turn, p, 32, 4).astype(BF16)
    for d in (2, 1, 3):
        two(0, 2, d).start()

    first_copy(dstat, 1).wait_recv()
    loop(REACH + 1, lambda d: second_copy(dstat, 1, d).start())
    to_three(0)
    to_three(1)

    for d in (1, 2, 3):
        two(0, 2, d).wait_recv()
    total = every(turn, y, 32, 4)
    for d in range(1, 4):
        total = total + rz2[d].astype(F32)
    put_total(turn, 128, total)
    for p in range(4):
        sz3[p] = every(turn, 128 + p, 16, 4).astype(BF16)
    for d in (2, 1, 3):
        two(0, 3, d).start()

    loop(REACH + 1, lambda d: second_copy(dstat, 1, d).wait_recv())
    bounds = [(own + f, clip_end(starts, own + f, frames)) for f in range(2)]
    backs = masked_rows(dstat, bounds)
    back_one, back_two = spread(backs, pltpu.roll(backs, 96, 1))
    for f in range(2):
        k = 2 + 2 * core + f
        values = xw[k].reshape(256, 256).astype(F32)
        result = (
            gwin[2 * core + f].reshape(256, 256).astype(F32)
            + da[f] * inv_rows[pl.ds(k, 1)]
            + back_one[f : f + 1]
            + values * (2.0 * back_two[f : f + 1])
        )
        grads_v[f] = result.reshape(16, 16, 256).astype(BF16)
    store_grads = pltpu.make_async_copy(grads_v, grads.at[0], store_sem.at[1])
    store_grads.start()

    for c in range(2):
        own_v[16 * c : 16 * c + 16] = every(total3, 128 * c + z, 16, 8)
    own_v[32:48] = every(turn, 128 + x, 16, 4)
    store_own = pltpu.make_async_copy(own_v, own3, store_sem.at[2])
    store_own.start()

    for kind, buffer in ((0, stat), (1, dstat)):
        first_copy(buffer, kind).wait_send()
        loop(REACH + 1, lambda d: second_copy(buffer, kind, d).wait_send())
    g_partner.wait_send()
    x_partner.wait_send()
    for f in range(2):
        pl.when(core == 0)(g_back[f].wait_send)
        pl.when(core == 1)(g_relay[f].wait_send)
    pl.when(core == 1)(x_ahead.wait_send)
    for d in (1, 2, 3):
        for i in PIECES:
            one_x(i, d).wait_send()
            one_y(i, d).wait_send()
        for c, kind in ((0, 0), (0, 1), (1, 0), (1, 1), (0, 2)):
            two(c, kind, d).wait_send()
    for i in Z_PIECES:
        loop(nz, lambda d: one_z(i, d).wait_send())
    loop(nz, lambda d: three(0, d).wait_send())

    store_out.wait()
    store_grads.wait()
    store_own.wait()
    for c in range(2):
        loop(nz, lambda d: three(c, d).wait_recv())
    for d in (1, 2, 3):
        two(0, 3, d).wait_recv()

    for d in (1, 2, 3):
        two(0, 3, d).wait_send()
    loop(nz, lambda d: three(1, d).wait_send())


def last_sum(scale, out, grads, own3, r3, rz3, *refs):
    out_to, grads_to, wgrads, out_v, grads_v, own_v, r3_v, rz3_v, w_v, sems = refs

    def copy(src, dst, k):
        return pltpu.make_async_copy(src, dst, sems.at[k])

    into = [
        copy(own3, own_v, 0),
        copy(r3, r3_v, 1),
        copy(rz3, rz3_v, 2),
        copy(out, out_v, 3),
        copy(grads, grads_v, 4),
    ]
    for part in into:
        part.start()
    into[3].wait()
    outward = [copy(out_v, out_to, 5)]
    outward[0].start()
    into[4].wait()
    outward.append(copy(grads_v, grads_to, 6))
    outward[1].start()
    for part in into[:3]:
        part.wait()
    total = own_v[0:32]
    for d in range(1, r3_v.shape[0]):
        total = total + r3_v[d].astype(F32)
    along_z = own_v[32:48]
    for d in range(1, rz3_v.shape[0]):
        along_z = along_z + rz3_v[d].astype(F32)
    places = [("z", k) for k in range(16)]
    for c, (low, count, first, length) in enumerate(HALVES):
        taps = [(axis, low + k) for axis in "xy" for k in range(length // 8)]
        places = places + taps + [None] * (16 - len(taps))
    rows = jnp.concatenate([along_z, total], axis=0) * scale
    for n in range(TAPS):
        k = places.index(place_of(n))
        to = 9 * (n % 3) + n // 3
        w_v[to] = rows[k : k + 1]
    outward.append(copy(w_v, wgrads, 7))
    outward[2].start()
    for part in outward:
        part.wait()


def local(nz, ny, scale, video_tile, clip_lengths, kernels, norm_gains, norm_shifts, cotangent):
    hbm = pl.BlockSpec(memory_space=pltpu.HBM)
    dma = pltpu.SemaphoreType.DMA
    made = pl.pallas_call(
        functools.partial(kernel, nz, ny),
        out_shape=(
            jax.ShapeDtypeStruct(video_tile.shape, BF16),
            jax.ShapeDtypeStruct(video_tile.shape, BF16),
            jax.ShapeDtypeStruct((48, 256), F32),
            jax.ShapeDtypeStruct((nz, 32, 256), BF16),
            jax.ShapeDtypeStruct((NX, 16, 256), BF16),
        ),
        in_specs=[hbm] * 6,
        out_specs=(hbm,) * 5,
        scratch_shapes=[
            pltpu.SMEM((1, 6), jnp.int32),
            pltpu.VMEM((1, 256), F32),
            pltpu.VMEM((1, 256), F32),
            pltpu.VMEM((6, 16, 16, 256), BF16),
            pltpu.VMEM((6, 16, 16, 256), BF16),
            pltpu.VMEM((3, 3, 3, 256, 256), BF16),
            pltpu.VMEM((6, 18, 16, 768), BF16),
            pltpu.VMEM((4, 18, 16, 768), BF16),
            pltpu.VMEM((6, 256, 256), BF16),
            pltpu.VMEM((384, 1536), BF16),
            pltpu.VMEM((nz * GROUP, 1, 128), F32),
            pltpu.VMEM((nz * GROUP, 1, 128), F32),
            pltpu.VMEM((8, 256), F32),
            pltpu.VMEM((8, 256), F32),
            pltpu.VMEM((8, 256), F32),
            pltpu.VMEM((2, 256, 256), F32),
            pltpu.VMEM((4, 11, 32, 256), BF16),
            pltpu.VMEM((4, 11, 32, 256), BF16),
            pltpu.VMEM((4, 11, 32, 256), BF16),
            pltpu.VMEM((4, 11, 32, 256), BF16),
            pltpu.VMEM((8, Z_TAPS, 16, 256), BF16),
            pltpu.VMEM((8, Z_TAPS, 16, 256), BF16),
            pltpu.VMEM((4, 96, 256), BF16),
            pltpu.VMEM((4, 96, 256), BF16),
            pltpu.VMEM((4, 96, 256), BF16),
            pltpu.VMEM((4, 96, 256), BF16),
            pltpu.VMEM((4, 32, 256), BF16),
            pltpu.VMEM((4, 32, 256), BF16),
            pltpu.VMEM((4, 16, 256), BF16),
            pltpu.VMEM((4, 96, 256), F32),
            pltpu.VMEM((4, 96, 256), F32),
            pltpu.VMEM((2, 128 * Z_TAPS + 8, 128), F32),
            pltpu.VMEM((2, 264, 128), F32),
            pltpu.VMEM((8, 32, 256), BF16),
            pltpu.VMEM((48, 256), F32),
            pltpu.VMEM((2, 16, 16, 256), BF16),
            pltpu.VMEM((2, 16, 16, 256), BF16),
            dma((8,)),
            dma((5,)),
            dma((5,)),
            dma((2, REACH + 1)),
            dma((2, REACH + 1)),
            dma((2, 5, 4)),
            dma((2, 5, 4)),
            dma((4, 2, 4)),
            dma((4, 2, 4)),
            dma((5, 8)),
            dma((5, 8)),
            dma((3,)),
        ],
        compiler_params=pltpu.CompilerParams(
            collective_id=0, has_side_effects=True, vmem_limit_bytes=60 * 1024 * 1024
        ),
        cost_estimate=pl.CostEstimate(flops=5_500_000_000, bytes_accessed=5_000_000, transcendentals=400_000),
    )(clip_lengths, norm_gains, norm_shifts, video_tile, cotangent, kernels)
    results = pl.pallas_call(
        functools.partial(last_sum, scale),
        out_shape=(
            jax.ShapeDtypeStruct(video_tile.shape, BF16),
            jax.ShapeDtypeStruct(video_tile.shape, BF16),
            jax.ShapeDtypeStruct((TAPS, 1, 256), F32),
        ),
        in_specs=[hbm] * 5,
        out_specs=(hbm,) * 3,
        scratch_shapes=[pltpu.VMEM(part.shape, part.dtype) for part in made]
        + [pltpu.VMEM((TAPS, 1, 256), F32), dma((8,))],
        compiler_params=pltpu.CompilerParams(vmem_limit_bytes=60 * 1024 * 1024),
    )(*made)
    return (results[0], results[1], results[2].transpose(1, 0, 2))


def solution(mesh):
    ny, tm = mesh.shape["dp"], mesh.shape["tm"]
    nz = tm // GROUP
    scale = 1.0 / math.sqrt(ny * tm * 2 * 256)
    placed = P("dp", "tm", None, None, None)
    return jax.shard_map(
        functools.partial(local, nz, ny, scale),
        mesh=mesh,
        in_specs=(placed, P("dp", None), P(), P(), P(), placed),
        out_specs=(placed, placed, P(None, None, ("dp", "tm"))),
        check_vma=False,
    )
```
